32 devices in a mesh: gx: 4 (over z), gy: 8 (over y, x, core).
Axes of the slice: x: 2, y: 2, z: 4, core: 2. Of those that a mesh axis runs over, the one named last changes fastest.
Arguments:
- fine_state: float32 [9, 16, 256, 1024], P(None, None, 'gx', 'gy'), may hold values from -6 to 6
- fine_medium: float32 [3, 16, 256, 1024], P(None, None, 'gx', 'gy'), may hold values from 0.5 to 2
- coarse_state: float32 [9, 8, 128, 512], P(None, None, 'gy', 'gx'), may hold values from -6 to 6
- coarse_medium: float32 [3, 8, 128, 512], P(None, None, 'gy', 'gx'), may hold values from 0.5 to 2
- coarse_past: float32 [9, 2, 128, 512], P(None, None, 'gy', 'gx'), may hold values from -6 to 6
- parent_rows: int32 [256], P('gx'), may hold values from 0 to 127, as said below
- parent_cols: int32 [1024], P('gy'), may hold values from 0 to 511, as said below
Outputs:
- fine_out: float32 [9, 16, 256, 1024], P(None, None, 'gx', 'gy')
- coarse_out: float32 [9, 8, 128, 512], P(None, None, 'gy', 'gx')
The draws below stay inside these ranges and needn't reach their ends.
Inputs may be any that keep to these rules, and one draw needn't show every extreme that they name: parent_rows[x] is x / 2 - 1 for x a positive multiple of 4, 0 for x = 0, x / 2 for x of remainder 2 by 4, (x - 1) / 2 or (x + 1) / 2 for remainder 1, and (x + 1) / 2 for remainder 3, never past the last coarse row. parent_cols[y] follows the same rule along columns, never past the last coarse column.
All inputs are finite; a program needn't handle non-finite values.
Results may differ from the reference program's by a relative error of at most 0.00002.
Values sent between devices are 32-bit elements; how exact they have to be, the bound alone decides.
No kernel may reach another device: no remote copies, remote signals or barrier semaphores. Data moves between devices by JAX's collectives and lax.ppermute only.
A program may use at most 192 MiB of HBM per device.

```python
import math
import jax
import jax.numpy as jnp
from jax import lax

FZ = 16
CZ = 8
FINE_X = 256
FINE_Y = 1024
COARSE_X = 128
COARSE_Y = 512


def parent_law(key, count, limit):
    flips = jax.random.randint(key, (count,), 0, 2).astype(jnp.int32)
    indices = jnp.arange(count).astype(jnp.int32)
    remain = indices % 4
    halves = indices // 2
    chosen = jnp.where(remain == 0, jnp.maximum(halves - 1, 0), jnp.where(remain == 2, halves, jnp.where(remain == 3, halves + 1, halves + flips)))
    return jnp.minimum(chosen, limit - 1).astype(jnp.int32)


def draw_parent_rows(key, part):
    return parent_law(jax.random.fold_in(key, 11), FINE_X, COARSE_X)


def draw_parent_cols(key, part):
    return parent_law(jax.random.fold_in(key, 23), FINE_Y, COARSE_Y)


def steps_of(rng, dims, pieces, least, largest):
    factor_of = 1.0
    for position, blocks in pieces:
        draws = jax.random.uniform(jax.random.fold_in(jax.random.fold_in(rng, 6), position), (blocks,), jnp.float32, least / len(pieces), largest / len(pieces))
        factor_of = factor_of * jnp.repeat(jnp.exp(draws), dims[position] // blocks).reshape((-1,) + (1,) * (len(dims) - 1 - position))
    return factor_of


def noise(key, dims, spread, bound, split=(), kind=jnp.bfloat16):
    loudness = steps_of(key, dims, split, -0.22, 0.18) if split else 1.0
    array = jax.random.normal(key, dims, jnp.float32) * spread * loudness
    return jnp.minimum(jnp.maximum(array, -bound), bound).astype(kind)


def setup_inputs(seed: int = 0) -> dict:
    streams_of = jax.random.split(jax.random.key(seed), 8)
    return {
        "fine_state": noise(streams_of[0], (9, FZ, FINE_X, FINE_Y), 1.0, 6.0, ((2, 4), (3, 8)), jnp.float32),
        "fine_medium": jnp.clip(jnp.exp(math.log(2.0) - 1.3862944 * jax.random.uniform(streams_of[1], (3, FZ, FINE_X, FINE_Y), jnp.float32) ** steps_of(streams_of[1], (3, FZ, FINE_X, FINE_Y), ((2, 4), (3, 8)), -0.2, 0.2)), 0.5, 2.0),
        "coarse_state": noise(streams_of[2], (9, CZ, COARSE_X, COARSE_Y), 1.0, 6.0, ((2, 8), (3, 4)), jnp.float32),
        "coarse_medium": jnp.clip(jnp.exp(math.log(2.0) - 1.3862944 * jax.random.uniform(streams_of[3], (3, CZ, COARSE_X, COARSE_Y), jnp.float32) ** steps_of(streams_of[3], (3, CZ, COARSE_X, COARSE_Y), ((2, 8), (3, 4)), -0.2, 0.2)), 0.5, 2.0),
        "coarse_past": noise(streams_of[4], (9, 2, COARSE_X, COARSE_Y), 1.0, 6.0, ((2, 8), (3, 4)), jnp.float32),
        "parent_rows": draw_parent_rows(jax.random.fold_in(streams_of[7], 71), 0),
        "parent_cols": draw_parent_cols(jax.random.fold_in(streams_of[7], 71), 0),
    }


COEFFS = (1225.0 / 1024.0, -245.0 / 3072.0, 49.0 / 5120.0, -5.0 / 7168.0)
STEP = 0.1


def derivative(values, dimension, forward, inv_spacing):
    rank_count = values.ndim
    dimension = dimension % rank_count
    cropped = values
    for other_dim in range(rank_count - 3, rank_count):
        if other_dim != dimension:
            cropped = lax.slice_in_dim(cropped, 4, cropped.shape[other_dim] - 4, axis=other_dim)
    length = cropped.shape[dimension] - 8
    result = None
    for tap_index in range(1, 5):
        upper_start = 4 + tap_index if forward else 3 + tap_index
        lower_start = 5 - tap_index if forward else 4 - tap_index
        upper_part = lax.slice_in_dim(cropped, upper_start, upper_start + length, axis=dimension)
        lower_part = lax.slice_in_dim(cropped, lower_start, lower_start + length, axis=dimension)
        tap_term = COEFFS[tap_index - 1] * (upper_part - lower_part)
        result = tap_term if result is None else result + tap_term
    return result * inv_spacing


def velocity_step(velocity, stress_pad, buoyancy, step_size, inv_spacing):
    first_rate = (derivative(stress_pad[0], -2, True, inv_spacing) + derivative(stress_pad[3], -1, False, inv_spacing)
                  + derivative(stress_pad[4], -3, False, inv_spacing))
    second_rate = (derivative(stress_pad[3], -2, False, inv_spacing) + derivative(stress_pad[1], -1, True, inv_spacing)
                   + derivative(stress_pad[5], -3, False, inv_spacing))
    third_rate = (derivative(stress_pad[4], -2, False, inv_spacing) + derivative(stress_pad[5], -1, False, inv_spacing)
                  + derivative(stress_pad[2], -3, True, inv_spacing))
    return velocity + step_size * buoyancy * jnp.stack([first_rate, second_rate, third_rate])


def stress_step(stress, velocity_pad, lame_first, shear_modulus, step_size, inv_spacing):
    strain_first = derivative(velocity_pad[0], -2, False, inv_spacing)
    strain_second = derivative(velocity_pad[1], -1, False, inv_spacing)
    strain_third = derivative(velocity_pad[2], -3, False, inv_spacing)
    dilation = strain_first + strain_second + strain_third
    rate_list = [
        lame_first * dilation + 2.0 * shear_modulus * strain_first,
        lame_first * dilation + 2.0 * shear_modulus * strain_second,
        lame_first * dilation + 2.0 * shear_modulus * strain_third,
        shear_modulus * (derivative(velocity_pad[0], -1, True, inv_spacing) + derivative(velocity_pad[1], -2, True, inv_spacing)),
        shear_modulus * (derivative(velocity_pad[0], -3, True, inv_spacing) + derivative(velocity_pad[2], -2, True, inv_spacing)),
        shear_modulus * (derivative(velocity_pad[1], -3, True, inv_spacing) + derivative(velocity_pad[2], -1, True, inv_spacing)),
    ]
    return stress + step_size * jnp.stack(rate_list)


def zero_layers(values, layer_count):
    return jnp.zeros((values.shape[0], layer_count) + values.shape[2:], values.dtype)


def fine_pad(values, ghost_cells):
    stacked = jnp.concatenate([zero_layers(values, 4), values, ghost_cells], axis=1)
    return jnp.pad(stacked, ((0, 0), (0, 0), (4, 4), (4, 4)))


def coarse_pad(values, ghost_cells):
    stacked = jnp.concatenate([ghost_cells, values, zero_layers(values, 4)], axis=1)
    return jnp.pad(stacked, ((0, 0), (0, 0), (4, 4), (4, 4)))


def reference(fine_state, fine_medium, coarse_state, coarse_medium, coarse_past, parent_rows, parent_cols):
    coarse_top = coarse_state[:, :2]
    time_levels = (coarse_top, 1.5 * coarse_top - 0.5 * coarse_past)
    fine_now = fine_state
    fine_depth = fine_state.shape[1]
    for coarse_level in time_levels:
        picked = jnp.take(jnp.take(coarse_level, parent_rows, axis=2), parent_cols, axis=3)
        ghost_cells = jnp.repeat(picked, 2, axis=1)
        velocity = velocity_step(fine_now[:3], fine_pad(fine_now[3:], ghost_cells[3:]), fine_medium[0], STEP, 1.0)
        stress = stress_step(fine_now[3:], fine_pad(velocity, ghost_cells[:3]), fine_medium[1], fine_medium[2], STEP, 1.0)
        fine_now = jnp.concatenate([velocity, stress], axis=0)
    blended = 0.5 * (fine_state[:, fine_depth - 8:] + fine_now[:, fine_depth - 8:])
    rows_half = blended.shape[2] // 2
    cols_half = blended.shape[3] // 2
    coarse_ghost = blended.reshape(9, 4, 2, rows_half, 2, cols_half, 2).mean(axis=(2, 4, 6))
    velocity = velocity_step(coarse_state[:3], coarse_pad(coarse_state[3:], coarse_ghost[3:]), coarse_medium[0], 2.0 * STEP, 0.5)
    stress = stress_step(coarse_state[3:], coarse_pad(velocity, coarse_ghost[:3]), coarse_medium[1], coarse_medium[2], 2.0 * STEP, 0.5)
    coarse_out = jnp.concatenate([velocity, stress], axis=0)
    return (fine_now, coarse_out)
```

```python
import functools

import jax
import jax.numpy as jnp
import ml_dtypes
import numpy as np
from jax import lax
from jax.experimental import pallas as pl
from jax.experimental.pallas import tpu as pltpu
from jax.sharding import PartitionSpec as P

COEFFS = (1225.0 / 1024.0, -245.0 / 3072.0, 49.0 / 5120.0, -5.0 / 7168.0)
STEP = 0.1
LANES = 128
F32 = jnp.float32
BF16 = jnp.bfloat16

VX, VY, VZ, SXX, SYY, SZZ, SXY, SXZ, SYZ = range(9)
CROSSING = (VX, VY, VZ, SXZ, SYZ, SZZ)
VEL_X = ((SXX, True), (SXY, False), (SXZ, False))
VEL_Y = ((SXY, False), (SYY, True), (SYZ, False))
VEL_Z = ((SXZ, False), (SYZ, False), (SZZ, True))
STR_X = ((VX, False), (VY, True), (VZ, True))
STR_Y = ((VX, True), (VY, False), (VZ, True))
STR_Z = ((VX, True), (VY, True), (VZ, False))


def band(width, forward):
    matrix = np.zeros((width + 8, width), np.float64)
    for out in range(width):
        for tap, coeff in enumerate(COEFFS, 1):
            upper = out + tap if forward else out + tap - 1
            lower = out + 1 - tap if forward else out - tap
            matrix[4 + upper, out] += coeff
            matrix[4 + lower, out] -= coeff
    return matrix


def two_part(matrix):
    high = matrix.astype(ml_dtypes.bfloat16)
    low = (matrix - high.astype(np.float64)).astype(ml_dtypes.bfloat16)
    return np.block([[high, low], [high, np.zeros_like(low)]]).astype(ml_dtypes.bfloat16)


def lane_constants():
    tile = np.stack([two_part(band(LANES, f)[4:-4]) for f in (False, True)])
    halo = []
    for parity in range(2):
        for forward in (False, True):
            matrix = band(LANES, forward)
            after = np.zeros((8, LANES))
            before = np.zeros((8, LANES))
            after[:4] = matrix[-4:]
            before[4:] = matrix[:4]
            pair = (after, before) if parity == 0 else (before, after)
            halo.append(two_part(np.concatenate(pair)))
    halo = np.stack(halo).reshape(2, 2, 32, 2 * LANES)
    edges = np.zeros((8, LANES), np.float32)
    for k in range(4):
        edges[k, k] = 1.0
        edges[4 + k, LANES - 4 + k] = 1.0
    edges = np.concatenate([edges, edges], axis=1).astype(ml_dtypes.bfloat16)
    return tile, halo, edges


def mean_constants():
    half = LANES // 2
    place = np.zeros((2, LANES, LANES), np.float32)
    for lane in range(LANES):
        for part in range(2):
            place[part, lane, part * half + lane // 2] = 1.0 / 16.0
    return np.concatenate([place, place], axis=1).astype(ml_dtypes.bfloat16)


def split(x):
    high = x.astype(BF16)
    return high, (x - high.astype(F32)).astype(BF16)


def fold(x):
    half = x.shape[1] // 2
    return x[:, :half] + x[:, half:]


def dot(a, b, dims=((1,), (0,))):
    return lax.dot_general(a, b, (dims, ((), ())), preferred_element_type=F32)


def dot_lanes(x, matrix):
    return fold(dot(jnp.concatenate(split(x), axis=1), matrix))


def dot_rows(x, matrix):
    return fold(dot(jnp.concatenate(split(x), axis=0), matrix, ((0,), (0,))))


def flat(x):
    return x.reshape(x.shape[0] * x.shape[1], x.shape[2])


def put_rows(out_a, out_b, base, fields, parity):
    even = parity == 0
    for k, (ref, f) in enumerate(fields):
        depth, rows = ref.shape[1], ref.shape[2]
        for z in range(depth):
            first = ref[f, z, 0:4, :]
            last = ref[f, z, rows - 4 : rows, :]
            at = pl.ds(base + 4 * (k * depth + z), 4)
            out_a[at, :] = jnp.where(even, last, first)
            out_b[at, :] = jnp.where(even, first, last)


def put_columns(outs, base, fields, edges):
    for k, (ref, f) in enumerate(fields):
        x = jnp.concatenate(split(flat(ref[f])), axis=1)
        turned = dot(edges, x, ((1,), (1,)))
        blocks = turned.shape[1] // LANES
        for m in range(blocks):
            for out in outs:
                out[pl.ds(base + 8 * (k * blocks + m), 8), :] = turned[:, m * LANES : (m + 1) * LANES]


def fill_x(ext, fields, msg_a, msg_b, base, parity):
    even = parity == 0
    for k, (ref, f) in enumerate(fields):
        depth, rows = ref.shape[1], ref.shape[2]
        ext[k, :, 8 : 8 + rows, :] = ref[f]
        for z in range(depth):
            at = pl.ds(base + 4 * (k * depth + z), 4)
            a, b = msg_a[at, :], msg_b[at, :]
            ext[k, z, 8 + rows : 12 + rows, :] = jnp.where(even, a, b)
            ext[k, z, 4:8, :] = jnp.where(even, b, a)


def fill_y(out, fields, directions, msg_a, msg_b, base, parity, tile, halo):
    for k, (ref, f) in enumerate(fields):
        count = ref.shape[1] * ref.shape[2]
        forward = int(directions[k])
        inner = dot_lanes(flat(ref[f]), tile[forward])
        factor = halo[parity, forward]
        for m in range(count // LANES):
            at = pl.ds(base + 8 * (k * (count // LANES) + m), 8)
            outer = dot_rows(jnp.concatenate([msg_a[at, :], msg_b[at, :]], axis=0), factor)
            out[k, m * LANES : (m + 1) * LANES, :] = inner[m * LANES : (m + 1) * LANES] + outer


def fill_z(ext, fields, top, bottom):
    for k, (ref, f) in enumerate(fields):
        depth = ref.shape[1]
        ext[k, 4 : 4 + depth] = ref[f]
        for g in range(4):
            ext[k, g] = top(k, g)
            ext[k, 4 + depth + g] = bottom(k, g)


def taps(read, forward):
    total = None
    for tap, coeff in enumerate(COEFFS, 1):
        upper = tap if forward else tap - 1
        lower = 1 - tap if forward else -tap
        term = coeff * (read(upper) - read(lower))
        total = term if total is None else total + term
    return total


def along_x(ext, k, z, rows, forward):
    return taps(lambda d: ext[k, z, 8 + d : 8 + d + rows, :], forward)


def along_z(ext, k, z, forward):
    return taps(lambda d: ext[k, z + 4 + d], forward)


def along_y(values, k, z, rows):
    return values[k, pl.ds(pl.multiple_of(z * rows, rows), rows), :]


def velocity_half(old, buoyancy, out, ex, ey, ez):
    depth, rows = old.shape[1], old.shape[2]

    def layer(z, _):
        scale = STEP * buoyancy[0, z]
        zx = along_z(ez, 0, z, False)
        zy = along_z(ez, 1, z, False)
        zz = along_z(ez, 2, z, True)
        x = along_x(ex, 0, z, rows, True)
        out[0, z] = old[0, z] + scale * (x + along_y(ey, 0, z, rows) + zx)
        x = along_x(ex, 1, z, rows, False)
        out[1, z] = old[1, z] + scale * (x + along_y(ey, 1, z, rows) + zy)
        x = along_x(ex, 2, z, rows, False)
        out[2, z] = old[2, z] + scale * (x + along_y(ey, 2, z, rows) + zz)
        return 0

    lax.fori_loop(0, depth, layer, 0)


def stress_half(old, lame, shear, out, base, ex, ey, ez):
    depth, rows = lame.shape[1], lame.shape[2]

    def layer(z, _):
        exx = along_x(ex, 0, z, rows, False)
        eyy = along_y(ey, 1, z, rows)
        ezz = along_z(ez, 2, z, False)
        mu = STEP * shear[0, z]
        common = (STEP * lame[0, z]) * (exx + eyy + ezz)
        double = mu + mu
        out[base, z] = old(0, z) + (common + double * exx)
        out[base + 1, z] = old(1, z) + (common + double * eyy)
        out[base + 2, z] = old(2, z) + (common + double * ezz)
        x = along_x(ex, 1, z, rows, True)
        out[base + 3, z] = old(3, z) + mu * (along_y(ey, 0, z, rows) + x)
        x = along_x(ex, 2, z, rows, True)
        out[base + 4, z] = old(4, z) + mu * (along_z(ez, 0, z, True) + x)
        y = along_y(ey, 2, z, rows)
        out[base + 5, z] = old(5, z) + mu * (along_z(ez, 1, z, True) + y)
        return 0

    lax.fori_loop(0, depth, layer, 0)


def zeros_like_plane(ref):
    return jnp.zeros(ref.shape[-2:], F32)


def planes_kernel(state, past, out):
    rows = state.shape[2]
    for n, f in enumerate(CROSSING):
        for layer in range(2):
            now = state[f, layer]
            out[pl.ds((2 * n + layer) * rows, rows), :] = now
            later = 1.5 * now - 0.5 * past[f, layer]
            out[pl.ds((12 + 2 * n + layer) * rows, rows), :] = later


def pack_kernel(par, fine, coarse, edges, out_a, out_b, out_1, out_2):
    pi, pj = par[0], par[1]
    depth, rows = fine.shape[1], fine.shape[2]
    fine_x = [(fine, f) for f, _ in VEL_X]
    fine_y = [(fine, f) for f, _ in VEL_Y]
    coarse_x = [(coarse, f) for f, _ in VEL_X]
    coarse_y = [(coarse, f) for f, _ in VEL_Y]
    put_rows(out_a, out_b, 0, fine_x, pi)
    put_columns((out_a, out_b), 12 * depth, coarse_y, edges[...])
    put_columns((out_1, out_2), 0, fine_y, edges[...])
    put_rows(out_1, out_2, 24 * (depth * rows // LANES), coarse_x, pj)


def ghost_kernel(par, own, other, prow, pcol, in_a, in_b, ghost, virtual, out_a, out_b):
    pi, pj = par[0], par[1]
    row_base, col_base = par[2], par[3]
    part = own.shape[0] // 24
    fine_rows = prow.shape[1]
    even_col = pj == 0
    source = lax.broadcasted_iota(jnp.int32, (LANES, LANES), 0)
    mine = (source == pcol[...] - col_base).astype(F32)
    beyond = (source == jnp.where(even_col, 0, LANES - 1)).astype(F32)
    pick_cols = jnp.concatenate([mine, beyond], axis=1).astype(BF16)
    pick_cols = jnp.concatenate([pick_cols, pick_cols], axis=0)
    source = lax.broadcasted_iota(jnp.int32, (2 * part, LANES), 0)
    lane = lax.broadcasted_iota(jnp.int32, (2 * part, LANES), 1)
    wanted = jnp.concatenate(
        [prow[...] - row_base, jnp.full((1, LANES - fine_rows), -1, jnp.int32)], axis=1
    )
    wanted = jnp.where(lane == fine_rows, 2 * part - 1, jnp.where(lane == fine_rows + 1, 0, wanted))
    pick_rows = (source == wanted).astype(BF16)
    pick_rows = jnp.concatenate([pick_rows, pick_rows], axis=0)

    def spread(ref):
        return dot(jnp.concatenate(split(ref[...]), axis=1), pick_cols)

    from_own, from_other = spread(own), spread(other)
    first = jnp.where(even_col, from_own, from_other)
    second = jnp.where(even_col, from_other, from_own)
    lanes = lax.broadcasted_iota(jnp.int32, (LANES, LANES), 1)
    aside = jnp.zeros((LANES, LANES), F32)
    even_row = pi == 0
    base = in_a.shape[0]
    out_a[0:base, :] = in_a[...]
    out_b[0:base, :] = in_b[...]
    for p in range(24):
        at = slice(p * part, (p + 1) * part)
        plane = jnp.concatenate([first[at], second[at]], axis=0)
        full = dot(pick_rows, jnp.concatenate(split(plane), axis=0), ((0,), (0,)))
        tile = full[:, :LANES]
        aside = jnp.where(lanes == p, full[:, LANES:], aside)
        ghost[p] = tile[:fine_rows]
        below, above = tile[fine_rows : fine_rows + 1], tile[fine_rows + 1 : fine_rows + 2]
        out_a[base + p : base + p + 1, :] = jnp.where(even_row, below, above)
        out_b[base + p : base + p + 1, :] = jnp.where(even_row, above, below)
    below, above = aside[fine_rows : fine_rows + 1], aside[fine_rows + 1 : fine_rows + 2]
    pad = jnp.zeros((7, LANES), F32)
    out_a[base + 24 : base + 32, :] = jnp.concatenate([jnp.where(even_row, below, above), pad], axis=0)
    out_b[base + 24 : base + 32, :] = jnp.concatenate([jnp.where(even_row, above, below), pad], axis=0)
    virtual[...] = aside[:fine_rows]


def after_before(msg_a, msg_b, at, parity):
    even = parity == 0
    a, b = msg_a[at, :], msg_b[at, :]
    return jnp.where(even, a, b), jnp.where(even, b, a)


def corner_kernel(par, msg_a, msg_b, virtual, in_1, in_2, out_1, out_2):
    base = in_1.shape[0]
    rows = virtual.shape[0]
    corner = msg_a.shape[0] - 8
    after, before = after_before(msg_a, msg_b, slice(corner, corner + 1), par[0])
    out_1[0:base, :] = in_1[...]
    out_2[0:base, :] = in_2[...]
    row = lax.broadcasted_iota(jnp.int32, (rows, LANES), 0)
    column = virtual[...]
    column = column + jnp.where(row == 0, before, 0.0) + jnp.where(row == rows - 1, after, 0.0)
    out_1[base : base + rows, :] = column
    out_2[base : base + rows, :] = column


def first_velocity_kernel(
    par, old, normal, shearing, buoyancy, ghost, msg_a, msg_b, msg_1, msg_2, tile, halo, edges,
    out, ghost_out, out_a, out_b, out_c, ex, ey, ez,
):
    pi, pj = par[0], par[1]
    rows = old.shape[2]
    strip = msg_a.shape[0] - 32
    after, before = after_before(msg_a, msg_b, slice(strip, strip + 24), pi)
    column = msg_2[msg_2.shape[0] - rows :, :]
    row = lax.broadcasted_iota(jnp.int32, (rows, LANES), 0)
    lane = lax.broadcasted_iota(jnp.int32, (rows, LANES), 1)
    edge = lane == jnp.where(pj == 0, 0, LANES - 1)
    for p in range(24):
        plane = ghost[p]
        plane = plane + jnp.where(row == 0, before[p : p + 1], 0.0)
        plane = plane + jnp.where(row == rows - 1, after[p : p + 1], 0.0)
        ghost_out[p] = plane + jnp.where(edge, column[:, p : p + 1], 0.0)
    velocity_body(
        par, old, normal, shearing, buoyancy, ghost_out, 0, msg_a, msg_b, msg_1, msg_2,
        tile, halo, edges, out, out_a, out_b, out_c, ex, ey, ez,
    )


def stress_ref(normal, shearing, f):
    return (normal, f - SXX) if f < SXY else (shearing, f - SXY)


def velocity_body(
    par, old, normal, shearing, buoyancy, ghost, level, msg_a, msg_b, msg_1, msg_2,
    tile, halo, edges, out, out_a, out_b, out_c, ex, ey, ez,
):
    pi, pj = par[0], par[1]
    pick = functools.partial(stress_ref, normal, shearing)
    none = zeros_like_plane(old)
    order = [CROSSING.index(f) for f, _ in VEL_Z]
    fill_z(
        ez, [pick(f) for f, _ in VEL_Z],
        lambda k, g: none, lambda k, g: ghost[12 * level + 2 * order[k] + g // 2],
    )
    fill_x(ex, [pick(f) for f, _ in VEL_X], msg_a, msg_b, 0, pi)
    fill_y(
        ey, [pick(f) for f, _ in VEL_Y], [d for _, d in VEL_Y], msg_1, msg_2, 0, pj, tile, halo
    )
    velocity_half(old, buoyancy, out, ex, ey, ez)
    moved = [(out, c) for c in range(3)]
    put_rows(out_a, out_b, 0, moved, pi)
    put_columns((out_c,), 0, moved, edges[...])


def velocity_kernel(
    par, old, normal, shearing, buoyancy, ghost, msg_a, msg_b, msg_1, msg_2, tile, halo, edges,
    out, out_a, out_b, out_c, ex, ey, ez,
):
    velocity_body(
        par, old, normal, shearing, buoyancy, ghost, 1, msg_a, msg_b, msg_1, msg_2,
        tile, halo, edges, out, out_a, out_b, out_c, ex, ey, ez,
    )


def stress_fill(par, velocity, ghost, level, msg_a, msg_b, msg_1, msg_2, tile, halo, ex, ey, ez):
    pi, pj = par[0], par[1]
    none = zeros_like_plane(velocity)
    fields = [(velocity, c) for c in range(3)]
    fill_z(
        ez, fields, lambda k, g: none, lambda k, g: ghost[12 * level + 2 * k + g // 2]
    )
    fill_x(ex, fields, msg_a, msg_b, 0, pi)
    fill_y(ey, fields, [d for _, d in STR_Y], msg_1, msg_2, 0, pj, tile, halo)


def stress_kernel(
    par, velocity, normal, shearing, lame, shear, ghost, msg_a, msg_b, msg_1, msg_2, tile, halo,
    edges, out, out_a, out_b, out_c, ex, ey, ez,
):
    pi, pj = par[0], par[1]
    stress_fill(par, velocity, ghost, 0, msg_a, msg_b, msg_1, msg_2, tile, halo, ex, ey, ez)
    old = lambda c, z: normal[c, z] if c < 3 else shearing[c - 3, z]
    stress_half(old, lame, shear, out, 0, ex, ey, ez)
    put_rows(out_a, out_b, 0, [(out, f - SXX) for f, _ in VEL_X], pi)
    put_columns((out_c,), 0, [(out, f - SXX) for f, _ in VEL_Y], edges[...])


def last_stress_kernel(
    par, velocity, normal, shearing, lame, shear, ghost, start, msg_a, msg_b, msg_1, msg_2,
    tile, halo, means, out, coarse, ex, ey, ez, summed, halves,
):
    stress_fill(par, velocity, ghost, 1, msg_a, msg_b, msg_1, msg_2, tile, halo, ex, ey, ez)
    old = lambda c, z: normal[c, z] if c < 3 else shearing[c - 3, z]
    out[0:3] = velocity[...]
    stress_half(old, lame, shear, out, 3, ex, ey, ez)
    depth, rows = velocity.shape[1], velocity.shape[2]
    part = rows // 4
    for n, f in enumerate(CROSSING):
        for m in range(4):
            z = depth - 8 + 2 * m
            total = (start[f, 2 * m] + start[f, 2 * m + 1]) + (out[f, z] + out[f, z + 1])
            summed[...] = total
            pairs = summed[pl.ds(0, 2 * part, stride=2), :] + summed[pl.ds(1, 2 * part, stride=2), :]
            at = pl.ds((4 * n + m) * part, part)
            halves[0, at, :] = pairs[:part]
            halves[1, at, :] = pairs[part:]
    upper = dot(jnp.concatenate(split(halves[0]), axis=1), means[0])
    lower = dot(jnp.concatenate(split(halves[1]), axis=1), means[1])
    coarse[...] = upper + lower


def coarse_velocity_kernel(
    par, state, medium, own, other, msg_a, msg_b, msg_1, msg_2, tile, halo, edges,
    out, ghost, out_1, out_2, out_c, ex, ey, ez, *, base_c, base_r,
):
    pi, pj = par[0], par[1]
    rows = state.shape[2]
    half = LANES // 2
    even = pj == 0
    left = jnp.where(even, own[...], other[...])
    right = jnp.where(even, other[...], own[...])
    low = lax.broadcasted_iota(jnp.int32, left.shape, 1) < half
    ghost[...] = jnp.where(
        even,
        jnp.where(low, left, pltpu.roll(right, half, 1)),
        jnp.where(low, pltpu.roll(left, half, 1), right),
    )
    none = zeros_like_plane(state)
    order = [CROSSING.index(f) for f, _ in VEL_Z]
    fill_z(
        ez, [(state, f) for f, _ in VEL_Z],
        lambda k, g: ghost[pl.ds((4 * order[k] + g) * rows, rows), :], lambda k, g: none,
    )
    fill_x(ex, [(state, f) for f, _ in VEL_X], msg_1, msg_2, base_r, pj)
    fill_y(
        ey, [(state, f) for f, _ in VEL_Y], [d for _, d in VEL_Y], msg_a, msg_b, base_c, pi,
        tile, halo,
    )
    velocity_half(state, medium, out, ex, ey, ez)
    moved = [(out, c) for c in range(3)]
    put_rows(out_1, out_2, 0, moved, pj)
    put_columns((out_c,), 0, moved, edges[...])


def coarse_stress_kernel(
    par, state, medium, velocity, ghost, msg_a, msg_b, msg_1, msg_2, tile, halo,
    out, ex, ey, ez,
):
    pi, pj = par[0], par[1]
    rows = state.shape[2]
    none = zeros_like_plane(state)
    fields = [(velocity, c) for c in range(3)]
    fill_z(
        ez, fields, lambda k, g: ghost[pl.ds((4 * k + g) * rows, rows), :], lambda k, g: none
    )
    fill_x(ex, fields, msg_1, msg_2, 0, pj)
    fill_y(ey, fields, [d for _, d in STR_Y], msg_a, msg_b, 0, pi, tile, halo)
    out[0:3] = velocity[...]
    stress_half(
        lambda c, z: state[3 + c, z], medium.at[1:2], medium.at[2:3], out, 3, ex, ey, ez
    )


def call(kernel, args, outs, scratch=()):
    specs, values = [], []
    for n, arg in enumerate(args):
        if n == 0:
            specs.append(pl.BlockSpec(memory_space=pltpu.SMEM))
            values.append(arg)
        elif isinstance(arg, tuple):
            array, block, index = arg
            specs.append(pl.BlockSpec(block, functools.partial(lambda where, _: where, index)))
            values.append(array)
        else:
            specs.append(pl.BlockSpec(arg.shape, functools.partial(lambda rank, _: (0,) * rank, arg.ndim)))
            values.append(arg)
    return pl.pallas_call(
        kernel,
        grid=(1,),
        in_specs=specs,
        out_specs=[
            pl.BlockSpec(o, functools.partial(lambda rank, _: (0,) * rank, len(o))) for o in outs
        ],
        out_shape=[jax.ShapeDtypeStruct(o, F32) for o in outs],
        scratch_shapes=[pltpu.VMEM(s, F32) for s in scratch],
        compiler_params=pltpu.CompilerParams(vmem_limit_bytes=48 * 1024 * 1024),
    )(*values)


def matchings(axis):
    size = lax.axis_size(axis)
    result = []
    for start in range(2):
        pairs = []
        for low in range(start, size - 1, 2):
            pairs += [(low, low + 1), (low + 1, low)]
        result.append(pairs)
    return result


def exchange(axis, first, second):
    one, two = matchings(axis)
    return lax.ppermute(first, axis, one), lax.ppermute(second, axis, two)


def body(
    fine_state, fine_medium, coarse_state, coarse_medium, coarse_past, parent_rows, parent_cols
):
    size_x, size_y = lax.axis_size("gx"), lax.axis_size("gy")
    i, j = lax.axis_index("gx"), lax.axis_index("gy")
    depth, rows, cols = fine_state.shape[1:]
    thick, part = coarse_state.shape[1:3]
    blocks = depth * rows // LANES
    par = jnp.stack([i % 2, j % 2, i * (rows // 2), (j // 2) * LANES]).astype(jnp.int32)
    tile, halo, edges = (jnp.asarray(c) for c in lane_constants())
    means = jnp.asarray(mean_constants())
    across = [
        (p * size_y + q, (q // 2) * size_y + 2 * p + q % 2)
        for p in range(size_x)
        for q in range(size_y)
    ]
    partner = matchings("gy")[0]

    def of_state(count, start):
        return (fine_state, (count, depth, rows, cols), (start // count, 0, 0, 0))

    def of_medium(index):
        return (fine_medium, (1, depth, rows, cols), (index, 0, 0, 0))

    planes = pl.pallas_call(
        planes_kernel,
        grid=(1,),
        in_specs=[
            pl.BlockSpec((9, 2, part, LANES), lambda _: (0, 0, 0, 0)),
            pl.BlockSpec((9, 2, part, LANES), lambda _: (0, 0, 0, 0)),
        ],
        out_specs=pl.BlockSpec((24 * part, LANES), lambda _: (0, 0)),
        out_shape=jax.ShapeDtypeStruct((24 * part, LANES), F32),
    )(coarse_state, coarse_past)
    own = lax.ppermute(planes, ("gx", "gy"), across)
    other = lax.ppermute(own, "gy", partner)

    rows_msg, cols_msg = 12 * depth, 24 * blocks
    coarse_cols, coarse_rows = 24, 12 * thick
    base_x = rows_msg + coarse_cols
    base_y = cols_msg + coarse_rows
    part_a, part_b, part_1, part_2 = call(
        pack_kernel,
        [par, fine_state, coarse_state, edges],
        [(base_x, LANES)] * 2 + [(base_y, LANES)] * 2,
    )
    ghost, virtual, out_a, out_b = call(
        ghost_kernel,
        [par, own, other, parent_rows.reshape(1, rows), parent_cols.reshape(1, cols), part_a, part_b],
        [(24, rows, cols), (rows, LANES), (base_x + 32, LANES), (base_x + 32, LANES)],
    )
    msg_a, msg_b = exchange("gx", out_a, out_b)
    out_1, out_2 = call(
        corner_kernel,
        [par, msg_a, msg_b, virtual, part_1, part_2],
        [(base_y + rows, LANES)] * 2,
    )
    msg_1, msg_2 = exchange("gy", out_1, out_2)
    begin_a, begin_b, begin_1, begin_2 = msg_a, msg_b, msg_1, msg_2

    shape = (depth, rows, cols)
    scratch = [
        (3, depth, rows + 16, cols), (3, depth * rows, cols), (3, depth + 8, rows, cols),
    ]
    halves = [(rows_msg, LANES)] * 2 + [(cols_msg, LANES)]
    velocity, ghost, out_a, out_b, out_c = call(
        first_velocity_kernel,
        [par, of_state(3, 0), of_state(3, 3), of_state(3, 6), of_medium(0), ghost,
         msg_a, msg_b, msg_1, msg_2, tile, halo, edges],
        [(3,) + shape, (24, rows, cols)] + halves,
        scratch,
    )
    msg_a, msg_b = exchange("gx", out_a, out_b)
    msg_1, msg_2 = exchange("gy", out_c, out_c)
    stress, out_a, out_b, out_c = call(
        stress_kernel,
        [par, velocity, of_state(3, 3), of_state(3, 6), of_medium(1), of_medium(2), ghost,
         msg_a, msg_b, msg_1, msg_2, tile, halo, edges],
        [(6,) + shape] + halves,
        scratch,
    )
    msg_a, msg_b = exchange("gx", out_a, out_b)
    msg_1, msg_2 = exchange("gy", out_c, out_c)
    normal = (stress, (3,) + shape, (0, 0, 0, 0))
    shearing = (stress, (3,) + shape, (1, 0, 0, 0))
    velocity, out_a, out_b, out_c = call(
        velocity_kernel,
        [par, velocity, normal, shearing, of_medium(0), ghost,
         msg_a, msg_b, msg_1, msg_2, tile, halo, edges],
        [(3,) + shape] + halves,
        scratch,
    )
    msg_a, msg_b = exchange("gx", out_a, out_b)
    msg_1, msg_2 = exchange("gy", out_c, out_c)
    start = (fine_state, (9, 8, rows, cols), (0, depth // 8 - 1, 0, 0))
    fine_out, lifted = call(
        last_stress_kernel,
        [par, velocity, normal, shearing, of_medium(1), of_medium(2), ghost, start,
         msg_a, msg_b, msg_1, msg_2, tile, halo, means],
        [(9,) + shape, (24 * part, LANES)],
        scratch + [(rows, cols), (2, 24 * part, LANES)],
    )
    own = lax.ppermute(lifted, ("gx", "gy"), across)
    other = lax.ppermute(own, "gy", partner)

    shape = (thick, part, LANES)
    scratch = [
        (3, thick, part + 16, LANES), (3, thick * part, LANES), (3, thick + 8, part, LANES),
    ]
    velocity, ghost, out_1, out_2, out_c = call(
        functools.partial(coarse_velocity_kernel, base_c=rows_msg, base_r=cols_msg),
        [par, coarse_state, (coarse_medium, (1,) + shape, (0, 0, 0, 0)), own, other,
         begin_a, begin_b, begin_1, begin_2, tile, halo, edges],
        [(3,) + shape, (24 * part, LANES), (coarse_rows, LANES), (coarse_rows, LANES),
         (coarse_cols, LANES)],
        scratch,
    )
    msg_a, msg_b = exchange("gx", out_c, out_c)
    msg_1, msg_2 = exchange("gy", out_1, out_2)
    (coarse_out,) = call(
        coarse_stress_kernel,
        [par, coarse_state, coarse_medium, velocity, ghost, msg_a, msg_b, msg_1, msg_2, tile, halo],
        [(9,) + shape],
        scratch,
    )
    return (fine_out, coarse_out)


def solution(mesh):
    placed = (
        P(None, None, "gx", "gy"),
        P(None, None, "gx", "gy"),
        P(None, None, "gy", "gx"),
        P(None, None, "gy", "gx"),
        P(None, None, "gy", "gx"),
        P("gx"),
        P("gy"),
    )
    return jax.shard_map(
        body,
        mesh=mesh,
        in_specs=placed,
        out_specs=(P(None, None, "gx", "gy"), P(None, None, "gy", "gx")),
        check_vma=False,
    )
```

```python
import functools

import jax
import jax.numpy as jnp
import ml_dtypes
import numpy as np
from jax import lax
from jax.experimental import pallas as pl
from jax.experimental.pallas import tpu as pltpu
from jax.sharding import PartitionSpec as P

COEFFS = (1225.0 / 1024.0, -245.0 / 3072.0, 49.0 / 5120.0, -5.0 / 7168.0)
STEP = 0.1
LANES = 128
F32 = jnp.float32
BF16 = jnp.bfloat16

VX, VY, VZ, SXX, SYY, SZZ, SXY, SXZ, SYZ = range(9)
CROSSING = (VX, VY, VZ, SXZ, SYZ, SZZ)
VEL_X = ((SXX, True), (SXY, False), (SXZ, False))
VEL_Y = ((SXY, False), (SYY, True), (SYZ, False))
VEL_Z = ((SXZ, False), (SYZ, False), (SZZ, True))
STR_X = ((VX, False), (VY, True), (VZ, True))
STR_Y = ((VX, True), (VY, False), (VZ, True))
STR_Z = ((VX, True), (VY, True), (VZ, False))


def band(width, forward):
    matrix = np.zeros((width + 8, width), np.float64)
    for out in range(width):
        for tap, coeff in enumerate(COEFFS, 1):
            upper = out + tap if forward else out + tap - 1
            lower = out + 1 - tap if forward else out - tap
            matrix[4 + upper, out] += coeff
            matrix[4 + lower, out] -= coeff
    return matrix


def two_part(matrix):
    high = matrix.astype(ml_dtypes.bfloat16)
    low = (matrix - high.astype(np.float64)).astype(ml_dtypes.bfloat16)
    return np.block([[high, low], [high, np.zeros_like(low)]]).astype(ml_dtypes.bfloat16)


def lane_constants():
    tile = np.stack([two_part(band(LANES, f)[4:-4]) for f in (False, True)])
    halo = []
    for parity in range(2):
        for forward in (False, True):
            matrix = band(LANES, forward)
            after = np.zeros((8, LANES))
            before = np.zeros((8, LANES))
            after[:4] = matrix[-4:]
            before[4:] = matrix[:4]
            pair = (after, before) if parity == 0 else (before, after)
            halo.append(two_part(np.concatenate(pair)))
    halo = np.stack(halo).reshape(2, 2, 32, 2 * LANES)
    return tile, halo


def mean_constants():
    half = LANES // 2
    place = np.zeros((2, LANES, LANES), np.float32)
    for lane in range(LANES):
        for part in range(2):
            place[part, lane, part * half + lane // 2] = 1.0 / 16.0
    return np.concatenate([place, place], axis=1).astype(ml_dtypes.bfloat16)


def split(x):
    high = x.astype(BF16)
    return high, (x - high.astype(F32)).astype(BF16)


def fold(x):
    half = x.shape[1] // 2
    return x[:, :half] + x[:, half:]


def dot(a, b, dims=((1,), (0,))):
    return lax.dot_general(a, b, (dims, ((), ())), preferred_element_type=F32)


def dot_lanes(x, matrix):
    return fold(dot(jnp.concatenate(split(x), axis=1), matrix))


def dot_rows(x, matrix):
    return fold(dot(jnp.concatenate(split(x), axis=0), matrix, ((0,), (0,))))


def flat(x):
    return x.reshape(x.shape[0] * x.shape[1], x.shape[2])


def upper_half(shape):
    return lax.broadcasted_iota(jnp.int32, shape, 0) < 4


def put_rows(out_a, out_b, base, fields, parity):
    parts = []
    for ref, f in fields:
        rows = ref.shape[2]
        parts.append((ref.at[:, :, 0:8, :], ref.at[:, :, rows - 8 : rows, :], f))
    put_edge_rows(out_a, out_b, base, parts, parity)


def put_edge_rows(out_a, out_b, base, fields, parity):
    even = parity == 0
    top = upper_half((8, LANES))
    for k, (head, tail, f) in enumerate(fields):
        depth = head.shape[1]
        for z in range(0, depth, 2):
            first = jnp.where(top, head[f, z], pltpu.roll(head[f, z + 1], 4, 0))
            last = jnp.where(top, pltpu.roll(tail[f, z], 4, 0), tail[f, z + 1])
            at = pl.ds(base + 4 * (k * depth + z), 8)
            out_a[at, :] = jnp.where(even, last, first)
            out_b[at, :] = jnp.where(even, first, last)


def put_columns(outs, base, fields):
    row = lax.broadcasted_iota(jnp.int32, (8, 2 * LANES), 0)
    lane = lax.broadcasted_iota(jnp.int32, (8, 2 * LANES), 1) % LANES
    edges = (lane == jnp.where(row < 4, row, LANES - 8 + row)).astype(BF16)
    for k, (ref, f) in enumerate(fields):
        x = ref[...] if f is None else flat(ref[f])
        x = jnp.concatenate(split(x), axis=1)
        turned = dot(edges, x, ((1,), (1,)))
        blocks = turned.shape[1] // LANES
        for m in range(blocks):
            for out in outs:
                out[pl.ds(base + 8 * (k * blocks + m), 8), :] = turned[:, m * LANES : (m + 1) * LANES]


def fill_x(ext, fields, msg_a, msg_b, base, parity, low=0, count=None):
    even = parity == 0
    for k, (ref, f) in enumerate(fields):
        depth, rows = ref.shape[1], ref.shape[2]
        layers = depth if count is None else count
        ext[k, :, 8 : 8 + rows, :] = ref[f, low : low + layers]
        for z in range(0, layers, 2):
            at = pl.ds(base + 4 * (k * depth + low + z), 8)
            a, b = msg_a[at, :], msg_b[at, :]
            after, before = jnp.where(even, a, b), jnp.where(even, b, a)
            ext[k, z, 8 + rows : 16 + rows, :] = after
            ext[k, z + 1, 8 + rows : 16 + rows, :] = pltpu.roll(after, 4, 0)
            ext[k, z, 0:8, :] = pltpu.roll(before, 4, 0)
            ext[k, z + 1, 0:8, :] = before


def fill_y(out, fields, directions, msg_a, msg_b, base, parity, tile, halo, low=0, count=None):
    for k, (ref, f) in enumerate(fields):
        depth, rows = ref.shape[1], ref.shape[2]
        layers = depth if count is None else count
        forward = int(directions[k])
        inner = dot_lanes(flat(ref[f, low : low + layers]), tile[forward])
        factor = halo[parity, forward]
        start, blocks = low * rows // LANES, depth * rows // LANES
        for m in range(layers * rows // LANES):
            at = pl.ds(base + 8 * (k * blocks + start + m), 8)
            outer = dot_rows(jnp.concatenate([msg_a[at, :], msg_b[at, :]], axis=0), factor)
            out[k, m * LANES : (m + 1) * LANES, :] = inner[m * LANES : (m + 1) * LANES] + outer


def fill_z(ext, fields, top, bottom, low=0, count=None):
    for k, (ref, f) in enumerate(fields):
        depth = ref.shape[1]
        layers = depth if count is None else count
        first, last = max(low - 4, 0), min(low + layers + 4, depth)
        ext[k, first - low + 4 : last - low + 4] = ref[f, first:last]
        for g in range(first - (low - 4)):
            ext[k, g] = top(k, 4 - first + low - 4 + g)
        for g in range(low + layers + 4 - last):
            ext[k, last - low + 4 + g] = bottom(k, g)


def taps(read, forward):
    total = None
    for tap, coeff in enumerate(COEFFS, 1):
        upper = tap if forward else tap - 1
        lower = 1 - tap if forward else -tap
        term = coeff * (read(upper) - read(lower))
        total = term if total is None else total + term
    return total


def along_x(ext, k, z, rows, forward):
    return taps(lambda d: ext[k, z, 8 + d : 8 + d + rows, :], forward)


def along_z(ext, k, z, forward):
    return taps(lambda d: ext[k, z + 4 + d], forward)


def along_y(values, k, z, rows):
    return values[k, pl.ds(pl.multiple_of(z * rows, rows), rows), :]


def velocity_half(old, buoyancy, out, ex, ey, ez):
    depth, rows = out.shape[1], out.shape[2]

    def layer(z, _):
        scale = STEP * buoyancy[0, z]
        zx = along_z(ez, 0, z, False)
        zy = along_z(ez, 1, z, False)
        zz = along_z(ez, 2, z, True)
        x = along_x(ex, 0, z, rows, True)
        out[0, z] = old[0, z] + scale * (x + along_y(ey, 0, z, rows) + zx)
        x = along_x(ex, 1, z, rows, False)
        out[1, z] = old[1, z] + scale * (x + along_y(ey, 1, z, rows) + zy)
        x = along_x(ex, 2, z, rows, False)
        out[2, z] = old[2, z] + scale * (x + along_y(ey, 2, z, rows) + zz)
        return 0

    lax.fori_loop(0, depth, layer, 0, unroll=2)


def stress_half(old, lame, shear, put, low, count, ex, ey, ez):
    rows = ex.shape[2] - 16

    def layer(n, _):
        z = n + low
        exx = along_x(ex, 0, n, rows, False)
        eyy = along_y(ey, 1, n, rows)
        ezz = along_z(ez, 2, n, False)
        mu = STEP * shear(z)
        common = (STEP * lame(z)) * (exx + eyy + ezz)
        double = mu + mu
        put(0, z, n, old(0, z) + (common + double * exx))
        put(1, z, n, old(1, z) + (common + double * eyy))
        put(2, z, n, old(2, z) + (common + double * ezz))
        x = along_x(ex, 1, n, rows, True)
        put(3, z, n, old(3, z) + mu * (along_y(ey, 0, n, rows) + x))
        x = along_x(ex, 2, n, rows, True)
        put(4, z, n, old(4, z) + mu * (along_z(ez, 0, n, True) + x))
        y = along_y(ey, 2, n, rows)
        put(5, z, n, old(5, z) + mu * (along_z(ez, 1, n, True) + y))
        return 0

    lax.fori_loop(0, count, layer, 0, unroll=2)


def zeros_like_plane(ref):
    return jnp.zeros(ref.shape[-2:], F32)


def pack_kernel(
    par, fine, coarse, past, out_a, out_b, out_1, out_2, planes, outer,
    turned, first, last, state, before, sems,
):
    pi, pj = par[0], par[1]
    depth, rows = fine.shape[1], fine.shape[2]
    part = coarse.shape[2]
    copies = [
        pltpu.make_async_copy(coarse, state, sems.at[0]),
        pltpu.make_async_copy(past, before, sems.at[1]),
    ]
    for k, (f, _) in enumerate(VEL_X):
        head, tail = fine.at[f, :, 0:8, :], fine.at[f, :, rows - 8 : rows, :]
        copies.append(pltpu.make_async_copy(head, first.at[k], sems.at[2 + 2 * k]))
        copies.append(pltpu.make_async_copy(tail, last.at[k], sems.at[3 + 2 * k]))
    for k, (f, _) in enumerate(VEL_Y):
        copies.append(pltpu.make_async_copy(fine.at[f], turned.at[k], sems.at[8 + k]))
    for copy in copies:
        copy.start()
    copies[0].wait()
    copies[1].wait()
    upper = pj == 0
    for n, f in enumerate(CROSSING):
        for layer in range(2):
            now = state[f, layer]
            later = 1.5 * now - 0.5 * before[f, layer]
            for p, plane in ((2 * n + layer, now), (12 + 2 * n + layer, later)):
                planes[pl.ds(p * part, part), :] = plane
                outer[p : p + 1, :] = jnp.where(upper, plane[:1], plane[part - 1 :])
    base = 12 * depth
    put_columns((out_a, out_b), base, [(state, f) for f, _ in VEL_Y])
    put_columns((out_a, out_b), base + 24, [(planes, None)])
    base = 24 * (depth * rows // LANES)
    put_rows(out_1, out_2, base, [(state, f) for f, _ in VEL_X], pj)
    base += 12 * coarse.shape[1]
    out_1[base : base + 24, :] = outer[...]
    out_2[base : base + 24, :] = outer[...]
    for copy in copies[2:8]:
        copy.wait()
    put_edge_rows(out_a, out_b, 0, [(first, last, k) for k in range(3)], pi)
    for k in range(3):
        copies[8 + k].wait()
        base = 8 * k * (depth * rows // LANES)
        put_columns((out_1, out_2), base, [(turned, k)])


def crossing_kernel(par, planes, msg_a, msg_b, msg_2, out):
    count = planes.shape[0]
    blocks = count // LANES
    out[0:count, :] = planes[...]
    out[count : count + 24, :] = msg_2[msg_2.shape[0] - 24 :, :]
    even = par[0] == 0
    base = msg_a.shape[0] - 8 * blocks
    left, right = [], []
    for m in range(blocks):
        a = msg_a[pl.ds(base + 8 * m, 8), :]
        b = msg_b[pl.ds(base + 8 * m, 8), :]
        left.append(jnp.where(even, b, a)[7:8])
        right.append(jnp.where(even, a, b)[0:1])
    fill = [jnp.zeros((8 - blocks, LANES), F32)]
    out[count + 24 : count + 32, :] = jnp.concatenate(left + fill, axis=0)
    out[count + 32 : count + 40, :] = jnp.concatenate(right + fill, axis=0)


def expand_ghosts(par, own, other, corner_1, corner_2, prow, pcol, ghost):
    core = par[1]
    row_base, col_base = par[2], par[3]
    part = (own.shape[0] - 40) // 24
    rows = prow.shape[1]
    low = core == 0
    count = 24 * part
    source = lax.broadcasted_iota(jnp.int32, (LANES, LANES), 0)
    pick_cols = (source == pcol[...] - col_base).astype(BF16)
    pick_cols = jnp.concatenate([pick_cols, pick_cols], axis=0)
    source = lax.broadcasted_iota(jnp.int32, (2 * part, rows), 0)
    pick_rows = (source == prow[...] - row_base).astype(BF16)
    pick_rows = jnp.concatenate([pick_rows, pick_rows], axis=0)

    def spread(x):
        return dot(jnp.concatenate(split(x), axis=1), pick_cols)

    mine, theirs = spread(own[0 : count + 24, :]), spread(other[0 : count + 24, :])
    first, second = jnp.where(low, mine, theirs), jnp.where(low, theirs, mine)
    above, below = first[count:], second[count:]
    beside = []
    for ref in (own, other):
        side = jnp.where(low, ref[count + 24 : count + 32, :], ref[count + 32 : count + 40, :])
        side = jnp.concatenate([side, jnp.zeros((LANES - 8, LANES), F32)], axis=0)
        beside.append(side.T)
    side_1 = jnp.where(low, beside[0], beside[1])
    side_2 = jnp.where(low, beside[1], beside[0])
    turn = jnp.where(low, 1, LANES - 1)
    top = pltpu.roll(jnp.where(low, corner_1[...], corner_2[...]), turn, 1)
    bottom = pltpu.roll(jnp.where(low, corner_2[...], corner_1[...]), turn, 1)

    lane = lax.broadcasted_iota(jnp.int32, (rows, LANES), 1)
    row = lax.broadcasted_iota(jnp.int32, (rows, LANES), 0)
    edge = lane == jnp.where(low, 0, LANES - 1)
    edge_row = edge[:1]
    above = above + jnp.where(edge_row, top, 0.0)
    below = below + jnp.where(edge_row, bottom, 0.0)
    group = LANES // part
    columns = []
    for q in range(group):
        at = slice(q * part, (q + 1) * part)
        column = jnp.concatenate([side_1[at], side_2[at]], axis=0)
        columns.append(dot(pick_rows, jnp.concatenate(split(column), axis=0), ((0,), (0,))))
    for p in range(24):
        at = slice(p * part, (p + 1) * part)
        plane = jnp.concatenate([first[at], second[at]], axis=0)
        full = dot(pick_rows, jnp.concatenate(split(plane), axis=0), ((0,), (0,)))
        column = columns[p % group][:, p // group : p // group + 1]
        full = full + jnp.where(edge, column, 0.0)
        full = full + jnp.where(row == 0, above[p : p + 1], 0.0)
        ghost[p] = full + jnp.where(row == rows - 1, below[p : p + 1], 0.0)


def ghost_kernel(
    par, half, buoyancy, own, other, corner_1, corner_2, prow, pcol,
    out, ghost, out_a, out_b, out_c,
):
    expand_ghosts(par, own, other, corner_1, corner_2, prow, pcol, ghost)
    depth = half.shape[1]
    for c, (f, forward) in enumerate(VEL_Z):
        out[c, 0 : depth - 4] = half[c, 0 : depth - 4]
        n = CROSSING.index(f)
        planes = [ghost[2 * n], ghost[2 * n + 1]]
        for z in range(depth - 4, depth):
            total = None
            for tap, coeff in enumerate(COEFFS, 1):
                g = z + (tap if forward else tap - 1) - depth
                if g >= 0:
                    term = coeff * planes[g // 2]
                    total = term if total is None else total + term
            value = half[c, z]
            if total is not None:
                value = value + (STEP * buoyancy[0, z]) * total
            out[c, z] = value
    moved = [(out, c) for c in range(3)]
    put_rows(out_a, out_b, 0, moved, par[0])
    put_columns((out_c,), 0, moved)


def stress_fields(ref, table):
    offset = 9 - ref.shape[0]
    return [(ref, f - offset) for f, _ in table]


def velocity_fill(par, stress, msg_a, msg_b, msg_1, msg_2, tile, halo, bottom, ex, ey, ez):
    pi, pj = par[0], par[1]
    none = zeros_like_plane(stress)
    fill_z(ez, stress_fields(stress, VEL_Z), lambda k, g: none, bottom)
    fill_x(ex, stress_fields(stress, VEL_X), msg_a, msg_b, 0, pi)
    fill_y(
        ey, stress_fields(stress, VEL_Y), [d for _, d in VEL_Y], msg_1, msg_2, 0, pj, tile, halo
    )


def first_velocity_kernel(
    par, state, buoyancy, msg_a, msg_b, msg_1, msg_2, tile, halo, out, ex, ey, ez
):
    none = zeros_like_plane(state)
    velocity_fill(
        par, state, msg_a, msg_b, msg_1, msg_2, tile, halo, lambda k, g: none, ex, ey, ez
    )
    velocity_half(state, buoyancy, out, ex, ey, ez)


def velocity_kernel(
    par, old, stress, buoyancy, ghost, msg_a, msg_b, msg_1, msg_2, tile, halo,
    out, out_a, out_b, out_c, ex, ey, ez,
):
    order = [CROSSING.index(f) for f, _ in VEL_Z]
    velocity_fill(
        par, stress, msg_a, msg_b, msg_1, msg_2, tile, halo,
        lambda k, g: ghost[12 + 2 * order[k] + g // 2], ex, ey, ez,
    )
    velocity_half(old, buoyancy, out, ex, ey, ez)
    moved = [(out, c) for c in range(3)]
    put_rows(out_a, out_b, 0, moved, par[0])
    put_columns((out_c,), 0, moved)


def stress_fill(
    par, velocity, bottom, msg_a, msg_b, msg_1, msg_2, tile, halo, ex, ey, ez, low, count
):
    pi, pj = par[0], par[1]
    none = zeros_like_plane(velocity)
    fields = [(velocity, c) for c in range(3)]
    fill_z(ez, fields, lambda k, g: none, bottom, low, count)
    fill_x(ex, fields, msg_a, msg_b, 0, pi, low, count)
    fill_y(
        ey, fields, [d for _, d in STR_Y], msg_1, msg_2, 0, pj, tile, halo, low, count
    )


def stress_kernel(
    par, velocity, state, medium, ghost, msg_a, msg_b, msg_1, msg_2, tile, halo,
    out, out_a, out_b, out_c, ex, ey, ez,
):
    depth = velocity.shape[1]
    stress_fill(
        par, velocity, lambda k, g: ghost[2 * k + g // 2], msg_a, msg_b, msg_1, msg_2,
        tile, halo, ex, ey, ez, 0, depth,
    )

    def put(c, z, n, value):
        out[c, z] = value

    stress_half(
        lambda c, z: state[SXX + c, z], lambda z: medium[1, z], lambda z: medium[2, z],
        put, 0, depth, ex, ey, ez,
    )
    put_rows(out_a, out_b, 0, stress_fields(out, VEL_X), par[0])
    put_columns((out_c,), 0, stress_fields(out, VEL_Y))


def lower_stress_kernel(
    par, velocity, stress, medium, ghost, start, msg_a, msg_b, msg_1, msg_2, tile, halo, means,
    out, coarse, ex, ey, ez, summed, halves,
):
    depth, rows = velocity.shape[1], velocity.shape[2]
    low = depth - 8
    stress_fill(
        par, velocity, lambda k, g: ghost[12 + 2 * k + g // 2], msg_a, msg_b, msg_1, msg_2,
        tile, halo, ex, ey, ez, low, 8,
    )
    out[0:3] = velocity[:, low:]

    def put(c, z, n, value):
        out[SXX + c, n] = value

    stress_half(
        lambda c, z: stress[c, z], lambda z: medium[1, z], lambda z: medium[2, z],
        put, low, 8, ex, ey, ez,
    )
    part = rows // 4
    for n, f in enumerate(CROSSING):
        for m in range(4):
            z = 2 * m
            total = (start[f, low + z] + start[f, low + z + 1]) + (out[f, z] + out[f, z + 1])
            summed[...] = total
            pairs = summed[pl.ds(0, 2 * part, stride=2), :] + summed[pl.ds(1, 2 * part, stride=2), :]
            at = pl.ds((4 * n + m) * part, part)
            halves[0, at, :] = pairs[:part]
            halves[1, at, :] = pairs[part:]
    upper = dot(jnp.concatenate(split(halves[0]), axis=1), means[0])
    lower = dot(jnp.concatenate(split(halves[1]), axis=1), means[1])
    coarse[...] = upper + lower


def upper_stress_kernel(
    par, below, velocity, stress, medium, msg_a, msg_b, msg_1, msg_2, tile, halo,
    out, done, ex, ey, ez,
):
    stress_fill(
        par, velocity, None, msg_a, msg_b, msg_1, msg_2, tile, halo, ex, ey, ez, 0, 8
    )
    out[0:3] = velocity[:, 0:8]

    def put(c, z, n, value):
        out[SXX + c, n] = value

    stress_half(
        lambda c, z: stress[c, z], lambda z: medium[1, z], lambda z: medium[2, z],
        put, 0, 8, ex, ey, ez,
    )
    done[...] = jnp.zeros_like(done)


def coarse_velocity_kernel(
    par, state, medium, own, other, msg_a, msg_b, msg_1, msg_2, tile, halo, done,
    out, ghost, out_1, out_2, out_c, ex, ey, ez, *, base_c, base_r,
):
    pi, pj = par[0], par[1]
    rows = state.shape[2]
    half = LANES // 2
    even = pj == 0
    left = jnp.where(even, own[...], other[...])
    right = jnp.where(even, other[...], own[...])
    low = lax.broadcasted_iota(jnp.int32, left.shape, 1) < half
    ghost[...] = jnp.where(
        even,
        jnp.where(low, left, pltpu.roll(right, half, 1)),
        jnp.where(low, pltpu.roll(left, half, 1), right),
    )
    none = zeros_like_plane(state)
    order = [CROSSING.index(f) for f, _ in VEL_Z]
    fill_z(
        ez, stress_fields(state, VEL_Z),
        lambda k, g: ghost[pl.ds((4 * order[k] + g) * rows, rows), :], lambda k, g: none,
    )
    fill_x(ex, stress_fields(state, VEL_X), msg_1, msg_2, base_r, pj)
    fill_y(
        ey, stress_fields(state, VEL_Y), [d for _, d in VEL_Y], msg_a, msg_b, base_c, pi,
        tile, halo,
    )
    velocity_half(state, medium, out, ex, ey, ez)
    moved = [(out, c) for c in range(3)]
    put_rows(out_1, out_2, 0, moved, pj)
    put_columns((out_c,), 0, moved)


def coarse_stress_kernel(
    par, state, medium, velocity, ghost, msg_a, msg_b, msg_1, msg_2, tile, halo,
    out, ex, ey, ez,
):
    pi, pj = par[0], par[1]
    depth, rows = state.shape[1], state.shape[2]
    none = zeros_like_plane(state)
    fields = [(velocity, c) for c in range(3)]
    fill_z(
        ez, fields, lambda k, g: ghost[pl.ds((4 * k + g) * rows, rows), :], lambda k, g: none
    )
    fill_x(ex, fields, msg_1, msg_2, 0, pj)
    fill_y(ey, fields, [d for _, d in STR_Y], msg_a, msg_b, 0, pi, tile, halo)
    out[0:3] = velocity[...]

    def put(c, z, n, value):
        out[SXX + c, z] = value

    stress_half(
        lambda c, z: state[SXX + c, z], lambda z: medium[1, z], lambda z: medium[2, z],
        put, 0, depth, ex, ey, ez,
    )


def whole(shape):
    return pl.BlockSpec(shape, functools.partial(lambda rank, _: (0,) * rank, len(shape)))


def call(kernel, args, outs, scratch=(), parts=(), flops=0, copied=0, **options):
    specs = [pl.BlockSpec(memory_space=pltpu.SMEM)]
    for n, a in enumerate(args[1:]):
        specs.append(pl.BlockSpec(memory_space=pltpu.HBM) if n < copied else whole(a.shape))
    if "above" in options:
        array = options.pop("above")
        specs.insert(1, pl.BlockSpec(memory_space=pl.ANY))
        args = [args[0], array] + list(args[1:])
        options["input_output_aliases"] = {1: 0}
    out_specs, out_shapes = [], []
    for n, shape in enumerate(outs):
        if n < len(parts):
            full, place = parts[n]
            out_specs.append(pl.BlockSpec(shape, functools.partial(lambda p, _: p, place)))
            out_shapes.append(jax.ShapeDtypeStruct(full, F32))
        else:
            out_specs.append(whole(shape))
            out_shapes.append(jax.ShapeDtypeStruct(shape, F32))
    size = sum(4 * int(np.prod(a.shape)) for a in args) + sum(4 * int(np.prod(o)) for o in outs)
    return pl.pallas_call(
        kernel,
        grid=(1,),
        in_specs=specs,
        out_specs=out_specs,
        out_shape=out_shapes,
        scratch_shapes=[pltpu.VMEM(s, F32) for s in scratch]
        + ([pltpu.SemaphoreType.DMA((11,))] if copied else []),
        compiler_params=pltpu.CompilerParams(vmem_limit_bytes=(60 if copied else 20) * 1024 * 1024),
        cost_estimate=pl.CostEstimate(flops=flops, bytes_accessed=size, transcendentals=0),
        **options,
    )(*args)


def matchings(axis):
    size = lax.axis_size(axis)
    result = []
    for start in range(2):
        pairs = []
        for low in range(start, size - 1, 2):
            pairs += [(low, low + 1), (low + 1, low)]
        result.append(pairs)
    return result


def exchange(axis, first, second):
    one, two = matchings(axis)
    return lax.ppermute(first, axis, one), lax.ppermute(second, axis, two)


def body(
    fine_state, fine_medium, coarse_state, coarse_medium, coarse_past, parent_rows, parent_cols
):
    size_x, size_y = lax.axis_size("gx"), lax.axis_size("gy")
    i, j = lax.axis_index("gx"), lax.axis_index("gy")
    depth, rows, cols = fine_state.shape[1:]
    thick, part = coarse_state.shape[1:3]
    blocks = depth * rows // LANES
    par = jnp.stack([i % 2, j % 2, i * (rows // 2), (j // 2) * LANES]).astype(jnp.int32)
    tile, halo = (jnp.asarray(c) for c in lane_constants())
    means = jnp.asarray(mean_constants())
    across = [
        (p * size_y + q, (q // 2) * size_y + 2 * p + q % 2)
        for p in range(size_x)
        for q in range(size_y)
    ]
    partner = matchings("gy")[0]

    corners = ([], [])
    for a in range(size_x):
        for b in range(size_y):
            above = b % 2 == 1
            chip = b // 2 + 1 if above else b // 2 - 1
            for n in range(2):
                left = above if n == 0 else not above
                near = a + 1 if left else a - 1
                if 0 <= chip < size_x and 0 <= near < size_x:
                    corners[n].append((a * size_y + b, chip * size_y + 2 * near + (0 if left else 1)))
    both = ("gx", "gy")

    rows_msg, cols_msg = 12 * depth, 24 * blocks
    coarse_cols, coarse_rows = 24, 12 * thick
    count = 24 * part
    out_a, out_b, out_1, out_2, planes, outer = call(
        pack_kernel,
        [par, fine_state, coarse_state, coarse_past],
        [(rows_msg + coarse_cols + count * 8 // LANES, LANES)] * 2
        + [(cols_msg + coarse_rows + 24, LANES)] * 2
        + [(count, LANES), (24, LANES)],
        [(3,) + fine_state.shape[1:], (3, depth, 8, cols), (3, depth, 8, cols),
         coarse_state.shape, coarse_past.shape],
        copied=3,
    )
    msg_a, msg_b = exchange("gx", out_a, out_b)
    msg_1, msg_2 = exchange("gy", out_1, out_2)
    begin = msg_a, msg_b, msg_1, msg_2
    (crossing,) = call(
        crossing_kernel, [par, planes, msg_a, msg_b, msg_2], [(count + 40, LANES)]
    )
    crossing, outer = lax.optimization_barrier((crossing, outer))
    own = lax.ppermute(crossing, both, across)
    corner_1 = lax.ppermute(outer, both, corners[0])
    corner_2 = lax.ppermute(outer, both, corners[1])

    shape = (depth, rows, cols)

    def scratch_of(depth, rows):
        return [
            (3, depth, rows + 16, LANES), (3, depth * rows, LANES), (3, depth + 8, rows, LANES),
        ]

    cells = depth * rows * cols
    halves = [(rows_msg, LANES)] * 2 + [(cols_msg, LANES)]
    (half,) = call(
        first_velocity_kernel,
        [par, fine_state, fine_medium, msg_a, msg_b, msg_1, msg_2, tile, halo],
        [(3,) + shape],
        scratch_of(depth, rows),
        flops=400 * cells,
    )
    own, half, corner_1, corner_2 = lax.optimization_barrier((own, half, corner_1, corner_2))
    other = lax.ppermute(own, "gy", partner)
    velocity, ghost, out_a, out_b, out_c = call(
        ghost_kernel,
        [par, half, fine_medium, own, other, corner_1, corner_2,
         parent_rows.reshape(1, rows), parent_cols.reshape(1, cols)],
        [(3,) + shape, (24, rows, cols)] + halves,
    )
    msgs = exchange("gx", out_a, out_b) + exchange("gy", out_c, out_c)
    stress, out_a, out_b, out_c = call(
        stress_kernel,
        [par, velocity, fine_state, fine_medium, ghost, *msgs, tile, halo],
        [(6,) + shape] + halves,
        scratch_of(depth, rows),
        flops=400 * cells,
    )
    msgs = exchange("gx", out_a, out_b) + exchange("gy", out_c, out_c)
    velocity, out_a, out_b, out_c = call(
        velocity_kernel,
        [par, velocity, stress, fine_medium, ghost, *msgs, tile, halo],
        [(3,) + shape] + halves,
        scratch_of(depth, rows),
        flops=400 * cells,
    )
    msgs = exchange("gx", out_a, out_b) + exchange("gy", out_c, out_c)
    half_shape = (9, 8, rows, cols)
    lower, lifted = call(
        lower_stress_kernel,
        [par, velocity, stress, fine_medium, ghost, fine_state, *msgs, tile, halo, means],
        [half_shape, (count, LANES)],
        scratch_of(8, rows) + [(rows, cols), (2, count, LANES)],
        parts=[((9,) + shape, (0, depth // 8 - 1, 0, 0))],
        flops=200 * cells,
    )
    own = lax.ppermute(lifted, both, across)
    fine_out, done = call(
        upper_stress_kernel,
        [par, velocity, stress, fine_medium, *msgs, tile, halo],
        [half_shape, (8, LANES)],
        scratch_of(8, rows),
        parts=[((9,) + shape, (0, 0, 0, 0))],
        flops=200 * cells,
        above=lower,
    )
    own, done = lax.optimization_barrier((own, done))
    other = lax.ppermute(own, "gy", partner)

    shape = (thick, part, LANES)
    velocity, ghost, out_1, out_2, out_c = call(
        functools.partial(coarse_velocity_kernel, base_c=rows_msg, base_r=cols_msg),
        [par, coarse_state, coarse_medium, own, other, *begin, tile, halo, done],
        [(3,) + shape, (count, LANES), (coarse_rows, LANES), (coarse_rows, LANES),
         (coarse_cols, LANES)],
        scratch_of(thick, part),
    )
    msgs = exchange("gx", out_c, out_c) + exchange("gy", out_1, out_2)
    (coarse_out,) = call(
        coarse_stress_kernel,
        [par, coarse_state, coarse_medium, velocity, ghost, *msgs, tile, halo],
        [(9,) + shape],
        scratch_of(thick, part),
    )
    return (fine_out, coarse_out)


def solution(mesh):
    placed = (
        P(None, None, "gx", "gy"),
        P(None, None, "gx", "gy"),
        P(None, None, "gy", "gx"),
        P(None, None, "gy", "gx"),
        P(None, None, "gy", "gx"),
        P("gx"),
        P("gy"),
    )
    return jax.shard_map(
        body,
        mesh=mesh,
        in_specs=placed,
        out_specs=(P(None, None, "gx", "gy"), P(None, None, "gy", "gx")),
        check_vma=False,
    )
```

```python
import functools

import jax
import jax.numpy as jnp
import ml_dtypes
import numpy as np
from jax import lax
from jax.experimental import pallas as pl
from jax.experimental.pallas import tpu as pltpu
from jax.sharding import PartitionSpec as P

COEFFS = (1225.0 / 1024.0, -245.0 / 3072.0, 49.0 / 5120.0, -5.0 / 7168.0)
STEP = 0.1
LANES = 128
F32 = jnp.float32
BF16 = jnp.bfloat16

VX, VY, VZ, SXX, SYY, SZZ, SXY, SXZ, SYZ = range(9)
CROSSING = (VX, VY, VZ, SXZ, SYZ, SZZ)
VEL_X = ((SXX, True), (SXY, False), (SXZ, False))
VEL_Y = ((SXY, False), (SYY, True), (SYZ, False))
VEL_Z = ((SXZ, False), (SYZ, False), (SZZ, True))
STR_X = ((VX, False), (VY, True), (VZ, True))
STR_Y = ((VX, True), (VY, False), (VZ, True))
STR_Z = ((VX, True), (VY, True), (VZ, False))


def above_planes(table):
    skip = table is VEL_Z
    return [(k, m) for k, (_, forward) in enumerate(table) for m in range(int(skip and forward), 4)]


def band(width, forward):
    matrix = np.zeros((width + 8, width), np.float64)
    for out in range(width):
        for tap, coeff in enumerate(COEFFS, 1):
            upper = out + tap if forward else out + tap - 1
            lower = out + 1 - tap if forward else out - tap
            matrix[4 + upper, out] += coeff
            matrix[4 + lower, out] -= coeff
    return matrix


def two_part(matrix):
    high = matrix.astype(ml_dtypes.bfloat16)
    low = (matrix - high.astype(np.float64)).astype(ml_dtypes.bfloat16)
    return np.block([[high, low], [high, np.zeros_like(low)]]).astype(ml_dtypes.bfloat16)


def lane_constants():
    tile = np.stack([two_part(band(LANES, f)[4:-4]) for f in (False, True)])
    halo = []
    for parity in range(2):
        for forward in (False, True):
            matrix = band(LANES, forward)
            after = np.zeros((8, LANES))
            before = np.zeros((8, LANES))
            after[:4] = matrix[-4:]
            before[4:] = matrix[:4]
            pair = (after, before) if parity == 0 else (before, after)
            halo.append(two_part(np.concatenate(pair)))
    halo = np.stack(halo).reshape(2, 2, 32, 2 * LANES)
    return tile, halo


def mean_constants():
    half = LANES // 2
    place = np.zeros((2, LANES, LANES), np.float32)
    for lane in range(LANES):
        for part in range(2):
            place[part, lane, part * half + lane // 2] = 1.0 / 16.0
    return np.concatenate([place, place], axis=1).astype(ml_dtypes.bfloat16)


def split(x):
    high = x.astype(BF16)
    return high, (x - high.astype(F32)).astype(BF16)


def fold(x):
    half = x.shape[1] // 2
    return x[:, :half] + x[:, half:]


def dot(a, b, dims=((1,), (0,))):
    return lax.dot_general(a, b, (dims, ((), ())), preferred_element_type=F32)


def dot_lanes(x, matrix):
    return fold(dot(jnp.concatenate(split(x), axis=1), matrix))


def dot_rows(x, matrix):
    return fold(dot(jnp.concatenate(split(x), axis=0), matrix, ((0,), (0,))))


def flat(x):
    return x.reshape(x.shape[0] * x.shape[1], x.shape[2])


def upper_half(shape):
    return lax.broadcasted_iota(jnp.int32, shape, 0) < 4


def put_rows(out_a, out_b, base, fields, parity):
    parts = []
    for ref, f in fields:
        rows = ref.shape[2]
        parts.append((ref.at[:, :, 0:8, :], ref.at[:, :, rows - 8 : rows, :], f))
    put_edge_rows(out_a, out_b, base, parts, parity)


def put_edge_rows(out_a, out_b, base, fields, parity):
    even = parity == 0
    top = upper_half((8, LANES))
    for k, (head, tail, f) in enumerate(fields):
        depth = head.shape[1]
        for z in range(0, depth, 2):
            first = jnp.where(top, head[f, z], pltpu.roll(head[f, z + 1], 4, 0))
            last = jnp.where(top, pltpu.roll(tail[f, z], 4, 0), tail[f, z + 1])
            at = pl.ds(base + 4 * (k * depth + z), 8)
            out_a[at, :] = jnp.where(even, last, first)
            out_b[at, :] = jnp.where(even, first, last)


def put_columns(outs, base, fields):
    row = lax.broadcasted_iota(jnp.int32, (8, 2 * LANES), 0)
    lane = lax.broadcasted_iota(jnp.int32, (8, 2 * LANES), 1) % LANES
    edges = (lane == jnp.where(row < 4, row, LANES - 8 + row)).astype(BF16)
    for k, (ref, f) in enumerate(fields):
        x = ref[...] if f is None else flat(ref[f])
        x = jnp.concatenate(split(x), axis=1)
        turned = dot(edges, x, ((1,), (1,)))
        blocks = turned.shape[1] // LANES
        for m in range(blocks):
            for out in outs:
                out[pl.ds(base + 8 * (k * blocks + m), 8), :] = turned[:, m * LANES : (m + 1) * LANES]


def fill_x(ext, fields, msg_a, msg_b, base, parity, low=0, count=None):
    even = parity == 0
    for k, (ref, f) in enumerate(fields):
        depth, rows = ref.shape[1], ref.shape[2]
        layers = depth if count is None else count
        ext[k, :, 8 : 8 + rows, :] = ref[f, low : low + layers]
        for z in range(0, layers, 2):
            at = pl.ds(base + 4 * (k * depth + low + z), 8)
            a, b = msg_a[at, :], msg_b[at, :]
            after, before = jnp.where(even, a, b), jnp.where(even, b, a)
            ext[k, z, 8 + rows : 16 + rows, :] = after
            ext[k, z + 1, 8 + rows : 16 + rows, :] = pltpu.roll(after, 4, 0)
            ext[k, z, 0:8, :] = pltpu.roll(before, 4, 0)
            ext[k, z + 1, 0:8, :] = before


def fill_y(out, fields, directions, msg_a, msg_b, base, parity, tile, halo, low=0, count=None):
    for k, (ref, f) in enumerate(fields):
        depth, rows = ref.shape[1], ref.shape[2]
        layers = depth if count is None else count
        forward = int(directions[k])
        inner = dot_lanes(flat(ref[f, low : low + layers]), tile[forward])
        factor = halo[parity, forward]
        start, blocks = low * rows // LANES, depth * rows // LANES
        for m in range(layers * rows // LANES):
            at = pl.ds(base + 8 * (k * blocks + start + m), 8)
            outer = dot_rows(jnp.concatenate([msg_a[at, :], msg_b[at, :]], axis=0), factor)
            out[k, m * LANES : (m + 1) * LANES, :] = inner[m * LANES : (m + 1) * LANES] + outer


def fill_z(ext, fields, top, bottom, low=0, count=None):
    for k, (ref, f) in enumerate(fields):
        depth = ref.shape[1]
        layers = depth if count is None else count
        first, last = max(low - 4, 0), min(low + layers + 4, depth)
        ext[k, first - low + 4 : last - low + 4] = ref[f, first:last]
        for g in range(first - (low - 4)):
            ext[k, g] = top(k, 4 - first + low - 4 + g)
        for g in range(low + layers + 4 - last):
            ext[k, last - low + 4 + g] = bottom(k, g)


def taps(read, forward):
    total = None
    for tap, coeff in enumerate(COEFFS, 1):
        upper = tap if forward else tap - 1
        lower = 1 - tap if forward else -tap
        term = coeff * (read(upper) - read(lower))
        total = term if total is None else total + term
    return total


def along_x(ext, k, z, rows, forward):
    return taps(lambda d: ext[k, z, 8 + d : 8 + d + rows, :], forward)


def along_z(ext, k, z, forward):
    return taps(lambda d: ext[k, z + 4 + d], forward)


def along_y(values, k, z, rows):
    return values[k, pl.ds(pl.multiple_of(z * rows, rows), rows), :]


def velocity_half(old, buoyancy, out, ex, ey, ez):
    depth, rows = out.shape[1], out.shape[2]

    def layer(z, _):
        scale = STEP * buoyancy[0, z]
        zx = along_z(ez, 0, z, False)
        zy = along_z(ez, 1, z, False)
        zz = along_z(ez, 2, z, True)
        x = along_x(ex, 0, z, rows, True)
        out[0, z] = old[0, z] + scale * (x + along_y(ey, 0, z, rows) + zx)
        x = along_x(ex, 1, z, rows, False)
        out[1, z] = old[1, z] + scale * (x + along_y(ey, 1, z, rows) + zy)
        x = along_x(ex, 2, z, rows, False)
        out[2, z] = old[2, z] + scale * (x + along_y(ey, 2, z, rows) + zz)
        return 0

    lax.fori_loop(0, depth, layer, 0, unroll=2 if rows > 16 else depth)


def stress_half(old, lame, shear, put, low, count, ex, ey, ez):
    rows = ex.shape[2] - 16

    def layer(n, _):
        z = n + low
        exx = along_x(ex, 0, n, rows, False)
        eyy = along_y(ey, 1, n, rows)
        ezz = along_z(ez, 2, n, False)
        mu = STEP * shear(z)
        common = (STEP * lame(z)) * (exx + eyy + ezz)
        double = mu + mu
        put(0, z, n, old(0, z) + (common + double * exx))
        put(1, z, n, old(1, z) + (common + double * eyy))
        put(2, z, n, old(2, z) + (common + double * ezz))
        x = along_x(ex, 1, n, rows, True)
        put(3, z, n, old(3, z) + mu * (along_y(ey, 0, n, rows) + x))
        x = along_x(ex, 2, n, rows, True)
        put(4, z, n, old(4, z) + mu * (along_z(ez, 0, n, True) + x))
        y = along_y(ey, 2, n, rows)
        put(5, z, n, old(5, z) + mu * (along_z(ez, 1, n, True) + y))
        return 0

    lax.fori_loop(0, count, layer, 0, unroll=2 if rows > 16 else count)


def zeros_like_plane(ref):
    return jnp.zeros(ref.shape[-2:], F32)


def pack_kernel(
    par, fine, coarse, past, out_a, out_b, out_1, out_2, planes, outer,
    turned, first, last, state, before, sems,
):
    pi, pj = par[0], par[1]
    depth, rows = fine.shape[1], fine.shape[2]
    part = coarse.shape[2]
    copies = [
        pltpu.make_async_copy(coarse, state, sems.at[0]),
        pltpu.make_async_copy(past, before, sems.at[1]),
    ]
    for k, (f, _) in enumerate(VEL_X):
        head, tail = fine.at[f, :, 0:8, :], fine.at[f, :, rows - 8 : rows, :]
        copies.append(pltpu.make_async_copy(head, first.at[k], sems.at[2 + 2 * k]))
        copies.append(pltpu.make_async_copy(tail, last.at[k], sems.at[3 + 2 * k]))
    for k, (f, _) in enumerate(VEL_Y):
        copies.append(pltpu.make_async_copy(fine.at[f], turned.at[k], sems.at[8 + k]))
    for copy in copies:
        copy.start()
    copies[0].wait()
    copies[1].wait()
    upper = pj == 0
    for n, f in enumerate(CROSSING):
        for layer in range(2):
            now = state[f, layer]
            later = 1.5 * now - 0.5 * before[f, layer]
            for p, plane in ((2 * n + layer, now), (12 + 2 * n + layer, later)):
                planes[pl.ds(p * part, part), :] = plane
                outer[p : p + 1, :] = jnp.where(upper, plane[:1], plane[part - 1 :])
    base = 12 * depth
    put_columns((out_a, out_b), base, [(state, f) for f, _ in VEL_Y])
    put_columns((out_a, out_b), base + 24, [(planes, None)])
    base = 24 * (depth * rows // LANES)
    put_rows(out_1, out_2, base, [(state, f) for f, _ in VEL_X], pj)
    base += 12 * coarse.shape[1]
    out_1[base : base + 24, :] = outer[...]
    out_2[base : base + 24, :] = outer[...]
    for copy in copies[2:8]:
        copy.wait()
    put_edge_rows(out_a, out_b, 0, [(first, last, k) for k in range(3)], pi)
    for k in range(3):
        copies[8 + k].wait()
        base = 8 * k * (depth * rows // LANES)
        put_columns((out_1, out_2), base, [(turned, k)])


def crossing_kernel(par, planes, msg_a, msg_b, msg_2, out):
    count = planes.shape[0]
    blocks = count // LANES
    out[0:count, :] = planes[...]
    out[count : count + 24, :] = msg_2[msg_2.shape[0] - 24 :, :]
    even = par[0] == 0
    base = msg_a.shape[0] - 8 * blocks
    left, right = [], []
    for m in range(blocks):
        a = msg_a[pl.ds(base + 8 * m, 8), :]
        b = msg_b[pl.ds(base + 8 * m, 8), :]
        left.append(jnp.where(even, b, a)[7:8])
        right.append(jnp.where(even, a, b)[0:1])
    fill = [jnp.zeros((8 - blocks, LANES), F32)]
    out[count + 24 : count + 32, :] = jnp.concatenate(left + fill, axis=0)
    out[count + 32 : count + 40, :] = jnp.concatenate(right + fill, axis=0)


def expand_ghosts(par, own, other, corner_1, corner_2, prow, pcol, ghost):
    core = par[1]
    row_base, col_base = par[2], par[3]
    part = (own.shape[0] - 40) // 24
    rows = prow.shape[1]
    low = core == 0
    count = 24 * part
    source = lax.broadcasted_iota(jnp.int32, (LANES, LANES), 0)
    pick_cols = (source == pcol[...] - col_base).astype(BF16)
    pick_cols = jnp.concatenate([pick_cols, pick_cols], axis=0)
    source = lax.broadcasted_iota(jnp.int32, (2 * part, rows), 0)
    pick_rows = (source == prow[...] - row_base).astype(BF16)
    pick_rows = jnp.concatenate([pick_rows, pick_rows], axis=0)

    def spread(x):
        return dot(jnp.concatenate(split(x), axis=1), pick_cols)

    mine, theirs = spread(own[0 : count + 24, :]), spread(other[0 : count + 24, :])
    first, second = jnp.where(low, mine, theirs), jnp.where(low, theirs, mine)
    above, below = first[count:], second[count:]
    beside = []
    for ref in (own, other):
        side = jnp.where(low, ref[count + 24 : count + 32, :], ref[count + 32 : count + 40, :])
        side = jnp.concatenate([side, jnp.zeros((LANES - 8, LANES), F32)], axis=0)
        beside.append(side.T)
    side_1 = jnp.where(low, beside[0], beside[1])
    side_2 = jnp.where(low, beside[1], beside[0])
    turn = jnp.where(low, 1, LANES - 1)
    top = pltpu.roll(jnp.where(low, corner_1[...], corner_2[...]), turn, 1)
    bottom = pltpu.roll(jnp.where(low, corner_2[...], corner_1[...]), turn, 1)

    lane = lax.broadcasted_iota(jnp.int32, (rows, LANES), 1)
    row = lax.broadcasted_iota(jnp.int32, (rows, LANES), 0)
    edge = lane == jnp.where(low, 0, LANES - 1)
    edge_row = edge[:1]
    above = above + jnp.where(edge_row, top, 0.0)
    below = below + jnp.where(edge_row, bottom, 0.0)
    group = LANES // part
    columns = []
    for q in range(group):
        at = slice(q * part, (q + 1) * part)
        column = jnp.concatenate([side_1[at], side_2[at]], axis=0)
        columns.append(dot(pick_rows, jnp.concatenate(split(column), axis=0), ((0,), (0,))))
    for p in range(24):
        at = slice(p * part, (p + 1) * part)
        plane = jnp.concatenate([first[at], second[at]], axis=0)
        full = dot(pick_rows, jnp.concatenate(split(plane), axis=0), ((0,), (0,)))
        column = columns[p % group][:, p // group : p // group + 1]
        full = full + jnp.where(edge, column, 0.0)
        full = full + jnp.where(row == 0, above[p : p + 1], 0.0)
        ghost[p] = full + jnp.where(row == rows - 1, below[p : p + 1], 0.0)


def ghost_kernel(
    par, half, buoyancy, own, other, corner_1, corner_2, prow, pcol,
    out, ghost, out_a, out_b, out_1, out_2,
):
    expand_ghosts(par, own, other, corner_1, corner_2, prow, pcol, ghost)
    depth = half.shape[1]
    for c, (f, forward) in enumerate(VEL_Z):
        out[c, 0 : depth - 4] = half[c, 0 : depth - 4]
        n = CROSSING.index(f)
        planes = [ghost[2 * n], ghost[2 * n + 1]]
        for z in range(depth - 4, depth):
            total = None
            for tap, coeff in enumerate(COEFFS, 1):
                g = z + (tap if forward else tap - 1) - depth
                if g >= 0:
                    term = coeff * planes[g // 2]
                    total = term if total is None else total + term
            value = half[c, z]
            if total is not None:
                value = value + (STEP * buoyancy[0, z]) * total
            out[c, z] = value
    moved = [(out, c) for c in range(3)]
    put_rows(out_a, out_b, 0, moved, par[0])
    put_columns((out_1, out_2), 0, moved)


def stress_fields(ref, table):
    offset = 9 - ref.shape[0]
    return [(ref, f - offset) for f, _ in table]


def velocity_fill(par, stress, msg_a, msg_b, msg_1, msg_2, tile, halo, bottom, ex, ey, ez):
    pi, pj = par[0], par[1]
    none = zeros_like_plane(stress)
    fill_z(ez, stress_fields(stress, VEL_Z), lambda k, g: none, bottom)
    fill_x(ex, stress_fields(stress, VEL_X), msg_a, msg_b, 0, pi)
    fill_y(
        ey, stress_fields(stress, VEL_Y), [d for _, d in VEL_Y], msg_1, msg_2, 0, pj, tile, halo
    )


def first_velocity_kernel(
    par, state, buoyancy, msg_a, msg_b, msg_1, msg_2, tile, halo, out, ex, ey, ez
):
    none = zeros_like_plane(state)
    velocity_fill(
        par, state, msg_a, msg_b, msg_1, msg_2, tile, halo, lambda k, g: none, ex, ey, ez
    )
    velocity_half(state, buoyancy, out, ex, ey, ez)


def velocity_kernel(
    par, old, stress, buoyancy, ghost, start, msg_a, msg_b, msg_1, msg_2, tile, halo, means,
    out, out_a, out_b, out_1, out_2, coarse, ex, ey, ez, summed, halves,
):
    order = [CROSSING.index(f) for f, _ in VEL_Z]
    velocity_fill(
        par, stress, msg_a, msg_b, msg_1, msg_2, tile, halo,
        lambda k, g: ghost[12 + 2 * order[k] + g // 2], ex, ey, ez,
    )
    velocity_half(old, buoyancy, out, ex, ey, ez)
    moved = [(out, c) for c in range(3)]
    put_rows(out_a, out_b, 0, moved, par[0])
    put_columns((out_1, out_2), 0, moved)
    low = out.shape[1] - 8
    lift(start, STR_Z, [out.at[c, low:] for c in range(3)], means, coarse, summed, halves)


def stress_fill(
    par, velocity, bottom, msg_a, msg_b, msg_1, msg_2, tile, halo, ex, ey, ez, low, count
):
    pi, pj = par[0], par[1]
    none = zeros_like_plane(velocity)
    fields = [(velocity, c) for c in range(3)]
    fill_z(ez, fields, lambda k, g: none, bottom, low, count)
    fill_x(ex, fields, msg_a, msg_b, 0, pi, low, count)
    fill_y(
        ey, fields, [d for _, d in STR_Y], msg_1, msg_2, 0, pj, tile, halo, low, count
    )


def stress_kernel(
    par, velocity, state, medium, ghost, msg_a, msg_b, msg_1, msg_2, tile, halo,
    out, out_a, out_b, out_1, out_2, ex, ey, ez,
):
    depth = velocity.shape[1]
    stress_fill(
        par, velocity, lambda k, g: ghost[2 * k + g // 2], msg_a, msg_b, msg_1, msg_2,
        tile, halo, ex, ey, ez, 0, depth,
    )

    def put(c, z, n, value):
        out[c, z] = value

    stress_half(
        lambda c, z: state[SXX + c, z], lambda z: medium[1, z], lambda z: medium[2, z],
        put, 0, depth, ex, ey, ez,
    )
    put_rows(out_a, out_b, 0, stress_fields(out, VEL_X), par[0])
    put_columns((out_1, out_2), 0, stress_fields(out, VEL_Y))


def lift(start, table, fields, means, coarse, summed, halves):
    rows = summed.shape[0]
    part = rows // 4
    low = start.shape[1] - 8
    for n, (k, m) in enumerate(above_planes(table)):
        f, new = table[k][0], fields[k]
        z = 2 * m
        total = (start[f, low + z] + start[f, low + z + 1]) + (new[z] + new[z + 1])
        summed[...] = total
        pairs = summed[pl.ds(0, 2 * part, stride=2), :] + summed[pl.ds(1, 2 * part, stride=2), :]
        at = pl.ds(n * part, part)
        halves[0, at, :] = pairs[:part]
        halves[1, at, :] = pairs[part:]
    count = coarse.shape[0]
    upper = dot(jnp.concatenate(split(halves[0, 0:count]), axis=1), means[0])
    lower = dot(jnp.concatenate(split(halves[1, 0:count]), axis=1), means[1])
    coarse[...] = upper + lower


def lower_stress_kernel(
    par, velocity, stress, medium, ghost, start, msg_a, msg_b, msg_1, msg_2, tile, halo, means,
    out, coarse, ex, ey, ez, summed, halves,
):
    depth, rows = velocity.shape[1], velocity.shape[2]
    low = depth - 8
    stress_fill(
        par, velocity, lambda k, g: ghost[12 + 2 * k + g // 2], msg_a, msg_b, msg_1, msg_2,
        tile, halo, ex, ey, ez, low, 8,
    )

    def put(c, z, n, value):
        out[c, n] = value

    stress_half(
        lambda c, z: stress[c, z], lambda z: medium[1, z], lambda z: medium[2, z],
        put, low, 8, ex, ey, ez,
    )
    fields = [out.at[f - SXX] for f, _ in VEL_Z]
    lift(start, VEL_Z, fields, means, coarse, summed, halves)


def upper_stress_kernel(
    par, below, velocity, stress, medium, msg_a, msg_b, msg_1, msg_2, tile, halo,
    out, done, ex, ey, ez,
):
    stress_fill(
        par, velocity, None, msg_a, msg_b, msg_1, msg_2, tile, halo, ex, ey, ez, 0, 8
    )
    out[0:3] = velocity[...]
    out[SXX:, velocity.shape[1] - 8 :] = below[...]

    def put(c, z, n, value):
        out[SXX + c, n] = value

    stress_half(
        lambda c, z: stress[c, z], lambda z: medium[1, z], lambda z: medium[2, z],
        put, 0, 8, ex, ey, ez,
    )
    done[...] = jnp.zeros_like(done)


def join(par, own, other, ghost, table, rows):
    half = LANES // 2
    even = par[1] == 0
    left = jnp.where(even, own[...], other[...])
    right = jnp.where(even, other[...], own[...])
    low = lax.broadcasted_iota(jnp.int32, left.shape, 1) < half
    ghost[...] = jnp.where(
        even,
        jnp.where(low, left, pltpu.roll(right, half, 1)),
        jnp.where(low, pltpu.roll(left, half, 1), right),
    )
    planes = above_planes(table)
    none = jnp.zeros((rows, LANES), F32)

    def layer(k, m):
        if (k, m) not in planes:
            return none
        return ghost[pl.ds(planes.index((k, m)) * rows, rows), :]

    return layer


def coarse_velocity_kernel(
    par, state, medium, own, other, msg_a, msg_b, msg_1, msg_2, tile, halo, done,
    out, out_1, out_2, out_c, ex, ey, ez, ghost, *, base_c, base_r,
):
    pi, pj = par[0], par[1]
    rows = state.shape[2]
    above = join(par, own, other, ghost, VEL_Z, state.shape[2])
    none = zeros_like_plane(state)
    fill_z(
        ez, stress_fields(state, VEL_Z),
        above, lambda k, g: none,
    )
    fill_x(ex, stress_fields(state, VEL_X), msg_1, msg_2, base_r, pj)
    fill_y(
        ey, stress_fields(state, VEL_Y), [d for _, d in VEL_Y], msg_a, msg_b, base_c, pi,
        tile, halo,
    )
    velocity_half(state, medium, out, ex, ey, ez)
    moved = [(out, c) for c in range(3)]
    put_rows(out_1, out_2, 0, moved, pj)
    put_columns((out_c,), 0, moved)


def coarse_stress_kernel(
    par, state, medium, velocity, own, other, msg_a, msg_b, msg_1, msg_2, tile, halo,
    out, ex, ey, ez, ghost,
):
    pi, pj = par[0], par[1]
    above = join(par, own, other, ghost, STR_Z, state.shape[2])
    depth, rows = state.shape[1], state.shape[2]
    none = zeros_like_plane(state)
    fields = [(velocity, c) for c in range(3)]
    fill_z(
        ez, fields, above, lambda k, g: none
    )
    fill_x(ex, fields, msg_1, msg_2, 0, pj)
    fill_y(ey, fields, [d for _, d in STR_Y], msg_a, msg_b, 0, pi, tile, halo)
    out[0:3] = velocity[...]

    def put(c, z, n, value):
        out[SXX + c, z] = value

    stress_half(
        lambda c, z: state[SXX + c, z], lambda z: medium[1, z], lambda z: medium[2, z],
        put, 0, depth, ex, ey, ez,
    )


def whole(shape):
    return pl.BlockSpec(shape, functools.partial(lambda rank, _: (0,) * rank, len(shape)))


def call(kernel, args, outs, scratch=(), flops=0, copied=0, light=False):
    specs = [pl.BlockSpec(memory_space=pltpu.SMEM)]
    for n, a in enumerate(args[1:]):
        specs.append(pl.BlockSpec(memory_space=pltpu.HBM) if n < copied else whole(a.shape))
    size = 1024 if light else sum(4 * int(np.prod(a.shape)) for a in args) + sum(4 * int(np.prod(o)) for o in outs)
    return pl.pallas_call(
        kernel,
        grid=(1,),
        in_specs=specs,
        out_specs=[whole(o) for o in outs],
        out_shape=[jax.ShapeDtypeStruct(o, F32) for o in outs],
        scratch_shapes=[pltpu.VMEM(s, F32) for s in scratch]
        + ([pltpu.SemaphoreType.DMA((11,))] if copied else []),
        compiler_params=pltpu.CompilerParams(vmem_limit_bytes=(52 if copied else 24) * 1024 * 1024),
        cost_estimate=pl.CostEstimate(flops=flops, bytes_accessed=size, transcendentals=0),
    )(*args)


def matchings(axis):
    size = lax.axis_size(axis)
    result = []
    for start in range(2):
        pairs = []
        for low in range(start, size - 1, 2):
            pairs += [(low, low + 1), (low + 1, low)]
        result.append(pairs)
    return result


def exchange(axis, first, second):
    one, two = matchings(axis)
    return lax.ppermute(first, axis, one), lax.ppermute(second, axis, two)


def body(
    fine_state, fine_medium, coarse_state, coarse_medium, coarse_past, parent_rows, parent_cols
):
    size_x, size_y = lax.axis_size("gx"), lax.axis_size("gy")
    i, j = lax.axis_index("gx"), lax.axis_index("gy")
    depth, rows, cols = fine_state.shape[1:]
    thick, part = coarse_state.shape[1:3]
    blocks = depth * rows // LANES
    par = jnp.stack([i % 2, j % 2, i * (rows // 2), (j // 2) * LANES]).astype(jnp.int32)
    tile, halo = (jnp.asarray(c) for c in lane_constants())
    means = jnp.asarray(mean_constants())
    across = [
        (p * size_y + q, (q // 2) * size_y + 2 * p + q % 2)
        for p in range(size_x)
        for q in range(size_y)
    ]
    partner = matchings("gy")[0]

    corners = ([], [])
    for a in range(size_x):
        for b in range(size_y):
            above = b % 2 == 1
            chip = b // 2 + 1 if above else b // 2 - 1
            for n in range(2):
                left = above if n == 0 else not above
                near = a + 1 if left else a - 1
                if 0 <= chip < size_x and 0 <= near < size_x:
                    corners[n].append((a * size_y + b, chip * size_y + 2 * near + (0 if left else 1)))
    both = ("gx", "gy")

    rows_msg, cols_msg = 12 * depth, 24 * blocks
    coarse_cols, coarse_rows = 24, 12 * thick
    count = 24 * part
    out_a, out_b, out_1, out_2, planes, outer = call(
        pack_kernel,
        [par, fine_state, coarse_state, coarse_past],
        [(rows_msg + coarse_cols + count * 8 // LANES, LANES)] * 2
        + [(cols_msg + coarse_rows + 24, LANES)] * 2
        + [(count, LANES), (24, LANES)],
        [(3,) + fine_state.shape[1:], (3, depth, 8, cols), (3, depth, 8, cols),
         coarse_state.shape, coarse_past.shape],
        copied=3,
    )
    msg_a, msg_b = exchange("gx", out_a, out_b)
    msg_1, msg_2 = exchange("gy", out_1, out_2)
    begin = msg_a, msg_b, msg_1, msg_2
    (crossing,) = call(
        crossing_kernel, [par, planes, msg_a, msg_b, msg_2], [(count + 40, LANES)]
    )
    crossing, outer = lax.optimization_barrier((crossing, outer))
    own = lax.ppermute(crossing, both, across)
    corner_1 = lax.ppermute(outer, both, corners[0])
    corner_2 = lax.ppermute(outer, both, corners[1])

    shape = (depth, rows, cols)

    def scratch_of(depth, rows):
        return [
            (3, depth, rows + 16, LANES), (3, depth * rows, LANES), (3, depth + 8, rows, LANES),
        ]

    cells = depth * rows * cols
    halves = [(rows_msg, LANES)] * 2 + [(cols_msg + 16, LANES), (cols_msg + 8, LANES)]
    (half,) = call(
        first_velocity_kernel,
        [par, fine_state, fine_medium, msg_a, msg_b, msg_1, msg_2, tile, halo],
        [(3,) + shape],
        scratch_of(depth, rows),
        flops=400 * cells,
    )
    own, half, corner_1, corner_2 = lax.optimization_barrier((own, half, corner_1, corner_2))
    other = lax.ppermute(own, "gy", partner)
    velocity, ghost, out_a, out_b, out_1, out_2 = call(
        ghost_kernel,
        [par, half, fine_medium, own, other, corner_1, corner_2,
         parent_rows.reshape(1, rows), parent_cols.reshape(1, cols)],
        [(3,) + shape, (24, rows, cols)] + halves,
    )
    msgs = exchange("gx", out_a, out_b) + exchange("gy", out_1, out_2)
    stress, out_a, out_b, out_1, out_2 = call(
        stress_kernel,
        [par, velocity, fine_state, fine_medium, ghost, *msgs, tile, halo],
        [(6,) + shape] + halves,
        scratch_of(depth, rows),
        flops=400 * cells,
    )
    msgs = exchange("gx", out_a, out_b) + exchange("gy", out_1, out_2)
    moved_v, moved_s = (len(above_planes(t)) * part for t in (STR_Z, VEL_Z))
    lift_scratch = [(rows, cols), (2, count // 2, LANES)]
    velocity, out_a, out_b, out_1, out_2, lifted = call(
        velocity_kernel,
        [par, velocity, stress, fine_medium, ghost, fine_state, *msgs, tile, halo, means],
        [(3,) + shape] + halves + [(moved_v, LANES)],
        scratch_of(depth, rows) + lift_scratch,
        flops=400 * cells,
    )
    msgs = exchange("gx", out_a, out_b) + exchange("gy", out_1, out_2)
    moving = lax.ppermute(lifted, both, across)
    below, lifted = call(
        lower_stress_kernel,
        [par, velocity, stress, fine_medium, ghost, fine_state, *msgs, tile, halo, means],
        [(6, 8, rows, cols), (moved_s, LANES)],
        scratch_of(8, rows) + lift_scratch,
        light=True,
    )
    own = lax.ppermute(lifted, both, across)
    fine_out, done = call(
        upper_stress_kernel,
        [par, below, velocity, stress, fine_medium, *msgs, tile, halo],
        [(9,) + shape, (8, LANES)],
        scratch_of(8, rows),
        flops=200 * cells,
    )
    own, done, moving = lax.optimization_barrier((own, done, moving))
    other = lax.ppermute(own, "gy", partner)
    moving_other = lax.ppermute(moving, "gy", partner)

    shape = (thick, part, LANES)
    velocity, out_1, out_2, out_c = call(
        functools.partial(coarse_velocity_kernel, base_c=rows_msg, base_r=cols_msg),
        [par, coarse_state, coarse_medium, own, other, *begin, tile, halo, done],
        [(3,) + shape, (coarse_rows, LANES), (coarse_rows, LANES), (coarse_cols, LANES)],
        scratch_of(thick, part) + [(moved_s, LANES)],
    )
    msgs = exchange("gx", out_c, out_c) + exchange("gy", out_1, out_2)
    (coarse_out,) = call(
        coarse_stress_kernel,
        [par, coarse_state, coarse_medium, velocity, moving, moving_other, *msgs, tile, halo],
        [(9,) + shape],
        scratch_of(thick, part) + [(moved_v, LANES)],
    )
    return (fine_out, coarse_out)


def solution(mesh):
    placed = (
        P(None, None, "gx", "gy"),
        P(None, None, "gx", "gy"),
        P(None, None, "gy", "gx"),
        P(None, None, "gy", "gx"),
        P(None, None, "gy", "gx"),
        P("gx"),
        P("gy"),
    )
    return jax.shard_map(
        body,
        mesh=mesh,
        in_specs=placed,
        out_specs=(P(None, None, "gx", "gy"), P(None, None, "gy", "gx")),
        check_vma=False,
    )
```

```python
import functools

import jax
import jax.numpy as jnp
import ml_dtypes
import numpy as np
from jax import lax
from jax.experimental import pallas as pl
from jax.experimental.pallas import tpu as pltpu
from jax.sharding import PartitionSpec as P

COEFFS = (1225.0 / 1024.0, -245.0 / 3072.0, 49.0 / 5120.0, -5.0 / 7168.0)
STEP = 0.1
LANES = 128
F32 = jnp.float32
BF16 = jnp.bfloat16

VX, VY, VZ, SXX, SYY, SZZ, SXY, SXZ, SYZ = range(9)
CROSSING = (VX, VY, VZ, SXZ, SYZ, SZZ)
VEL_X = ((SXX, True), (SXY, False), (SXZ, False))
VEL_Y = ((SXY, False), (SYY, True), (SYZ, False))
VEL_Z = ((SXZ, False), (SYZ, False), (SZZ, True))
STR_X = ((VX, False), (VY, True), (VZ, True))
STR_Y = ((VX, True), (VY, False), (VZ, True))
STR_Z = ((VX, True), (VY, True), (VZ, False))


def above_planes(table):
    skip = table is VEL_Z
    return [(k, m) for k, (_, forward) in enumerate(table) for m in range(int(skip and forward), 4)]


def band(width, forward):
    matrix = np.zeros((width + 8, width), np.float64)
    for out in range(width):
        for tap, coeff in enumerate(COEFFS, 1):
            upper = out + tap if forward else out + tap - 1
            lower = out + 1 - tap if forward else out - tap
            matrix[4 + upper, out] += coeff
            matrix[4 + lower, out] -= coeff
    return matrix


def two_part(matrix):
    high = matrix.astype(ml_dtypes.bfloat16)
    low = (matrix - high.astype(np.float64)).astype(ml_dtypes.bfloat16)
    return np.block([[high, low], [high, np.zeros_like(low)]]).astype(ml_dtypes.bfloat16)


def lane_constants():
    tile = np.stack([two_part(band(LANES, f)[4:-4]) for f in (False, True)])
    halo = []
    for parity in range(2):
        for forward in (False, True):
            matrix = band(LANES, forward)
            after = np.zeros((8, LANES))
            before = np.zeros((8, LANES))
            after[:4] = matrix[-4:]
            before[4:] = matrix[:4]
            pair = (after, before) if parity == 0 else (before, after)
            halo.append(two_part(np.concatenate(pair)))
    halo = np.stack(halo).reshape(2, 2, 32, 2 * LANES)
    return tile, halo


def mean_constants():
    half = LANES // 2
    place = np.zeros((2, LANES, LANES), np.float32)
    for lane in range(LANES):
        for part in range(2):
            place[part, lane, part * half + lane // 2] = 1.0 / 16.0
    return np.concatenate([place, place], axis=1).astype(ml_dtypes.bfloat16)


def split(x):
    high = x.astype(BF16)
    return high, (x - high.astype(F32)).astype(BF16)


def fold(x):
    half = x.shape[1] // 2
    return x[:, :half] + x[:, half:]


def dot(a, b, dims=((1,), (0,))):
    return lax.dot_general(a, b, (dims, ((), ())), preferred_element_type=F32)


def dot_lanes(x, matrix):
    return fold(dot(jnp.concatenate(split(x), axis=1), matrix))


def dot_rows(x, matrix):
    return fold(dot(jnp.concatenate(split(x), axis=0), matrix, ((0,), (0,))))


def flat(x):
    return x.reshape(x.shape[0] * x.shape[1], x.shape[2])


def upper_half(shape):
    return lax.broadcasted_iota(jnp.int32, shape, 0) < 4


def put_rows(out_a, out_b, base, fields, parity):
    parts = []
    for ref, f in fields:
        rows = ref.shape[2]
        parts.append((ref.at[:, :, 0:8, :], ref.at[:, :, rows - 8 : rows, :], f))
    put_edge_rows(out_a, out_b, base, parts, parity)


def put_edge_rows(out_a, out_b, base, fields, parity):
    even = parity == 0
    top = upper_half((8, LANES))
    for k, (head, tail, f) in enumerate(fields):
        depth = head.shape[1]
        for z in range(0, depth, 2):
            first = jnp.where(top, head[f, z], pltpu.roll(head[f, z + 1], 4, 0))
            last = jnp.where(top, pltpu.roll(tail[f, z], 4, 0), tail[f, z + 1])
            at = pl.ds(base + 4 * (k * depth + z), 8)
            out_a[at, :] = jnp.where(even, last, first)
            out_b[at, :] = jnp.where(even, first, last)


def put_columns(outs, base, fields):
    row = lax.broadcasted_iota(jnp.int32, (8, 2 * LANES), 0)
    lane = lax.broadcasted_iota(jnp.int32, (8, 2 * LANES), 1) % LANES
    edges = (lane == jnp.where(row < 4, row, LANES - 8 + row)).astype(BF16)
    for k, (ref, f) in enumerate(fields):
        x = ref[...] if f is None else flat(ref[f])
        x = jnp.concatenate(split(x), axis=1)
        turned = dot(edges, x, ((1,), (1,)))
        blocks = turned.shape[1] // LANES
        for m in range(blocks):
            for out in outs:
                out[pl.ds(base + 8 * (k * blocks + m), 8), :] = turned[:, m * LANES : (m + 1) * LANES]


def fill_x(ext, fields, msg_a, msg_b, base, parity, low=0, count=None):
    even = parity == 0
    for k, (ref, f) in enumerate(fields):
        depth, rows = ref.shape[1], ref.shape[2]
        layers = depth if count is None else count
        ext[k, :, 8 : 8 + rows, :] = ref[f, low : low + layers]
        for z in range(0, layers, 2):
            at = pl.ds(base + 4 * (k * depth + low + z), 8)
            a, b = msg_a[at, :], msg_b[at, :]
            after, before = jnp.where(even, a, b), jnp.where(even, b, a)
            ext[k, z, 8 + rows : 16 + rows, :] = after
            ext[k, z + 1, 8 + rows : 16 + rows, :] = pltpu.roll(after, 4, 0)
            ext[k, z, 0:8, :] = pltpu.roll(before, 4, 0)
            ext[k, z + 1, 0:8, :] = before


def fill_y(out, fields, directions, msg_a, msg_b, base, parity, tile, halo, low=0, count=None):
    for k, (ref, f) in enumerate(fields):
        depth, rows = ref.shape[1], ref.shape[2]
        layers = depth if count is None else count
        forward = int(directions[k])
        inner = dot_lanes(flat(ref[f, low : low + layers]), tile[forward])
        factor = halo[parity, forward]
        start, blocks = low * rows // LANES, depth * rows // LANES
        for m in range(layers * rows // LANES):
            at = pl.ds(base + 8 * (k * blocks + start + m), 8)
            outer = dot_rows(jnp.concatenate([msg_a[at, :], msg_b[at, :]], axis=0), factor)
            out[k, m * LANES : (m + 1) * LANES, :] = inner[m * LANES : (m + 1) * LANES] + outer


def fill_z(ext, fields, top, bottom, low=0, count=None):
    for k, (ref, f) in enumerate(fields):
        depth = ref.shape[1]
        layers = depth if count is None else count
        first, last = max(low - 4, 0), min(low + layers + 4, depth)
        ext[k, first - low + 4 : last - low + 4] = ref[f, first:last]
        for g in range(first - (low - 4)):
            ext[k, g] = top(k, 4 - first + low - 4 + g)
        for g in range(low + layers + 4 - last):
            ext[k, last - low + 4 + g] = bottom(k, g)


def taps(read, forward):
    total = None
    for tap, coeff in enumerate(COEFFS, 1):
        upper = tap if forward else tap - 1
        lower = 1 - tap if forward else -tap
        term = coeff * (read(upper) - read(lower))
        total = term if total is None else total + term
    return total


def along_x(ext, k, z, rows, forward):
    return taps(lambda d: ext[k, z, 8 + d : 8 + d + rows, :], forward)


def along_z(ext, k, z, forward):
    return taps(lambda d: ext[k, z + 4 + d], forward)


def along_y(values, k, z, rows):
    return values[k, pl.ds(pl.multiple_of(z * rows, rows), rows), :]


def velocity_half(old, buoyancy, out, ex, ey, ez):
    depth, rows = out.shape[1], out.shape[2]

    def layer(z, _):
        scale = STEP * buoyancy[0, z]
        zx = along_z(ez, 0, z, False)
        zy = along_z(ez, 1, z, False)
        zz = along_z(ez, 2, z, True)
        x = along_x(ex, 0, z, rows, True)
        out[0, z] = old[0, z] + scale * (x + along_y(ey, 0, z, rows) + zx)
        x = along_x(ex, 1, z, rows, False)
        out[1, z] = old[1, z] + scale * (x + along_y(ey, 1, z, rows) + zy)
        x = along_x(ex, 2, z, rows, False)
        out[2, z] = old[2, z] + scale * (x + along_y(ey, 2, z, rows) + zz)
        return 0

    lax.fori_loop(0, depth, layer, 0, unroll=4 if rows > 16 else depth)


def stress_half(old, lame, shear, put, low, count, ex, ey, ez):
    rows = ex.shape[2] - 16

    def layer(n, _):
        z = n + low
        exx = along_x(ex, 0, n, rows, False)
        eyy = along_y(ey, 1, n, rows)
        ezz = along_z(ez, 2, n, False)
        mu = STEP * shear(z)
        common = (STEP * lame(z)) * (exx + eyy + ezz)
        double = mu + mu
        put(0, z, n, old(0, z) + (common + double * exx))
        put(1, z, n, old(1, z) + (common + double * eyy))
        put(2, z, n, old(2, z) + (common + double * ezz))
        x = along_x(ex, 1, n, rows, True)
        put(3, z, n, old(3, z) + mu * (along_y(ey, 0, n, rows) + x))
        x = along_x(ex, 2, n, rows, True)
        put(4, z, n, old(4, z) + mu * (along_z(ez, 0, n, True) + x))
        y = along_y(ey, 2, n, rows)
        put(5, z, n, old(5, z) + mu * (along_z(ez, 1, n, True) + y))
        return 0

    lax.fori_loop(0, count, layer, 0, unroll=4 if rows > 16 else count)


def zeros_like_plane(ref):
    return jnp.zeros(ref.shape[-2:], F32)


def pack_kernel(
    par, fine, coarse, past, out_a, out_b, out_1, out_2, planes, outer,
    turned, first, last, state, before, sems,
):
    pi, pj = par[0], par[1]
    depth, rows = fine.shape[1], fine.shape[2]
    part = coarse.shape[2]
    copies = [
        pltpu.make_async_copy(coarse, state, sems.at[0]),
        pltpu.make_async_copy(past, before, sems.at[1]),
    ]
    for k, (f, _) in enumerate(VEL_X):
        head, tail = fine.at[f, :, 0:8, :], fine.at[f, :, rows - 8 : rows, :]
        copies.append(pltpu.make_async_copy(head, first.at[k], sems.at[2 + 2 * k]))
        copies.append(pltpu.make_async_copy(tail, last.at[k], sems.at[3 + 2 * k]))
    for k, (f, _) in enumerate(VEL_Y):
        copies.append(pltpu.make_async_copy(fine.at[f], turned.at[k], sems.at[8 + k]))
    for copy in copies:
        copy.start()
    copies[0].wait()
    copies[1].wait()
    upper = pj == 0
    for n, f in enumerate(CROSSING):
        for layer in range(2):
            now = state[f, layer]
            later = 1.5 * now - 0.5 * before[f, layer]
            for p, plane in ((2 * n + layer, now), (12 + 2 * n + layer, later)):
                planes[pl.ds(p * part, part), :] = plane
                outer[p : p + 1, :] = jnp.where(upper, plane[:1], plane[part - 1 :])
    base = 12 * depth
    put_columns((out_a, out_b), base, [(state, f) for f, _ in VEL_Y])
    put_columns((out_a, out_b), base + 24, [(planes, None)])
    base = 24 * (depth * rows // LANES)
    put_rows(out_1, out_2, base, [(state, f) for f, _ in VEL_X], pj)
    base += 12 * coarse.shape[1]
    out_1[base : base + 24, :] = outer[...]
    out_2[base : base + 24, :] = outer[...]
    for copy in copies[2:8]:
        copy.wait()
    put_edge_rows(out_a, out_b, 0, [(first, last, k) for k in range(3)], pi)
    for k in range(3):
        copies[8 + k].wait()
        base = 8 * k * (depth * rows // LANES)
        put_columns((out_1, out_2), base, [(turned, k)])


def crossing_kernel(par, planes, msg_a, msg_b, msg_2, first, second):
    count = planes.shape[0]
    blocks = count // LANES
    even = par[0] == 0
    base = msg_a.shape[0] - 8 * blocks
    left, right = [], []
    for m in range(blocks):
        a = msg_a[pl.ds(base + 8 * m, 8), :]
        b = msg_b[pl.ds(base + 8 * m, 8), :]
        left.append(jnp.where(even, b, a)[7:8])
        right.append(jnp.where(even, a, b)[0:1])
    fill = [jnp.zeros((8 - blocks, LANES), F32)]
    left, right = (jnp.concatenate(side + fill, axis=0) for side in (left, right))
    half = count // 2
    first[0:half, :] = planes[:half, :]
    first[half : half + 24, :] = msg_2[msg_2.shape[0] - 24 :, :]
    first[half + 24 : half + 32, :] = left
    first[half + 32 : half + 40, :] = right
    second[...] = planes[half:, :]


def expand_ghosts(par, own, other, corner_1, corner_2, prow, pcol, ghost, level, planes):
    core = par[1]
    row_base, col_base = par[2], par[3]
    part = (own.shape[0] - 40) // 12
    rows = prow.shape[1]
    low = core == 0
    count = 12 * part
    source = lax.broadcasted_iota(jnp.int32, (LANES, LANES), 0)
    pick_cols = (source == pcol[...] - col_base).astype(BF16)
    pick_cols = jnp.concatenate([pick_cols, pick_cols], axis=0)
    source = lax.broadcasted_iota(jnp.int32, (2 * part, rows), 0)
    pick_rows = (source == prow[...] - row_base).astype(BF16)
    pick_rows = jnp.concatenate([pick_rows, pick_rows], axis=0)

    def spread(x):
        return dot(jnp.concatenate(split(x), axis=1), pick_cols)

    mine, theirs = (
        spread(jnp.concatenate([main[0:count, :], ref[count : count + 24, :]], axis=0))
        for main, ref in zip(planes, (own, other))
    )
    first, second = jnp.where(low, mine, theirs), jnp.where(low, theirs, mine)
    above, below = first[count:], second[count:]
    beside = []
    for ref in (own, other):
        side = jnp.where(low, ref[count + 24 : count + 32, :], ref[count + 32 : count + 40, :])
        side = jnp.concatenate([side, jnp.zeros((LANES - 8, LANES), F32)], axis=0)
        beside.append(side.T)
    side_1 = jnp.where(low, beside[0], beside[1])
    side_2 = jnp.where(low, beside[1], beside[0])
    turn = jnp.where(low, 1, LANES - 1)
    top = pltpu.roll(jnp.where(low, corner_1[...], corner_2[...]), turn, 1)
    bottom = pltpu.roll(jnp.where(low, corner_2[...], corner_1[...]), turn, 1)

    lane = lax.broadcasted_iota(jnp.int32, (rows, LANES), 1)
    row = lax.broadcasted_iota(jnp.int32, (rows, LANES), 0)
    edge = lane == jnp.where(low, 0, LANES - 1)
    edge_row = edge[:1]
    above = above + jnp.where(edge_row, top, 0.0)
    below = below + jnp.where(edge_row, bottom, 0.0)
    group = LANES // part
    columns = []
    for q in range(group):
        at = slice(q * part, (q + 1) * part)
        column = jnp.concatenate([side_1[at], side_2[at]], axis=0)
        columns.append(dot(pick_rows, jnp.concatenate(split(column), axis=0), ((0,), (0,))))
    for n in range(12):
        p = 12 * level + n
        at = slice(n * part, (n + 1) * part)
        plane = jnp.concatenate([first[at], second[at]], axis=0)
        full = dot(pick_rows, jnp.concatenate(split(plane), axis=0), ((0,), (0,)))
        column = columns[p % group][:, p // group : p // group + 1]
        full = full + jnp.where(edge, column, 0.0)
        full = full + jnp.where(row == 0, above[p : p + 1], 0.0)
        ghost[n] = full + jnp.where(row == rows - 1, below[p : p + 1], 0.0)


def later_ghost_kernel(
    par, own, other, corner_1, corner_2, prow, pcol, later_own, later_other, ghost
):
    planes = later_own, later_other
    expand_ghosts(par, own, other, corner_1, corner_2, prow, pcol, ghost, 1, planes)


def ghost_kernel(
    par, half, buoyancy, own, other, corner_1, corner_2, prow, pcol,
    out, ghost, out_a, out_b, out_1, out_2,
):
    planes = own, other
    expand_ghosts(par, own, other, corner_1, corner_2, prow, pcol, ghost, 0, planes)
    depth = half.shape[1]
    for c, (f, forward) in enumerate(VEL_Z):
        out[c, 0 : depth - 4] = half[c, 0 : depth - 4]
        n = CROSSING.index(f)
        planes = [ghost[2 * n], ghost[2 * n + 1]]
        for z in range(depth - 4, depth):
            total = None
            for tap, coeff in enumerate(COEFFS, 1):
                g = z + (tap if forward else tap - 1) - depth
                if g >= 0:
                    term = coeff * planes[g // 2]
                    total = term if total is None else total + term
            value = half[c, z]
            if total is not None:
                value = value + (STEP * buoyancy[0, z]) * total
            out[c, z] = value
    moved = [(out, c) for c in range(3)]
    put_rows(out_a, out_b, 0, moved, par[0])
    put_columns((out_1, out_2), 0, moved)


def stress_fields(ref, table):
    offset = 9 - ref.shape[0]
    return [(ref, f - offset) for f, _ in table]


def velocity_fill(par, stress, msg_a, msg_b, msg_1, msg_2, tile, halo, bottom, ex, ey, ez):
    pi, pj = par[0], par[1]
    none = zeros_like_plane(stress)
    fill_z(ez, stress_fields(stress, VEL_Z), lambda k, g: none, bottom)
    fill_x(ex, stress_fields(stress, VEL_X), msg_a, msg_b, 0, pi)
    fill_y(
        ey, stress_fields(stress, VEL_Y), [d for _, d in VEL_Y], msg_1, msg_2, 0, pj, tile, halo
    )


def first_velocity_kernel(
    par, state, buoyancy, msg_a, msg_b, msg_1, msg_2, tile, halo, out, ex, ey, ez
):
    none = zeros_like_plane(state)
    velocity_fill(
        par, state, msg_a, msg_b, msg_1, msg_2, tile, halo, lambda k, g: none, ex, ey, ez
    )
    velocity_half(state, buoyancy, out, ex, ey, ez)


def velocity_kernel(
    par, old, stress, buoyancy, ghost, start, msg_a, msg_b, msg_1, msg_2, tile, halo, means,
    out, out_a, out_b, out_1, out_2, coarse, ex, ey, ez, summed, halves,
):
    order = [CROSSING.index(f) for f, _ in VEL_Z]
    velocity_fill(
        par, stress, msg_a, msg_b, msg_1, msg_2, tile, halo,
        lambda k, g: ghost[2 * order[k] + g // 2], ex, ey, ez,
    )
    velocity_half(old, buoyancy, out, ex, ey, ez)
    moved = [(out, c) for c in range(3)]
    put_rows(out_a, out_b, 0, moved, par[0])
    put_columns((out_1, out_2), 0, moved)
    low = out.shape[1] - 8
    lift(start, STR_Z, [out.at[c, low:] for c in range(3)], means, coarse, summed, halves)


def stress_fill(
    par, velocity, bottom, msg_a, msg_b, msg_1, msg_2, tile, halo, ex, ey, ez, low, count
):
    pi, pj = par[0], par[1]
    none = zeros_like_plane(velocity)
    fields = [(velocity, c) for c in range(3)]
    fill_z(ez, fields, lambda k, g: none, bottom, low, count)
    fill_x(ex, fields, msg_a, msg_b, 0, pi, low, count)
    fill_y(
        ey, fields, [d for _, d in STR_Y], msg_1, msg_2, 0, pj, tile, halo, low, count
    )


def stress_kernel(
    par, velocity, state, medium, ghost, msg_a, msg_b, msg_1, msg_2, tile, halo,
    out, out_a, out_b, out_1, out_2, ex, ey, ez,
):
    depth = velocity.shape[1]
    stress_fill(
        par, velocity, lambda k, g: ghost[2 * k + g // 2], msg_a, msg_b, msg_1, msg_2,
        tile, halo, ex, ey, ez, 0, depth,
    )

    def put(c, z, n, value):
        out[c, z] = value

    stress_half(
        lambda c, z: state[SXX + c, z], lambda z: medium[1, z], lambda z: medium[2, z],
        put, 0, depth, ex, ey, ez,
    )
    put_rows(out_a, out_b, 0, stress_fields(out, VEL_X), par[0])
    put_columns((out_1, out_2), 0, stress_fields(out, VEL_Y))


def lift(start, table, fields, means, coarse, summed, halves):
    rows = summed.shape[0]
    part = rows // 4
    low = start.shape[1] - 8
    for n, (k, m) in enumerate(above_planes(table)):
        f, new = table[k][0], fields[k]
        z = 2 * m
        total = (start[f, low + z] + start[f, low + z + 1]) + (new[z] + new[z + 1])
        summed[...] = total
        pairs = summed[pl.ds(0, 2 * part, stride=2), :] + summed[pl.ds(1, 2 * part, stride=2), :]
        at = pl.ds(n * part, part)
        halves[0, at, :] = pairs[:part]
        halves[1, at, :] = pairs[part:]
    count = coarse.shape[0]
    upper = dot(jnp.concatenate(split(halves[0, 0:count]), axis=1), means[0])
    lower = dot(jnp.concatenate(split(halves[1, 0:count]), axis=1), means[1])
    coarse[...] = upper + lower


def lower_stress_kernel(
    par, velocity, stress, medium, ghost, start, msg_a, msg_b, msg_1, msg_2, tile, halo, means,
    out, coarse, ex, ey, ez, summed, halves,
):
    depth, rows = velocity.shape[1], velocity.shape[2]
    low = depth - 8
    stress_fill(
        par, velocity, lambda k, g: ghost[2 * k + g // 2], msg_a, msg_b, msg_1, msg_2,
        tile, halo, ex, ey, ez, low, 8,
    )

    def put(c, z, n, value):
        out[c, n] = value

    stress_half(
        lambda c, z: stress[c, z], lambda z: medium[1, z], lambda z: medium[2, z],
        put, low, 8, ex, ey, ez,
    )
    fields = [out.at[f - SXX] for f, _ in VEL_Z]
    lift(start, VEL_Z, fields, means, coarse, summed, halves)


def upper_stress_kernel(
    par, below, velocity, stress, medium, msg_a, msg_b, msg_1, msg_2, tile, halo,
    out, done, ex, ey, ez,
):
    stress_fill(
        par, velocity, None, msg_a, msg_b, msg_1, msg_2, tile, halo, ex, ey, ez, 0, 8
    )
    out[0:3] = velocity[...]
    out[SXX:, velocity.shape[1] - 8 :] = below[...]

    def put(c, z, n, value):
        out[SXX + c, n] = value

    stress_half(
        lambda c, z: stress[c, z], lambda z: medium[1, z], lambda z: medium[2, z],
        put, 0, 8, ex, ey, ez,
    )
    done[...] = jnp.zeros_like(done)


def join(par, own, other, ghost, table, rows):
    half = LANES // 2
    even = par[1] == 0
    left = jnp.where(even, own[...], other[...])
    right = jnp.where(even, other[...], own[...])
    low = lax.broadcasted_iota(jnp.int32, left.shape, 1) < half
    ghost[...] = jnp.where(
        even,
        jnp.where(low, left, pltpu.roll(right, half, 1)),
        jnp.where(low, pltpu.roll(left, half, 1), right),
    )
    planes = above_planes(table)
    none = jnp.zeros((rows, LANES), F32)

    def layer(k, m):
        if (k, m) not in planes:
            return none
        return ghost[pl.ds(planes.index((k, m)) * rows, rows), :]

    return layer


def coarse_velocity_kernel(
    par, state, medium, own, other, msg_a, msg_b, msg_1, msg_2, tile, halo, done,
    out, out_1, out_2, out_c, ex, ey, ez, ghost, *, base_c, base_r,
):
    pi, pj = par[0], par[1]
    rows = state.shape[2]
    above = join(par, own, other, ghost, VEL_Z, state.shape[2])
    none = zeros_like_plane(state)
    fill_z(
        ez, stress_fields(state, VEL_Z),
        above, lambda k, g: none,
    )
    fill_x(ex, stress_fields(state, VEL_X), msg_1, msg_2, base_r, pj)
    fill_y(
        ey, stress_fields(state, VEL_Y), [d for _, d in VEL_Y], msg_a, msg_b, base_c, pi,
        tile, halo,
    )
    velocity_half(state, medium, out, ex, ey, ez)
    moved = [(out, c) for c in range(3)]
    put_rows(out_1, out_2, 0, moved, pj)
    put_columns((out_c,), 0, moved)


def coarse_stress_kernel(
    par, state, medium, velocity, own, other, msg_a, msg_b, msg_1, msg_2, tile, halo,
    out, ex, ey, ez, ghost,
):
    pi, pj = par[0], par[1]
    above = join(par, own, other, ghost, STR_Z, state.shape[2])
    depth, rows = state.shape[1], state.shape[2]
    none = zeros_like_plane(state)
    fields = [(velocity, c) for c in range(3)]
    fill_z(
        ez, fields, above, lambda k, g: none
    )
    fill_x(ex, fields, msg_1, msg_2, 0, pj)
    fill_y(ey, fields, [d for _, d in STR_Y], msg_a, msg_b, 0, pi, tile, halo)
    out[0:3] = velocity[...]

    def put(c, z, n, value):
        out[SXX + c, z] = value

    stress_half(
        lambda c, z: state[SXX + c, z], lambda z: medium[1, z], lambda z: medium[2, z],
        put, 0, depth, ex, ey, ez,
    )


def whole(shape):
    return pl.BlockSpec(shape, functools.partial(lambda rank, _: (0,) * rank, len(shape)))


def call(kernel, args, outs, scratch=(), flops=0, copied=0, light=False):
    specs = [pl.BlockSpec(memory_space=pltpu.SMEM)]
    for n, a in enumerate(args[1:]):
        specs.append(pl.BlockSpec(memory_space=pltpu.HBM) if n < copied else whole(a.shape))
    size = 1024 if light else sum(4 * int(np.prod(a.shape)) for a in args) + sum(4 * int(np.prod(o)) for o in outs)
    return pl.pallas_call(
        kernel,
        grid=(1,),
        in_specs=specs,
        out_specs=[whole(o) for o in outs],
        out_shape=[jax.ShapeDtypeStruct(o, F32) for o in outs],
        scratch_shapes=[pltpu.VMEM(s, F32) for s in scratch]
        + ([pltpu.SemaphoreType.DMA((11,))] if copied else []),
        compiler_params=pltpu.CompilerParams(vmem_limit_bytes=(46 if copied else 24) * 1024 * 1024),
        cost_estimate=pl.CostEstimate(flops=flops, bytes_accessed=size, transcendentals=0),
    )(*args)


def matchings(axis):
    size = lax.axis_size(axis)
    result = []
    for start in range(2):
        pairs = []
        for low in range(start, size - 1, 2):
            pairs += [(low, low + 1), (low + 1, low)]
        result.append(pairs)
    return result


def exchange(axis, first, second):
    one, two = matchings(axis)
    return lax.ppermute(first, axis, one), lax.ppermute(second, axis, two)


def body(
    fine_state, fine_medium, coarse_state, coarse_medium, coarse_past, parent_rows, parent_cols
):
    size_x, size_y = lax.axis_size("gx"), lax.axis_size("gy")
    i, j = lax.axis_index("gx"), lax.axis_index("gy")
    depth, rows, cols = fine_state.shape[1:]
    thick, part = coarse_state.shape[1:3]
    blocks = depth * rows // LANES
    par = jnp.stack([i % 2, j % 2, i * (rows // 2), (j // 2) * LANES]).astype(jnp.int32)
    tile, halo = (jnp.asarray(c) for c in lane_constants())
    means = jnp.asarray(mean_constants())
    across = [
        (p * size_y + q, (q // 2) * size_y + 2 * p + q % 2)
        for p in range(size_x)
        for q in range(size_y)
    ]
    partner = matchings("gy")[0]

    corners = ([], [])
    for a in range(size_x):
        for b in range(size_y):
            above = b % 2 == 1
            chip = b // 2 + 1 if above else b // 2 - 1
            for n in range(2):
                left = above if n == 0 else not above
                near = a + 1 if left else a - 1
                if 0 <= chip < size_x and 0 <= near < size_x:
                    corners[n].append((a * size_y + b, chip * size_y + 2 * near + (0 if left else 1)))
    both = ("gx", "gy")

    rows_msg, cols_msg = 12 * depth, 24 * blocks
    coarse_cols, coarse_rows = 24, 12 * thick
    count = 24 * part
    out_a, out_b, out_1, out_2, planes, outer = call(
        pack_kernel,
        [par, fine_state, coarse_state, coarse_past],
        [(rows_msg + coarse_cols + count * 8 // LANES, LANES)] * 2
        + [(cols_msg + coarse_rows + 24, LANES)] * 2
        + [(count, LANES), (24, LANES)],
        [(3,) + fine_state.shape[1:], (3, depth, 8, cols), (3, depth, 8, cols),
         coarse_state.shape, coarse_past.shape],
        copied=3,
    )
    msg_a, msg_b = exchange("gx", out_a, out_b)
    msg_1, msg_2 = exchange("gy", out_1, out_2)
    begin = msg_a, msg_b, msg_1, msg_2
    crossing, later = call(
        crossing_kernel,
        [par, planes, msg_a, msg_b, msg_2],
        [(count // 2 + 40, LANES), (count // 2, LANES)],
    )
    crossing, outer = lax.optimization_barrier((crossing, outer))
    own = lax.ppermute(crossing, both, across)
    corner_1 = lax.ppermute(outer, both, corners[0])
    corner_2 = lax.ppermute(outer, both, corners[1])

    shape = (depth, rows, cols)

    def scratch_of(depth, rows):
        return [
            (3, depth, rows + 16, LANES), (3, depth * rows, LANES), (3, depth + 8, rows, LANES),
        ]

    cells = depth * rows * cols
    halves = [(rows_msg + 8, LANES)] * 2 + [(cols_msg + 24, LANES), (cols_msg + 16, LANES)]
    (half,) = call(
        first_velocity_kernel,
        [par, fine_state, fine_medium, msg_a, msg_b, msg_1, msg_2, tile, halo],
        [(3,) + shape],
        scratch_of(depth, rows),
        flops=400 * cells,
    )
    own, half, corner_1, corner_2 = lax.optimization_barrier((own, half, corner_1, corner_2))
    other = lax.ppermute(own, "gy", partner)
    parents = parent_rows.reshape(1, rows), parent_cols.reshape(1, cols)
    velocity, ghost, out_a, out_b, out_1, out_2 = call(
        ghost_kernel,
        [par, half, fine_medium, own, other, corner_1, corner_2,
         *parents],
        [(3,) + shape, (12, rows, cols)] + halves,
    )
    msgs = exchange("gx", out_a, out_b) + exchange("gy", out_1, out_2)
    later, velocity = lax.optimization_barrier((later, velocity))
    later = lax.ppermute(later, both, across)
    stress, out_a, out_b, out_1, out_2 = call(
        stress_kernel,
        [par, velocity, fine_state, fine_medium, ghost, *msgs, tile, halo],
        [(6,) + shape] + halves,
        scratch_of(depth, rows),
        flops=400 * cells,
    )
    msgs = exchange("gx", out_a, out_b) + exchange("gy", out_1, out_2)
    later, stress = lax.optimization_barrier((later, stress))
    later_other = lax.ppermute(later, "gy", partner)
    (ghost,) = call(
        later_ghost_kernel,
        [par, own, other, corner_1, corner_2, *parents, later, later_other],
        [(12, rows, cols)],
    )
    moved_v, moved_s = (len(above_planes(t)) * part for t in (STR_Z, VEL_Z))
    lift_scratch = [(rows, cols), (2, count // 2, LANES)]
    velocity, out_a, out_b, out_1, out_2, lifted = call(
        velocity_kernel,
        [par, velocity, stress, fine_medium, ghost, fine_state, *msgs, tile, halo, means],
        [(3,) + shape] + halves + [(moved_v, LANES)],
        scratch_of(depth, rows) + lift_scratch,
        flops=400 * cells,
    )
    msgs = exchange("gx", out_a, out_b) + exchange("gy", out_1, out_2)
    moving = lax.ppermute(lifted, both, across)
    below, lifted = call(
        lower_stress_kernel,
        [par, velocity, stress, fine_medium, ghost, fine_state, *msgs, tile, halo, means],
        [(6, 8, rows, cols), (moved_s, LANES)],
        scratch_of(8, rows) + lift_scratch,
        light=True,
    )
    own = lax.ppermute(lifted, both, across)
    fine_out, done = call(
        upper_stress_kernel,
        [par, below, velocity, stress, fine_medium, *msgs, tile, halo],
        [(9,) + shape, (8, LANES)],
        scratch_of(8, rows),
        flops=200 * cells,
    )
    own, done, moving = lax.optimization_barrier((own, done, moving))
    other = lax.ppermute(own, "gy", partner)
    moving_other = lax.ppermute(moving, "gy", partner)

    shape = (thick, part, LANES)
    velocity, out_1, out_2, out_c = call(
        functools.partial(coarse_velocity_kernel, base_c=rows_msg, base_r=cols_msg),
        [par, coarse_state, coarse_medium, own, other, *begin, tile, halo, done],
        [(3,) + shape, (coarse_rows, LANES), (coarse_rows, LANES), (coarse_cols, LANES)],
        scratch_of(thick, part) + [(moved_s, LANES)],
    )
    msgs = exchange("gx", out_c, out_c) + exchange("gy", out_1, out_2)
    (coarse_out,) = call(
        coarse_stress_kernel,
        [par, coarse_state, coarse_medium, velocity, moving, moving_other, *msgs, tile, halo],
        [(9,) + shape],
        scratch_of(thick, part) + [(moved_v, LANES)],
    )
    return (fine_out, coarse_out)


def solution(mesh):
    placed = (
        P(None, None, "gx", "gy"),
        P(None, None, "gx", "gy"),
        P(None, None, "gy", "gx"),
        P(None, None, "gy", "gx"),
        P(None, None, "gy", "gx"),
        P("gx"),
        P("gy"),
    )
    return jax.shard_map(
        body,
        mesh=mesh,
        in_specs=placed,
        out_specs=(P(None, None, "gx", "gy"), P(None, None, "gy", "gx")),
        check_vma=False,
    )
```

```python
import functools

import jax
import jax.numpy as jnp
import ml_dtypes
import numpy as np
from jax import lax
from jax.experimental import pallas as pl
from jax.experimental.pallas import tpu as pltpu
from jax.sharding import PartitionSpec as P

COEFFS = (1225.0 / 1024.0, -245.0 / 3072.0, 49.0 / 5120.0, -5.0 / 7168.0)
STEP = 0.1
LANES = 128
F32 = jnp.float32
BF16 = jnp.bfloat16

VX, VY, VZ, SXX, SYY, SZZ, SXY, SXZ, SYZ = range(9)
CROSSING = (VX, VY, VZ, SXZ, SYZ, SZZ)
VEL_X = ((SXX, True), (SXY, False), (SXZ, False))
VEL_Y = ((SXY, False), (SYY, True), (SYZ, False))
VEL_Z = ((SXZ, False), (SYZ, False), (SZZ, True))
STR_X = ((VX, False), (VY, True), (VZ, True))
STR_Y = ((VX, True), (VY, False), (VZ, True))
STR_Z = ((VX, True), (VY, True), (VZ, False))


def above_planes(table):
    skip = table is VEL_Z
    return [(k, m) for k, (_, forward) in enumerate(table) for m in range(int(skip and forward), 4)]


def band(width, forward):
    matrix = np.zeros((width + 8, width), np.float64)
    for out in range(width):
        for tap, coeff in enumerate(COEFFS, 1):
            upper = out + tap if forward else out + tap - 1
            lower = out + 1 - tap if forward else out - tap
            matrix[4 + upper, out] += coeff
            matrix[4 + lower, out] -= coeff
    return matrix


def two_part(matrix):
    high = matrix.astype(ml_dtypes.bfloat16)
    low = (matrix - high.astype(np.float64)).astype(ml_dtypes.bfloat16)
    return np.block([[high, low], [high, np.zeros_like(low)]]).astype(ml_dtypes.bfloat16)


def lane_constants():
    tile = np.stack([two_part(band(LANES, f)[4:-4]) for f in (False, True)])
    halo = []
    for parity in range(2):
        for forward in (False, True):
            matrix = band(LANES, forward)
            after = np.zeros((8, LANES))
            before = np.zeros((8, LANES))
            after[:4] = matrix[-4:]
            before[4:] = matrix[:4]
            pair = (after, before) if parity == 0 else (before, after)
            halo.append(two_part(np.concatenate(pair)))
    halo = np.stack(halo).reshape(2, 2, 32, 2 * LANES)
    return tile, halo


def mean_constants():
    half = LANES // 2
    place = np.zeros((2, LANES, LANES), np.float32)
    for lane in range(LANES):
        for part in range(2):
            place[part, lane, part * half + lane // 2] = 1.0 / 16.0
    return np.concatenate([place, place], axis=1).astype(ml_dtypes.bfloat16)


def split(x):
    high = x.astype(BF16)
    return high, (x - high.astype(F32)).astype(BF16)


def fold(x):
    half = x.shape[1] // 2
    return x[:, :half] + x[:, half:]


def dot(a, b, dims=((1,), (0,))):
    return lax.dot_general(a, b, (dims, ((), ())), preferred_element_type=F32)


def dot_lanes(x, matrix):
    return fold(dot(jnp.concatenate(split(x), axis=1), matrix))


def dot_rows(x, matrix):
    return fold(dot(jnp.concatenate(split(x), axis=0), matrix, ((0,), (0,))))


def flat(x):
    return x.reshape(x.shape[0] * x.shape[1], x.shape[2])


def upper_half(shape):
    return lax.broadcasted_iota(jnp.int32, shape, 0) < 4


def put_rows(out_a, out_b, base, fields, parity):
    parts = []
    for ref, f in fields:
        rows = ref.shape[2]
        parts.append((ref.at[:, :, 0:8, :], ref.at[:, :, rows - 8 : rows, :], f))
    put_edge_rows(out_a, out_b, base, parts, parity)


def put_edge_rows(out_a, out_b, base, fields, parity):
    even = parity == 0
    top = upper_half((8, LANES))
    for k, (head, tail, f) in enumerate(fields):
        depth = head.shape[1]
        for z in range(0, depth, 2):
            first = jnp.where(top, head[f, z], pltpu.roll(head[f, z + 1], 4, 0))
            last = jnp.where(top, pltpu.roll(tail[f, z], 4, 0), tail[f, z + 1])
            at = pl.ds(base + 4 * (k * depth + z), 8)
            out_a[at, :] = jnp.where(even, last, first)
            out_b[at, :] = jnp.where(even, first, last)


def put_columns(outs, base, fields):
    row = lax.broadcasted_iota(jnp.int32, (8, 2 * LANES), 0)
    lane = lax.broadcasted_iota(jnp.int32, (8, 2 * LANES), 1) % LANES
    edges = (lane == jnp.where(row < 4, row, LANES - 8 + row)).astype(BF16)
    for k, (ref, f) in enumerate(fields):
        x = ref[...] if f is None else flat(ref[f])
        x = jnp.concatenate(split(x), axis=1)
        turned = dot(edges, x, ((1,), (1,)))
        blocks = turned.shape[1] // LANES
        for m in range(blocks):
            for out in outs:
                out[pl.ds(base + 8 * (k * blocks + m), 8), :] = turned[:, m * LANES : (m + 1) * LANES]


def fill_x(ext, fields, msg_a, msg_b, base, parity, low=0, count=None):
    even = parity == 0
    for k, (ref, f) in enumerate(fields):
        depth, rows = ref.shape[1], ref.shape[2]
        layers = depth if count is None else count
        ext[k, :, 8 : 8 + rows, :] = ref[f, low : low + layers]
        for z in range(0, layers, 2):
            at = pl.ds(base + 4 * (k * depth + low + z), 8)
            a, b = msg_a[at, :], msg_b[at, :]
            after, before = jnp.where(even, a, b), jnp.where(even, b, a)
            ext[k, z, 8 + rows : 16 + rows, :] = after
            ext[k, z + 1, 8 + rows : 16 + rows, :] = pltpu.roll(after, 4, 0)
            ext[k, z, 0:8, :] = pltpu.roll(before, 4, 0)
            ext[k, z + 1, 0:8, :] = before


def fill_y(out, fields, directions, msg_a, msg_b, base, parity, tile, halo, low=0, count=None):
    for k, (ref, f) in enumerate(fields):
        depth, rows = ref.shape[1], ref.shape[2]
        layers = depth if count is None else count
        forward = int(directions[k])
        inner = dot_lanes(flat(ref[f, low : low + layers]), tile[forward])
        factor = halo[parity, forward]
        start, blocks = low * rows // LANES, depth * rows // LANES
        for m in range(layers * rows // LANES):
            at = pl.ds(base + 8 * (k * blocks + start + m), 8)
            outer = dot_rows(jnp.concatenate([msg_a[at, :], msg_b[at, :]], axis=0), factor)
            out[k, m * LANES : (m + 1) * LANES, :] = inner[m * LANES : (m + 1) * LANES] + outer


def fill_z(ext, fields, top, bottom, low=0, count=None):
    for k, (ref, f) in enumerate(fields):
        depth = ref.shape[1]
        layers = depth if count is None else count
        first, last = max(low - 4, 0), min(low + layers + 4, depth)
        ext[k, first - low + 4 : last - low + 4] = ref[f, first:last]
        for g in range(first - (low - 4)):
            ext[k, g] = top(k, 4 - first + low - 4 + g)
        for g in range(low + layers + 4 - last):
            ext[k, last - low + 4 + g] = bottom(k, g)


def taps(read, forward):
    total = None
    for tap, coeff in enumerate(COEFFS, 1):
        upper = tap if forward else tap - 1
        lower = 1 - tap if forward else -tap
        term = coeff * (read(upper) - read(lower))
        total = term if total is None else total + term
    return total


def along_x(ext, k, z, rows, forward):
    return taps(lambda d: ext[k, z, 8 + d : 8 + d + rows, :], forward)


def along_z(ext, k, z, forward):
    return taps(lambda d: ext[k, z + 4 + d], forward)


def along_y(values, k, z, rows):
    return values[k, pl.ds(pl.multiple_of(z * rows, rows), rows), :]


def velocity_half(old, buoyancy, out, ex, ey, ez):
    depth, rows = out.shape[1], out.shape[2]

    def layer(z, _):
        scale = STEP * buoyancy[0, z]
        zx = along_z(ez, 0, z, False)
        zy = along_z(ez, 1, z, False)
        zz = along_z(ez, 2, z, True)
        x = along_x(ex, 0, z, rows, True)
        out[0, z] = old[0, z] + scale * (x + along_y(ey, 0, z, rows) + zx)
        x = along_x(ex, 1, z, rows, False)
        out[1, z] = old[1, z] + scale * (x + along_y(ey, 1, z, rows) + zy)
        x = along_x(ex, 2, z, rows, False)
        out[2, z] = old[2, z] + scale * (x + along_y(ey, 2, z, rows) + zz)
        return 0

    lax.fori_loop(0, depth, layer, 0, unroll=4 if rows > 16 else depth)


def stress_half(old, lame, shear, put, low, count, ex, ey, ez):
    rows = ex.shape[2] - 16

    def layer(n, _):
        z = n + low
        exx = along_x(ex, 0, n, rows, False)
        eyy = along_y(ey, 1, n, rows)
        ezz = along_z(ez, 2, n, False)
        mu = STEP * shear(z)
        common = (STEP * lame(z)) * (exx + eyy + ezz)
        double = mu + mu
        put(0, z, n, old(0, z) + (common + double * exx))
        put(1, z, n, old(1, z) + (common + double * eyy))
        put(2, z, n, old(2, z) + (common + double * ezz))
        x = along_x(ex, 1, n, rows, True)
        put(3, z, n, old(3, z) + mu * (along_y(ey, 0, n, rows) + x))
        x = along_x(ex, 2, n, rows, True)
        put(4, z, n, old(4, z) + mu * (along_z(ez, 0, n, True) + x))
        y = along_y(ey, 2, n, rows)
        put(5, z, n, old(5, z) + mu * (along_z(ez, 1, n, True) + y))
        return 0

    lax.fori_loop(0, count, layer, 0, unroll=4 if rows > 16 else count)


def zeros_like_plane(ref):
    return jnp.zeros(ref.shape[-2:], F32)


def after_before(msg_a, msg_b, at, parity):
    even = parity == 0
    a, b = msg_a[at, :], msg_b[at, :]
    return jnp.where(even, a, b), jnp.where(even, b, a)


def pack_kernel(
    par, fine, coarse, past, medium, out_a, out_b, out_1, out_2, planes, outer,
    turned, first, last, state, before, light, sems,
):
    pi, pj = par[0], par[1]
    depth, rows = fine.shape[1], fine.shape[2]
    part = coarse.shape[2]
    copies = [
        pltpu.make_async_copy(coarse, state, sems.at[0]),
        pltpu.make_async_copy(past, before, sems.at[1]),
        pltpu.make_async_copy(medium.at[0:1, depth - 4 :], light, sems.at[2]),
    ]
    for k, (f, _) in enumerate(VEL_X):
        head, tail = fine.at[f, :, 0:8, :], fine.at[f, :, rows - 8 : rows, :]
        copies.append(pltpu.make_async_copy(head, first.at[k], sems.at[3 + 2 * k]))
        copies.append(pltpu.make_async_copy(tail, last.at[k], sems.at[4 + 2 * k]))
    for k, (f, _) in enumerate(VEL_Y):
        copies.append(pltpu.make_async_copy(fine.at[f], turned.at[k], sems.at[9 + k]))
    for copy in copies:
        copy.start()
    for copy in copies[:3]:
        copy.wait()
    upper = pj == 0
    for n, f in enumerate(CROSSING):
        for layer in range(2):
            now = state[f, layer]
            later = 1.5 * now - 0.5 * before[f, layer]
            for p, plane in ((2 * n + layer, now), (12 + 2 * n + layer, later)):
                planes[pl.ds(p * part, part), :] = plane
                outer[p : p + 1, :] = jnp.where(upper, plane[:1], plane[part - 1 :])
    base = 12 * depth
    put_columns((out_a, out_b), base, [(state, f) for f, _ in VEL_Y])
    put_rows(out_a, out_b, base + 24, [(light, 0)], pi)
    put_columns((out_a, out_b), base + 40, [(planes, None)])
    base = 24 * (depth * rows // LANES)
    put_rows(out_1, out_2, base, [(state, f) for f, _ in VEL_X], pj)
    base += 12 * coarse.shape[1]
    put_columns((out_1, out_2), base, [(light, 0)])
    out_1[base + 16 : base + 40, :] = outer[...]
    out_2[base + 16 : base + 40, :] = outer[...]
    for copy in copies[3:9]:
        copy.wait()
    put_edge_rows(out_a, out_b, 0, [(first, last, k) for k in range(3)], pi)
    for k in range(3):
        copies[9 + k].wait()
        base = 8 * k * (depth * rows // LANES)
        put_columns((out_1, out_2), base, [(turned, k)])


def crossing_kernel(par, planes, msg_a, msg_b, msg_2, first, second):
    count = planes.shape[0]
    blocks = count // LANES
    even = par[0] == 0
    base = msg_a.shape[0] - 8 * blocks
    left, right = [], []
    for m in range(blocks):
        a = msg_a[pl.ds(base + 8 * m, 8), :]
        b = msg_b[pl.ds(base + 8 * m, 8), :]
        left.append(jnp.where(even, b, a)[7:8])
        right.append(jnp.where(even, a, b)[0:1])
    fill = [jnp.zeros((8 - blocks, LANES), F32)]
    left, right = (jnp.concatenate(side + fill, axis=0) for side in (left, right))
    half = count // 2
    first[0:half, :] = planes[:half, :]
    first[half : half + 24, :] = msg_2[msg_2.shape[0] - 24 :, :]
    first[half + 24 : half + 32, :] = left
    first[half + 32 : half + 40, :] = right
    second[...] = planes[half:, :]


def expand_ghosts(
    par, own, other, prow, pcol, ghost, level, planes, ends=None, known=None
):
    core = par[1]
    row_base, col_base = par[2], par[3]
    part = (own.shape[0] - 40) // 12
    rows = prow.shape[1]
    low = core == 0
    count = 12 * part
    source = lax.broadcasted_iota(jnp.int32, (LANES, LANES), 0)
    pick_cols = (source == pcol[...] - col_base).astype(BF16)
    pick_cols = jnp.concatenate([pick_cols, pick_cols], axis=0)
    source = lax.broadcasted_iota(jnp.int32, (2 * part, rows), 0)
    pick_rows = (source == prow[...] - row_base).astype(BF16)
    pick_rows = jnp.concatenate([pick_rows, pick_rows], axis=0)

    def spread(x):
        return dot(jnp.concatenate(split(x), axis=1), pick_cols)

    mine, theirs = (
        spread(jnp.concatenate([main[0:count, :], ref[count : count + 24, :]], axis=0))
        for main, ref in zip(planes, (own, other))
    )
    first, second = jnp.where(low, mine, theirs), jnp.where(low, theirs, mine)
    above, below = first[count:], second[count:]
    beside = []
    for ref in (own, other):
        side = jnp.where(low, ref[count + 24 : count + 32, :], ref[count + 32 : count + 40, :])
        side = jnp.concatenate([side, jnp.zeros((LANES - 8, LANES), F32)], axis=0)
        beside.append(side.T)
    side_1 = jnp.where(low, beside[0], beside[1])
    side_2 = jnp.where(low, beside[1], beside[0])
    lane = lax.broadcasted_iota(jnp.int32, (rows, LANES), 1)
    row = lax.broadcasted_iota(jnp.int32, (rows, LANES), 0)
    edge = lane == jnp.where(low, 0, LANES - 1)
    edge_row = edge[:1]
    if ends is not None:
        above = above + jnp.where(edge_row, ends[0], 0.0)
        below = below + jnp.where(edge_row, ends[1], 0.0)
    group = LANES // part
    if known is not None:
        own_row, other_row = own[count : count + 24, :], other[count : count + 24, :]
        for base, x in (
            (48, jnp.where(low, own_row, other_row)), (72, jnp.where(low, other_row, own_row))
        ):
            x = jnp.where(low, x[:, :1], x[:, LANES - 1 :])
            known[base : base + 24, :] = jnp.broadcast_to(x, (24, LANES))
        for p in range(24):
            q, t = p % group, p // group
            last = side_2[(q + 1) * part - 1 : (q + 1) * part, t : t + 1]
            first_row = side_1[q * part : q * part + 1, t : t + 1]
            known[p : p + 1, :] = jnp.broadcast_to(last, (1, LANES))
            known[24 + p : 25 + p, :] = jnp.broadcast_to(first_row, (1, LANES))
    columns = []
    for q in range(group):
        at = slice(q * part, (q + 1) * part)
        column = jnp.concatenate([side_1[at], side_2[at]], axis=0)
        columns.append(dot(pick_rows, jnp.concatenate(split(column), axis=0), ((0,), (0,))))
    for n in range(12):
        p = 12 * level + n
        at = slice(n * part, (n + 1) * part)
        plane = jnp.concatenate([first[at], second[at]], axis=0)
        full = dot(pick_rows, jnp.concatenate(split(plane), axis=0), ((0,), (0,)))
        column = columns[p % group][:, p // group : p // group + 1]
        full = full + jnp.where(edge, column, 0.0)
        full = full + jnp.where(row == 0, above[p : p + 1], 0.0)
        ghost[n] = full + jnp.where(row == rows - 1, below[p : p + 1], 0.0)


def ends_of(par, msg_a, msg_b):
    base = msg_a.shape[0] - 24
    below, above = after_before(msg_a, msg_b, slice(base, base + 24), par[0])
    return above, below


def later_ghost_kernel(
    par, own, other, prow, pcol, later_own, later_other, msg_a, msg_b, ghost
):
    planes = later_own, later_other
    ends = ends_of(par, msg_a, msg_b)
    expand_ghosts(par, own, other, prow, pcol, ghost, 1, planes, ends=ends)


def ghost_rate(planes, z, depth, forward):
    total = None
    for tap, coeff in enumerate(COEFFS, 1):
        g = z + (tap if forward else tap - 1) - depth
        if g >= 0:
            term = coeff * planes[g // 2]
            total = term if total is None else total + term
    return total


def ghost_kernel(
    par, half, buoyancy, own, other, prow, pcol,
    out, ghost, known, out_a, out_b, out_1, out_2,
):
    planes = own, other
    expand_ghosts(par, own, other, prow, pcol, ghost, 0, planes, known=known)
    depth = half.shape[1]
    for c, (f, forward) in enumerate(VEL_Z):
        out[c, 0 : depth - 4] = half[c, 0 : depth - 4]
        n = CROSSING.index(f)
        planes = [ghost[2 * n], ghost[2 * n + 1]]
        for z in range(depth - 4, depth):
            value = half[c, z]
            rate = ghost_rate(planes, z, depth, forward)
            if rate is not None:
                value = value + (STEP * buoyancy[0, z]) * rate
            out[c, z] = value
    moved = [(out, c) for c in range(3)]
    put_rows(out_a, out_b, 0, moved, par[0])
    put_columns((out_1, out_2), 0, moved)
    even = par[0] == 0
    up, down = known[0:24, :], known[24:48, :]
    base = 12 * depth
    out_a[base:, :] = jnp.where(even, up, down)
    out_b[base:, :] = jnp.where(even, down, up)


def add_corners(
    par, half, buoyancy, half_ghost, known, begin_a, begin_b, begin_2, msg_a, msg_b, msg_2,
    velocity, ghost, rows_a, rows_b, cols_2, base_x, base_y,
):
    pi, low = par[0], par[1] == 0
    depth, rows = half.shape[1], half.shape[2]
    lane = lax.broadcasted_iota(jnp.int32, (rows, LANES), 1)
    row = lax.broadcasted_iota(jnp.int32, (rows, LANES), 0)
    edge = lane == jnp.where(low, 0, LANES - 1)
    first, last = edge & (row == 0), edge & (row == rows - 1)
    above, below = ends_of(par, msg_a, msg_b)
    for n in range(12):
        plane = half_ghost[n] + jnp.where(first, above[n : n + 1], 0.0)
        ghost[n] = plane + jnp.where(last, below[n : n + 1], 0.0)
    for source, target in ((msg_a, rows_a), (msg_b, rows_b), (msg_2, cols_2)):
        target[...] = source[...]
    even = pi == 0
    near = lax.broadcasted_iota(jnp.int32, (8, LANES), 0)
    lane = lax.broadcasted_iota(jnp.int32, (8, LANES), 1)
    edge = lane == jnp.where(low, 0, LANES - 1)
    beside = near == jnp.where(low, 7, 0)
    blocks = depth * rows // LANES
    none = jnp.zeros((1, LANES), F32)

    def rates(x, n, z, forward):
        found = []
        for odd in range(2):
            rate = ghost_rate([x[2 * n : 2 * n + 1], x[2 * n + 1 : 2 * n + 2]], z + odd, depth, forward)
            found.append(none if rate is None else rate)
        return found

    up, down = known[0:12, :], known[24:36, :]
    row_above, row_below = known[48:60, :], known[72:84, :]
    for c, (f, forward) in enumerate(VEL_Z):
        n = CROSSING.index(f)
        velocity[c, 0 : depth - 4] = half[c, 0 : depth - 4]
        for pair in range(2):
            z = depth - 4 + 2 * pair
            tops, bottoms = rates(above, n, z, forward), rates(below, n, z, forward)
            for odd in range(2):
                change = jnp.where(first, tops[odd], 0.0) + jnp.where(last, bottoms[odd], 0.0)
                scale = STEP * buoyancy[0, z + odd]
                velocity[c, z + odd] = half[c, z + odd] + scale * change
            after, before = after_before(
                begin_a, begin_b, slice(base_x + 8 * pair, base_x + 8 * pair + 8), pi
            )
            rate = rates(up, n, z, forward)
            change = jnp.where(near == 0, rate[0], jnp.where(near == 4, rate[1], 0.0))
            after = jnp.where(edge, (STEP * after) * change, 0.0)
            rate = rates(down, n, z, forward)
            change = jnp.where(near == 3, rate[0], jnp.where(near == 7, rate[1], 0.0))
            before = jnp.where(edge, (STEP * before) * change, 0.0)
            at = pl.ds(4 * (c * depth + z), 8)
            rows_a[at, :] = rows_a[at, :] + jnp.where(even, after, before)
            rows_b[at, :] = rows_b[at, :] + jnp.where(even, before, after)
            tops, bottoms = rates(row_above, n, z, forward), rates(row_below, n, z, forward)
            change = jnp.where(lane == 0, tops[0], jnp.where(lane == rows - 1, bottoms[0], 0.0))
            change = jnp.where(lane == rows, tops[1], change)
            change = jnp.where(lane == 2 * rows - 1, bottoms[1], change)
            light = begin_2[base_y + 8 * pair : base_y + 8 * pair + 8, :]
            at = pl.ds(8 * (c * blocks + blocks - 2 + pair), 8)
            cols_2[at, :] = cols_2[at, :] + jnp.where(beside, (STEP * light) * change, 0.0)


def stress_fields(ref, table):
    offset = 9 - ref.shape[0]
    return [(ref, f - offset) for f, _ in table]


def velocity_fill(par, stress, msg_a, msg_b, msg_1, msg_2, tile, halo, bottom, ex, ey, ez):
    pi, pj = par[0], par[1]
    none = zeros_like_plane(stress)
    fill_z(ez, stress_fields(stress, VEL_Z), lambda k, g: none, bottom)
    fill_x(ex, stress_fields(stress, VEL_X), msg_a, msg_b, 0, pi)
    fill_y(
        ey, stress_fields(stress, VEL_Y), [d for _, d in VEL_Y], msg_1, msg_2, 0, pj, tile, halo
    )


def first_velocity_kernel(
    par, state, buoyancy, msg_a, msg_b, msg_1, msg_2, tile, halo, out, ex, ey, ez
):
    none = zeros_like_plane(state)
    velocity_fill(
        par, state, msg_a, msg_b, msg_1, msg_2, tile, halo, lambda k, g: none, ex, ey, ez
    )
    velocity_half(state, buoyancy, out, ex, ey, ez)


def velocity_kernel(
    par, old, stress, buoyancy, ghost, start, msg_a, msg_b, msg_1, msg_2, tile, halo, means,
    out, out_a, out_b, out_1, out_2, coarse, ex, ey, ez, summed, halves,
):
    order = [CROSSING.index(f) for f, _ in VEL_Z]
    velocity_fill(
        par, stress, msg_a, msg_b, msg_1, msg_2, tile, halo,
        lambda k, g: ghost[2 * order[k] + g // 2], ex, ey, ez,
    )
    velocity_half(old, buoyancy, out, ex, ey, ez)
    moved = [(out, c) for c in range(3)]
    put_rows(out_a, out_b, 0, moved, par[0])
    put_columns((out_1, out_2), 0, moved)
    low = out.shape[1] - 8
    lift(start, STR_Z, [out.at[c, low:] for c in range(3)], means, coarse, summed, halves)


def stress_fill(
    par, velocity, bottom, msg_a, msg_b, msg_1, msg_2, tile, halo, ex, ey, ez, low, count
):
    pi, pj = par[0], par[1]
    none = zeros_like_plane(velocity)
    fields = [(velocity, c) for c in range(3)]
    fill_z(ez, fields, lambda k, g: none, bottom, low, count)
    fill_x(ex, fields, msg_a, msg_b, 0, pi, low, count)
    fill_y(
        ey, fields, [d for _, d in STR_Y], msg_1, msg_2, 0, pj, tile, halo, low, count
    )


def stress_kernel(
    par, half, state, medium, half_ghost, known, begin_a, begin_b, begin_2, msg_a, msg_b, msg_1,
    msg_2, tile, halo, out, velocity, out_a, out_b, out_1, out_2, ex, ey, ez, ghost, rows_a, rows_b,
    cols_2, *, base_x, base_y,
):
    depth = half.shape[1]
    add_corners(
        par, half, medium, half_ghost, known, begin_a, begin_b, begin_2, msg_a, msg_b, msg_2,
        velocity, ghost, rows_a, rows_b, cols_2, base_x, base_y,
    )
    stress_fill(
        par, velocity, lambda k, g: ghost[2 * k + g // 2], rows_a, rows_b, msg_1, cols_2,
        tile, halo, ex, ey, ez, 0, depth,
    )

    def put(c, z, n, value):
        out[c, z] = value

    stress_half(
        lambda c, z: state[SXX + c, z], lambda z: medium[1, z], lambda z: medium[2, z],
        put, 0, depth, ex, ey, ez,
    )
    put_rows(out_a, out_b, 0, stress_fields(out, VEL_X), par[0])
    put_columns((out_1, out_2), 0, stress_fields(out, VEL_Y))


def lift(start, table, fields, means, coarse, summed, halves):
    rows = summed.shape[0]
    part = rows // 4
    low = start.shape[1] - 8
    for n, (k, m) in enumerate(above_planes(table)):
        f, new = table[k][0], fields[k]
        z = 2 * m
        total = (start[f, low + z] + start[f, low + z + 1]) + (new[z] + new[z + 1])
        summed[...] = total
        pairs = summed[pl.ds(0, 2 * part, stride=2), :] + summed[pl.ds(1, 2 * part, stride=2), :]
        at = pl.ds(n * part, part)
        halves[0, at, :] = pairs[:part]
        halves[1, at, :] = pairs[part:]
    count = coarse.shape[0]
    upper = dot(jnp.concatenate(split(halves[0, 0:count]), axis=1), means[0])
    lower = dot(jnp.concatenate(split(halves[1, 0:count]), axis=1), means[1])
    coarse[...] = upper + lower


def lower_stress_kernel(
    par, velocity, stress, medium, ghost, start, msg_a, msg_b, msg_1, msg_2, tile, halo, means,
    out, coarse, ex, ey, ez, summed, halves,
):
    depth, rows = velocity.shape[1], velocity.shape[2]
    low = depth - 8
    stress_fill(
        par, velocity, lambda k, g: ghost[2 * k + g // 2], msg_a, msg_b, msg_1, msg_2,
        tile, halo, ex, ey, ez, low, 8,
    )

    def put(c, z, n, value):
        out[c, n] = value

    stress_half(
        lambda c, z: stress[c, z], lambda z: medium[1, z], lambda z: medium[2, z],
        put, low, 8, ex, ey, ez,
    )
    fields = [out.at[f - SXX] for f, _ in VEL_Z]
    lift(start, VEL_Z, fields, means, coarse, summed, halves)


def upper_stress_kernel(
    par, below, velocity, stress, medium, msg_a, msg_b, msg_1, msg_2, tile, halo,
    out, done, ex, ey, ez,
):
    stress_fill(
        par, velocity, None, msg_a, msg_b, msg_1, msg_2, tile, halo, ex, ey, ez, 0, 8
    )
    out[0:3] = velocity[...]
    out[SXX:, velocity.shape[1] - 8 :] = below[...]

    def put(c, z, n, value):
        out[SXX + c, n] = value

    stress_half(
        lambda c, z: stress[c, z], lambda z: medium[1, z], lambda z: medium[2, z],
        put, 0, 8, ex, ey, ez,
    )
    done[...] = jnp.zeros_like(done)


def join(par, own, other, ghost, table, rows):
    half = LANES // 2
    even = par[1] == 0
    left = jnp.where(even, own[...], other[...])
    right = jnp.where(even, other[...], own[...])
    low = lax.broadcasted_iota(jnp.int32, left.shape, 1) < half
    ghost[...] = jnp.where(
        even,
        jnp.where(low, left, pltpu.roll(right, half, 1)),
        jnp.where(low, pltpu.roll(left, half, 1), right),
    )
    planes = above_planes(table)
    none = jnp.zeros((rows, LANES), F32)

    def layer(k, m):
        if (k, m) not in planes:
            return none
        return ghost[pl.ds(planes.index((k, m)) * rows, rows), :]

    return layer


def coarse_velocity_kernel(
    par, state, medium, own, other, msg_a, msg_b, msg_1, msg_2, tile, halo, done,
    out, out_1, out_2, out_c, ex, ey, ez, ghost, *, base_c, base_r,
):
    pi, pj = par[0], par[1]
    rows = state.shape[2]
    above = join(par, own, other, ghost, VEL_Z, state.shape[2])
    none = zeros_like_plane(state)
    fill_z(
        ez, stress_fields(state, VEL_Z),
        above, lambda k, g: none,
    )
    fill_x(ex, stress_fields(state, VEL_X), msg_1, msg_2, base_r, pj)
    fill_y(
        ey, stress_fields(state, VEL_Y), [d for _, d in VEL_Y], msg_a, msg_b, base_c, pi,
        tile, halo,
    )
    velocity_half(state, medium, out, ex, ey, ez)
    moved = [(out, c) for c in range(3)]
    put_rows(out_1, out_2, 0, moved, pj)
    put_columns((out_c,), 0, moved)


def coarse_stress_kernel(
    par, state, medium, velocity, own, other, msg_a, msg_b, msg_1, msg_2, tile, halo,
    out, ex, ey, ez, ghost,
):
    pi, pj = par[0], par[1]
    above = join(par, own, other, ghost, STR_Z, state.shape[2])
    depth, rows = state.shape[1], state.shape[2]
    none = zeros_like_plane(state)
    fields = [(velocity, c) for c in range(3)]
    fill_z(
        ez, fields, above, lambda k, g: none
    )
    fill_x(ex, fields, msg_1, msg_2, 0, pj)
    fill_y(ey, fields, [d for _, d in STR_Y], msg_a, msg_b, 0, pi, tile, halo)
    out[0:3] = velocity[...]

    def put(c, z, n, value):
        out[SXX + c, z] = value

    stress_half(
        lambda c, z: state[SXX + c, z], lambda z: medium[1, z], lambda z: medium[2, z],
        put, 0, depth, ex, ey, ez,
    )


def whole(shape):
    return pl.BlockSpec(shape, functools.partial(lambda rank, _: (0,) * rank, len(shape)))


def call(kernel, args, outs, scratch=(), flops=0, copied=0, light=False):
    specs = [pl.BlockSpec(memory_space=pltpu.SMEM)]
    for n, a in enumerate(args[1:]):
        specs.append(pl.BlockSpec(memory_space=pltpu.HBM) if n < copied else whole(a.shape))
    size = 1024 if light else sum(4 * int(np.prod(a.shape)) for a in args) + sum(4 * int(np.prod(o)) for o in outs)
    return pl.pallas_call(
        kernel,
        grid=(1,),
        in_specs=specs,
        out_specs=[whole(o) for o in outs],
        out_shape=[jax.ShapeDtypeStruct(o, F32) for o in outs],
        scratch_shapes=[pltpu.VMEM(s, F32) for s in scratch]
        + ([pltpu.SemaphoreType.DMA((12,))] if copied else []),
        compiler_params=pltpu.CompilerParams(vmem_limit_bytes=(54 if copied else 24) * 1024 * 1024),
        cost_estimate=pl.CostEstimate(flops=flops, bytes_accessed=size, transcendentals=0),
    )(*args)


def matchings(axis):
    size = lax.axis_size(axis)
    result = []
    for start in range(2):
        pairs = []
        for low in range(start, size - 1, 2):
            pairs += [(low, low + 1), (low + 1, low)]
        result.append(pairs)
    return result


def exchange(axis, first, second):
    one, two = matchings(axis)
    return lax.ppermute(first, axis, one), lax.ppermute(second, axis, two)


def body(
    fine_state, fine_medium, coarse_state, coarse_medium, coarse_past, parent_rows, parent_cols
):
    size_x, size_y = lax.axis_size("gx"), lax.axis_size("gy")
    i, j = lax.axis_index("gx"), lax.axis_index("gy")
    depth, rows, cols = fine_state.shape[1:]
    thick, part = coarse_state.shape[1:3]
    blocks = depth * rows // LANES
    par = jnp.stack([i % 2, j % 2, i * (rows // 2), (j // 2) * LANES]).astype(jnp.int32)
    tile, halo = (jnp.asarray(c) for c in lane_constants())
    means = jnp.asarray(mean_constants())
    across = [
        (p * size_y + q, (q // 2) * size_y + 2 * p + q % 2)
        for p in range(size_x)
        for q in range(size_y)
    ]
    partner = matchings("gy")[0]

    both = ("gx", "gy")

    rows_msg, cols_msg = 12 * depth, 24 * blocks
    coarse_cols, coarse_rows = 24, 12 * thick
    count = 24 * part
    out_a, out_b, out_1, out_2, planes, outer = call(
        pack_kernel,
        [par, fine_state, coarse_state, coarse_past, fine_medium],
        [(rows_msg + coarse_cols + 16 + count * 8 // LANES, LANES)] * 2
        + [(cols_msg + coarse_rows + 40, LANES)] * 2
        + [(count, LANES), (24, LANES)],
        [(3,) + fine_state.shape[1:], (3, depth, 8, cols), (3, depth, 8, cols),
         coarse_state.shape, coarse_past.shape, (1, 4, rows, cols)],
        copied=4,
    )
    msg_a, msg_b = exchange("gx", out_a, out_b)
    msg_1, msg_2 = exchange("gy", out_1, out_2)
    begin = msg_a, msg_b, msg_1, msg_2
    crossing, later = call(
        crossing_kernel,
        [par, planes, msg_a, msg_b, msg_2],
        [(count // 2 + 40, LANES), (count // 2, LANES)],
    )
    own = lax.ppermute(crossing, both, across)

    shape = (depth, rows, cols)

    def scratch_of(depth, rows):
        return [
            (3, depth, rows + 16, LANES), (3, depth * rows, LANES), (3, depth + 8, rows, LANES),
        ]

    cells = depth * rows * cols
    halves = [(rows_msg + 8, LANES)] * 2 + [(cols_msg + 24, LANES), (cols_msg + 16, LANES)]
    (half,) = call(
        first_velocity_kernel,
        [par, fine_state, fine_medium, msg_a, msg_b, msg_1, msg_2, tile, halo],
        [(3,) + shape],
        scratch_of(depth, rows),
        flops=400 * cells,
    )
    own, half = lax.optimization_barrier((own, half))
    other = lax.ppermute(own, "gy", partner)
    parents = parent_rows.reshape(1, rows), parent_cols.reshape(1, cols)
    half, half_ghost, known, out_a, out_b, out_1, out_2 = call(
        ghost_kernel,
        [par, half, fine_medium, own, other, *parents],
        [(3,) + shape, (12, rows, cols), (96, LANES)] + [(rows_msg + 24, LANES)] * 2
        + [(cols_msg + 40, LANES), (cols_msg + 32, LANES)],
    )
    msgs = exchange("gx", out_a, out_b) + exchange("gy", out_1, out_2)
    later, half = lax.optimization_barrier((later, half))
    later = lax.ppermute(later, both, across)
    ends = msgs[:2]
    stress, velocity, out_a, out_b, out_1, out_2 = call(
        functools.partial(
            stress_kernel, base_x=rows_msg + coarse_cols, base_y=cols_msg + coarse_rows
        ),
        [par, half, fine_state, fine_medium, half_ghost, known, begin[0], begin[1], begin[3],
         *msgs, tile, halo],
        [(6,) + shape, (3,) + shape] + halves,
        scratch_of(depth, rows)
        + [(12, rows, cols)] + [(rows_msg + 24, LANES)] * 2 + [(cols_msg + 32, LANES)],
        flops=400 * cells,
    )
    msgs = exchange("gx", out_a, out_b) + exchange("gy", out_1, out_2)
    later, stress = lax.optimization_barrier((later, stress))
    later_other = lax.ppermute(later, "gy", partner)
    (ghost,) = call(
        later_ghost_kernel,
        [par, own, other, *parents, later, later_other, *ends],
        [(12, rows, cols)],
    )
    moved_v, moved_s = (len(above_planes(t)) * part for t in (STR_Z, VEL_Z))
    lift_scratch = [(rows, cols), (2, count // 2, LANES)]
    velocity, out_a, out_b, out_1, out_2, lifted = call(
        velocity_kernel,
        [par, velocity, stress, fine_medium, ghost, fine_state, *msgs, tile, halo, means],
        [(3,) + shape] + halves + [(moved_v, LANES)],
        scratch_of(depth, rows) + lift_scratch,
        flops=400 * cells,
    )
    msgs = exchange("gx", out_a, out_b) + exchange("gy", out_1, out_2)
    moving = lax.ppermute(lifted, both, across)
    below, lifted = call(
        lower_stress_kernel,
        [par, velocity, stress, fine_medium, ghost, fine_state, *msgs, tile, halo, means],
        [(6, 8, rows, cols), (moved_s, LANES)],
        scratch_of(8, rows) + lift_scratch,
        light=True,
    )
    own = lax.ppermute(lifted, both, across)
    fine_out, done = call(
        upper_stress_kernel,
        [par, below, velocity, stress, fine_medium, *msgs, tile, halo],
        [(9,) + shape, (8, LANES)],
        scratch_of(8, rows),
        flops=200 * cells,
    )
    own, done, moving = lax.optimization_barrier((own, done, moving))
    other = lax.ppermute(own, "gy", partner)
    moving_other = lax.ppermute(moving, "gy", partner)

    shape = (thick, part, LANES)
    velocity, out_1, out_2, out_c = call(
        functools.partial(coarse_velocity_kernel, base_c=rows_msg, base_r=cols_msg),
        [par, coarse_state, coarse_medium, own, other, *begin, tile, halo, done],
        [(3,) + shape, (coarse_rows, LANES), (coarse_rows, LANES), (coarse_cols, LANES)],
        scratch_of(thick, part) + [(moved_s, LANES)],
    )
    msgs = exchange("gx", out_c, out_c) + exchange("gy", out_1, out_2)
    (coarse_out,) = call(
        coarse_stress_kernel,
        [par, coarse_state, coarse_medium, velocity, moving, moving_other, *msgs, tile, halo],
        [(9,) + shape],
        scratch_of(thick, part) + [(moved_v, LANES)],
    )
    return (fine_out, coarse_out)


def solution(mesh):
    placed = (
        P(None, None, "gx", "gy"),
        P(None, None, "gx", "gy"),
        P(None, None, "gy", "gx"),
        P(None, None, "gy", "gx"),
        P(None, None, "gy", "gx"),
        P("gx"),
        P("gy"),
    )
    return jax.shard_map(
        body,
        mesh=mesh,
        in_specs=placed,
        out_specs=(P(None, None, "gx", "gy"), P(None, None, "gy", "gx")),
        check_vma=False,
    )
```

```python
import functools

import jax
import jax.numpy as jnp
import ml_dtypes
import numpy as np
from jax import lax
from jax.experimental import pallas as pl
from jax.experimental.pallas import tpu as pltpu
from jax.sharding import PartitionSpec as P

COEFFS = (1225.0 / 1024.0, -245.0 / 3072.0, 49.0 / 5120.0, -5.0 / 7168.0)
STEP = 0.1
LANES = 128
F32 = jnp.float32
BF16 = jnp.bfloat16

VX, VY, VZ, SXX, SYY, SZZ, SXY, SXZ, SYZ = range(9)
CROSSING = (VX, VY, VZ, SXZ, SYZ, SZZ)
VEL_X = ((SXX, True), (SXY, False), (SXZ, False))
VEL_Y = ((SXY, False), (SYY, True), (SYZ, False))
VEL_Z = ((SXZ, False), (SYZ, False), (SZZ, True))
STR_X = ((VX, False), (VY, True), (VZ, True))
STR_Y = ((VX, True), (VY, False), (VZ, True))
STR_Z = ((VX, True), (VY, True), (VZ, False))


def above_planes(table):
    skip = table is VEL_Z
    return [(k, m) for k, (_, forward) in enumerate(table) for m in range(int(skip and forward), 4)]


def band(width, forward):
    matrix = np.zeros((width + 8, width), np.float64)
    for out in range(width):
        for tap, coeff in enumerate(COEFFS, 1):
            upper = out + tap if forward else out + tap - 1
            lower = out + 1 - tap if forward else out - tap
            matrix[4 + upper, out] += coeff
            matrix[4 + lower, out] -= coeff
    return matrix


def two_part(matrix):
    high = matrix.astype(ml_dtypes.bfloat16)
    low = (matrix - high.astype(np.float64)).astype(ml_dtypes.bfloat16)
    return np.block([[high, low], [high, np.zeros_like(low)]]).astype(ml_dtypes.bfloat16)


def lane_constants():
    tile = np.stack([two_part(band(LANES, f)[4:-4]) for f in (False, True)])
    halo = []
    for parity in range(2):
        for forward in (False, True):
            matrix = band(LANES, forward)
            after = np.zeros((8, LANES))
            before = np.zeros((8, LANES))
            after[:4] = matrix[-4:]
            before[4:] = matrix[:4]
            pair = (after, before) if parity == 0 else (before, after)
            halo.append(two_part(np.concatenate(pair)))
    halo = np.stack(halo).reshape(2, 2, 32, 2 * LANES)
    return tile, halo


def mean_constants():
    half = LANES // 2
    place = np.zeros((2, LANES, LANES), np.float32)
    for lane in range(LANES):
        for part in range(2):
            place[part, lane, part * half + lane // 2] = 1.0 / 16.0
    return np.concatenate([place, place], axis=1).astype(ml_dtypes.bfloat16)


def split(x):
    high = x.astype(BF16)
    return high, (x - high.astype(F32)).astype(BF16)


def fold(x):
    half = x.shape[1] // 2
    return x[:, :half] + x[:, half:]


def dot(a, b, dims=((1,), (0,))):
    return lax.dot_general(a, b, (dims, ((), ())), preferred_element_type=F32)


def dot_lanes(x, matrix):
    return fold(dot(jnp.concatenate(split(x), axis=1), matrix))


def dot_rows(x, matrix):
    return fold(dot(jnp.concatenate(split(x), axis=0), matrix, ((0,), (0,))))


def flat(x):
    return x.reshape(x.shape[0] * x.shape[1], x.shape[2])


def upper_half(shape):
    return lax.broadcasted_iota(jnp.int32, shape, 0) < 4


def put_rows(out_a, out_b, base, fields, parity):
    parts = []
    for ref, f in fields:
        rows = ref.shape[2]
        parts.append((ref.at[:, :, 0:8, :], ref.at[:, :, rows - 8 : rows, :], f))
    put_edge_rows(out_a, out_b, base, parts, parity)


def put_edge_rows(out_a, out_b, base, fields, parity):
    even = parity == 0
    top = upper_half((8, LANES))
    for k, (head, tail, f) in enumerate(fields):
        depth = head.shape[1]
        for z in range(0, depth, 2):
            first = jnp.where(top, head[f, z], pltpu.roll(head[f, z + 1], 4, 0))
            last = jnp.where(top, pltpu.roll(tail[f, z], 4, 0), tail[f, z + 1])
            at = pl.ds(base + 4 * (k * depth + z), 8)
            out_a[at, :] = jnp.where(even, last, first)
            out_b[at, :] = jnp.where(even, first, last)


def put_columns(outs, base, fields):
    row = lax.broadcasted_iota(jnp.int32, (8, 2 * LANES), 0)
    lane = lax.broadcasted_iota(jnp.int32, (8, 2 * LANES), 1) % LANES
    edges = (lane == jnp.where(row < 4, row, LANES - 8 + row)).astype(BF16)
    for k, (ref, f) in enumerate(fields):
        x = ref[...] if f is None else flat(ref[f])
        x = jnp.concatenate(split(x), axis=1)
        turned = dot(edges, x, ((1,), (1,)))
        blocks = turned.shape[1] // LANES
        for m in range(blocks):
            for out in outs:
                out[pl.ds(base + 8 * (k * blocks + m), 8), :] = turned[:, m * LANES : (m + 1) * LANES]


def fill_x(ext, fields, msg_a, msg_b, base, parity, low=0, count=None):
    even = parity == 0
    for k, (ref, f) in enumerate(fields):
        depth, rows = ref.shape[1], ref.shape[2]
        layers = depth if count is None else count
        ext[k, :, 8 : 8 + rows, :] = ref[f, low : low + layers]
        for z in range(0, layers, 2):
            at = pl.ds(base + 4 * (k * depth + low + z), 8)
            a, b = msg_a[at, :], msg_b[at, :]
            after, before = jnp.where(even, a, b), jnp.where(even, b, a)
            ext[k, z, 8 + rows : 16 + rows, :] = after
            ext[k, z + 1, 8 + rows : 16 + rows, :] = pltpu.roll(after, 4, 0)
            ext[k, z, 0:8, :] = pltpu.roll(before, 4, 0)
            ext[k, z + 1, 0:8, :] = before


def fill_y(out, fields, directions, msg_a, msg_b, base, parity, tile, halo, low=0, count=None):
    for k, (ref, f) in enumerate(fields):
        depth, rows = ref.shape[1], ref.shape[2]
        layers = depth if count is None else count
        forward = int(directions[k])
        inner = dot_lanes(flat(ref[f, low : low + layers]), tile[forward])
        factor = halo[parity, forward]
        start, blocks = low * rows // LANES, depth * rows // LANES
        for m in range(layers * rows // LANES):
            at = pl.ds(base + 8 * (k * blocks + start + m), 8)
            outer = dot_rows(jnp.concatenate([msg_a[at, :], msg_b[at, :]], axis=0), factor)
            out[k, m * LANES : (m + 1) * LANES, :] = inner[m * LANES : (m + 1) * LANES] + outer


def fill_z(ext, fields, top, bottom, low=0, count=None):
    for k, (ref, f) in enumerate(fields):
        depth = ref.shape[1]
        layers = depth if count is None else count
        first, last = max(low - 4, 0), min(low + layers + 4, depth)
        ext[k, first - low + 4 : last - low + 4] = ref[f, first:last]
        for g in range(first - (low - 4)):
            ext[k, g] = top(k, 4 - first + low - 4 + g)
        for g in range(low + layers + 4 - last):
            ext[k, last - low + 4 + g] = bottom(k, g)


def taps(read, forward):
    total = None
    for tap, coeff in enumerate(COEFFS, 1):
        upper = tap if forward else tap - 1
        lower = 1 - tap if forward else -tap
        term = coeff * (read(upper) - read(lower))
        total = term if total is None else total + term
    return total


def along_x(ext, k, z, rows, forward):
    return taps(lambda d: ext[k, z, 8 + d : 8 + d + rows, :], forward)


def along_z(ext, k, z, forward):
    return taps(lambda d: ext[k, z + 4 + d], forward)


def along_y(values, k, z, rows):
    return values[k, pl.ds(pl.multiple_of(z * rows, rows), rows), :]


def velocity_half(old, buoyancy, out, ex, ey, ez):
    depth, rows = out.shape[1], out.shape[2]

    def layer(z, _):
        scale = STEP * buoyancy[0, z]
        zx = along_z(ez, 0, z, False)
        zy = along_z(ez, 1, z, False)
        zz = along_z(ez, 2, z, True)
        x = along_x(ex, 0, z, rows, True)
        out[0, z] = old[0, z] + scale * (x + along_y(ey, 0, z, rows) + zx)
        x = along_x(ex, 1, z, rows, False)
        out[1, z] = old[1, z] + scale * (x + along_y(ey, 1, z, rows) + zy)
        x = along_x(ex, 2, z, rows, False)
        out[2, z] = old[2, z] + scale * (x + along_y(ey, 2, z, rows) + zz)
        return 0

    lax.fori_loop(0, depth, layer, 0, unroll=4 if rows > 16 else depth)


def stress_half(old, lame, shear, put, low, count, ex, ey, ez):
    rows = ex.shape[2] - 16

    def layer(n, _):
        z = n + low
        exx = along_x(ex, 0, n, rows, False)
        eyy = along_y(ey, 1, n, rows)
        ezz = along_z(ez, 2, n, False)
        mu = STEP * shear(z)
        common = (STEP * lame(z)) * (exx + eyy + ezz)
        double = mu + mu
        put(0, z, n, old(0, z) + (common + double * exx))
        put(1, z, n, old(1, z) + (common + double * eyy))
        put(2, z, n, old(2, z) + (common + double * ezz))
        x = along_x(ex, 1, n, rows, True)
        put(3, z, n, old(3, z) + mu * (along_y(ey, 0, n, rows) + x))
        x = along_x(ex, 2, n, rows, True)
        put(4, z, n, old(4, z) + mu * (along_z(ez, 0, n, True) + x))
        y = along_y(ey, 2, n, rows)
        put(5, z, n, old(5, z) + mu * (along_z(ez, 1, n, True) + y))
        return 0

    lax.fori_loop(0, count, layer, 0, unroll=4 if rows > 16 else count)


def zeros_like_plane(ref):
    return jnp.zeros(ref.shape[-2:], F32)


def after_before(msg_a, msg_b, at, parity):
    even = parity == 0
    a, b = msg_a[at, :], msg_b[at, :]
    return jnp.where(even, a, b), jnp.where(even, b, a)


def pack_kernel(
    par, fine, coarse, past, medium, out_a, out_b, out_1, out_2, planes, outer,
    turned, first, last, state, before, light, sems,
):
    pi, pj = par[0], par[1]
    depth, rows = fine.shape[1], fine.shape[2]
    part = coarse.shape[2]
    copies = [
        pltpu.make_async_copy(coarse, state, sems.at[0]),
        pltpu.make_async_copy(past, before, sems.at[1]),
        pltpu.make_async_copy(medium.at[0:1, depth - 4 :], light, sems.at[2]),
    ]
    for k, (f, _) in enumerate(VEL_X):
        head, tail = fine.at[f, :, 0:8, :], fine.at[f, :, rows - 8 : rows, :]
        copies.append(pltpu.make_async_copy(head, first.at[k], sems.at[3 + 2 * k]))
        copies.append(pltpu.make_async_copy(tail, last.at[k], sems.at[4 + 2 * k]))
    for k, (f, _) in enumerate(VEL_Y):
        copies.append(pltpu.make_async_copy(fine.at[f], turned.at[k], sems.at[9 + k]))
    for copy in copies:
        copy.start()
    for copy in copies[:3]:
        copy.wait()
    upper = pj == 0
    for n, f in enumerate(CROSSING):
        for layer in range(2):
            now = state[f, layer]
            later = 1.5 * now - 0.5 * before[f, layer]
            for p, plane in ((2 * n + layer, now), (12 + 2 * n + layer, later)):
                planes[pl.ds(p * part, part), :] = plane
                outer[p : p + 1, :] = jnp.where(upper, plane[:1], plane[part - 1 :])
    base = 12 * depth
    put_columns((out_a, out_b), base, [(state, f) for f, _ in VEL_Y])
    put_rows(out_a, out_b, base + 24, [(light, 0)], pi)
    put_columns((out_a, out_b), base + 40, [(planes, None)])
    base = 24 * (depth * rows // LANES)
    put_rows(out_1, out_2, base, [(state, f) for f, _ in VEL_X], pj)
    base += 12 * coarse.shape[1]
    put_columns((out_1, out_2), base, [(light, 0)])
    out_1[base + 16 : base + 40, :] = outer[...]
    out_2[base + 16 : base + 40, :] = outer[...]
    for copy in copies[3:9]:
        copy.wait()
    put_edge_rows(out_a, out_b, 0, [(first, last, k) for k in range(3)], pi)
    for k in range(3):
        copies[9 + k].wait()
        base = 8 * k * (depth * rows // LANES)
        put_columns((out_1, out_2), base, [(turned, k)])


def crossing_kernel(par, planes, msg_a, msg_b, msg_2, first, second):
    count = planes.shape[0]
    blocks = count // LANES
    even = par[0] == 0
    base = msg_a.shape[0] - 8 * blocks
    left, right = [], []
    for m in range(blocks):
        a = msg_a[pl.ds(base + 8 * m, 8), :]
        b = msg_b[pl.ds(base + 8 * m, 8), :]
        left.append(jnp.where(even, b, a)[7:8])
        right.append(jnp.where(even, a, b)[0:1])
    fill = [jnp.zeros((8 - blocks, LANES), F32)]
    left, right = (jnp.concatenate(side + fill, axis=0) for side in (left, right))
    half = count // 2
    first[0:half, :] = planes[:half, :]
    first[half : half + 24, :] = msg_2[msg_2.shape[0] - 24 :, :]
    first[half + 24 : half + 32, :] = left
    first[half + 32 : half + 40, :] = right
    second[...] = planes[half:, :]


def expand_ghosts(
    par, own, other, prow, pcol, ghost, level, planes, ends=None, known=None
):
    core = par[1]
    row_base, col_base = par[2] * (prow.shape[1] // 2), par[3] * LANES
    part = (own.shape[0] - 40) // 12
    rows = prow.shape[1]
    low = core == 0
    count = 12 * part
    source = lax.broadcasted_iota(jnp.int32, (LANES, LANES), 0)
    pick_cols = (source == pcol[...] - col_base).astype(BF16)
    pick_cols = jnp.concatenate([pick_cols, pick_cols], axis=0)
    source = lax.broadcasted_iota(jnp.int32, (2 * part, rows), 0)
    pick_rows = (source == prow[...] - row_base).astype(BF16)
    pick_rows = jnp.concatenate([pick_rows, pick_rows], axis=0)

    def spread(x):
        return dot(jnp.concatenate(split(x), axis=1), pick_cols)

    mine, theirs = (
        spread(jnp.concatenate([main[0:count, :], ref[count : count + 24, :]], axis=0))
        for main, ref in zip(planes, (own, other))
    )
    first, second = jnp.where(low, mine, theirs), jnp.where(low, theirs, mine)
    above, below = first[count:], second[count:]
    beside = []
    for ref in (own, other):
        side = jnp.where(low, ref[count + 24 : count + 32, :], ref[count + 32 : count + 40, :])
        side = jnp.concatenate([side, jnp.zeros((LANES - 8, LANES), F32)], axis=0)
        beside.append(side.T)
    side_1 = jnp.where(low, beside[0], beside[1])
    side_2 = jnp.where(low, beside[1], beside[0])
    lane = lax.broadcasted_iota(jnp.int32, (rows, LANES), 1)
    row = lax.broadcasted_iota(jnp.int32, (rows, LANES), 0)
    edge = lane == jnp.where(low, 0, LANES - 1)
    edge_row = edge[:1]
    if ends is not None:
        above = above + jnp.where(edge_row, ends[0], 0.0)
        below = below + jnp.where(edge_row, ends[1], 0.0)
    group = LANES // part
    if known is not None:
        own_row, other_row = own[count : count + 24, :], other[count : count + 24, :]
        for base, x in (
            (48, jnp.where(low, own_row, other_row)), (72, jnp.where(low, other_row, own_row))
        ):
            x = jnp.where(low, x[:, :1], x[:, LANES - 1 :])
            known[base : base + 24, :] = jnp.broadcast_to(x, (24, LANES))
        for p in range(24):
            q, t = p % group, p // group
            last = side_2[(q + 1) * part - 1 : (q + 1) * part, t : t + 1]
            first_row = side_1[q * part : q * part + 1, t : t + 1]
            known[p : p + 1, :] = jnp.broadcast_to(last, (1, LANES))
            known[24 + p : 25 + p, :] = jnp.broadcast_to(first_row, (1, LANES))
    columns = []
    for q in range(group):
        at = slice(q * part, (q + 1) * part)
        column = jnp.concatenate([side_1[at], side_2[at]], axis=0)
        columns.append(dot(pick_rows, jnp.concatenate(split(column), axis=0), ((0,), (0,))))
    for n in range(12):
        p = 12 * level + n
        at = slice(n * part, (n + 1) * part)
        plane = jnp.concatenate([first[at], second[at]], axis=0)
        full = dot(pick_rows, jnp.concatenate(split(plane), axis=0), ((0,), (0,)))
        column = columns[p % group][:, p // group : p // group + 1]
        full = full + jnp.where(edge, column, 0.0)
        full = full + jnp.where(row == 0, above[p : p + 1], 0.0)
        ghost[n] = full + jnp.where(row == rows - 1, below[p : p + 1], 0.0)


def ends_of(par, msg_a, msg_b):
    base = msg_a.shape[0] - 24
    below, above = after_before(msg_a, msg_b, slice(base, base + 24), par[0])
    return above, below


def later_ghost_kernel(
    par, own, other, prow, pcol, later_own, later_other, msg_a, msg_b, ghost
):
    planes = later_own, later_other
    ends = ends_of(par, msg_a, msg_b)
    expand_ghosts(par, own, other, prow, pcol, ghost, 1, planes, ends=ends)


def ghost_rate(planes, z, depth, forward):
    total = None
    for tap, coeff in enumerate(COEFFS, 1):
        g = z + (tap if forward else tap - 1) - depth
        if g >= 0:
            term = coeff * planes[g // 2]
            total = term if total is None else total + term
    return total


def ghost_kernel(
    par, half, buoyancy, own, other, prow, pcol,
    out, ghost, known, out_a, out_b, out_1, out_2,
):
    planes = own, other
    expand_ghosts(par, own, other, prow, pcol, ghost, 0, planes, known=known)
    depth = half.shape[1]
    for c, (f, forward) in enumerate(VEL_Z):
        out[c, 0 : depth - 4] = half[c, 0 : depth - 4]
        n = CROSSING.index(f)
        planes = [ghost[2 * n], ghost[2 * n + 1]]
        for z in range(depth - 4, depth):
            value = half[c, z]
            rate = ghost_rate(planes, z, depth, forward)
            if rate is not None:
                value = value + (STEP * buoyancy[0, z]) * rate
            out[c, z] = value
    moved = [(out, c) for c in range(3)]
    put_rows(out_a, out_b, 0, moved, par[0])
    put_columns((out_1, out_2), 0, moved)
    even = par[0] == 0
    up, down = known[0:24, :], known[24:48, :]
    base = 12 * depth
    out_a[base:, :] = jnp.where(even, up, down)
    out_b[base:, :] = jnp.where(even, down, up)


def add_corners(
    par, half, buoyancy, half_ghost, known, begin_a, begin_b, begin_2, msg_a, msg_b, msg_2,
    velocity, ghost, rows_a, rows_b, cols_2, base_x, base_y,
):
    pi, low = par[0], par[1] == 0
    depth, rows = half.shape[1], half.shape[2]
    lane = lax.broadcasted_iota(jnp.int32, (rows, LANES), 1)
    row = lax.broadcasted_iota(jnp.int32, (rows, LANES), 0)
    edge = lane == jnp.where(low, 0, LANES - 1)
    first, last = edge & (row == 0), edge & (row == rows - 1)
    above, below = ends_of(par, msg_a, msg_b)
    for n in range(12):
        plane = half_ghost[n] + jnp.where(first, above[n : n + 1], 0.0)
        ghost[n] = plane + jnp.where(last, below[n : n + 1], 0.0)
    for source, target in ((msg_a, rows_a), (msg_b, rows_b), (msg_2, cols_2)):
        target[...] = source[...]
    even = pi == 0
    near = lax.broadcasted_iota(jnp.int32, (8, LANES), 0)
    lane = lax.broadcasted_iota(jnp.int32, (8, LANES), 1)
    edge = lane == jnp.where(low, 0, LANES - 1)
    beside = near == jnp.where(low, 7, 0)
    blocks = depth * rows // LANES
    none = jnp.zeros((1, LANES), F32)

    def rates(x, n, z, forward):
        found = []
        for odd in range(2):
            rate = ghost_rate([x[2 * n : 2 * n + 1], x[2 * n + 1 : 2 * n + 2]], z + odd, depth, forward)
            found.append(none if rate is None else rate)
        return found

    up, down = known[0:12, :], known[24:36, :]
    row_above, row_below = known[48:60, :], known[72:84, :]
    for c, (f, forward) in enumerate(VEL_Z):
        n = CROSSING.index(f)
        velocity[c, 0 : depth - 4] = half[c, 0 : depth - 4]
        for pair in range(2):
            z = depth - 4 + 2 * pair
            tops, bottoms = rates(above, n, z, forward), rates(below, n, z, forward)
            for odd in range(2):
                change = jnp.where(first, tops[odd], 0.0) + jnp.where(last, bottoms[odd], 0.0)
                scale = STEP * buoyancy[0, z + odd]
                velocity[c, z + odd] = half[c, z + odd] + scale * change
            after, before = after_before(
                begin_a, begin_b, slice(base_x + 8 * pair, base_x + 8 * pair + 8), pi
            )
            rate = rates(up, n, z, forward)
            change = jnp.where(near == 0, rate[0], jnp.where(near == 4, rate[1], 0.0))
            after = jnp.where(edge, (STEP * after) * change, 0.0)
            rate = rates(down, n, z, forward)
            change = jnp.where(near == 3, rate[0], jnp.where(near == 7, rate[1], 0.0))
            before = jnp.where(edge, (STEP * before) * change, 0.0)
            at = pl.ds(4 * (c * depth + z), 8)
            rows_a[at, :] = rows_a[at, :] + jnp.where(even, after, before)
            rows_b[at, :] = rows_b[at, :] + jnp.where(even, before, after)
            tops, bottoms = rates(row_above, n, z, forward), rates(row_below, n, z, forward)
            change = jnp.where(lane == 0, tops[0], jnp.where(lane == rows - 1, bottoms[0], 0.0))
            change = jnp.where(lane == rows, tops[1], change)
            change = jnp.where(lane == 2 * rows - 1, bottoms[1], change)
            light = begin_2[base_y + 8 * pair : base_y + 8 * pair + 8, :]
            at = pl.ds(8 * (c * blocks + blocks - 2 + pair), 8)
            cols_2[at, :] = cols_2[at, :] + jnp.where(beside, (STEP * light) * change, 0.0)


def stress_fields(ref, table):
    offset = 9 - ref.shape[0]
    return [(ref, f - offset) for f, _ in table]


def velocity_fill(par, stress, msg_a, msg_b, msg_1, msg_2, tile, halo, bottom, ex, ey, ez):
    pi, pj = par[0], par[1]
    none = zeros_like_plane(stress)
    fill_z(ez, stress_fields(stress, VEL_Z), lambda k, g: none, bottom)
    fill_x(ex, stress_fields(stress, VEL_X), msg_a, msg_b, 0, pi)
    fill_y(
        ey, stress_fields(stress, VEL_Y), [d for _, d in VEL_Y], msg_1, msg_2, 0, pj, tile, halo
    )


def first_velocity_kernel(
    par, state, buoyancy, msg_a, msg_b, msg_1, msg_2, tile, halo, out, ex, ey, ez
):
    none = zeros_like_plane(state)
    velocity_fill(
        par, state, msg_a, msg_b, msg_1, msg_2, tile, halo, lambda k, g: none, ex, ey, ez
    )
    velocity_half(state, buoyancy, out, ex, ey, ez)


def velocity_kernel(
    par, old, stress, buoyancy, ghost, start, msg_a, msg_b, msg_1, msg_2, tile, halo, means,
    out, out_a, out_b, out_1, out_2, coarse, ex, ey, ez, summed, halves,
):
    order = [CROSSING.index(f) for f, _ in VEL_Z]
    velocity_fill(
        par, stress, msg_a, msg_b, msg_1, msg_2, tile, halo,
        lambda k, g: ghost[2 * order[k] + g // 2], ex, ey, ez,
    )
    velocity_half(old, buoyancy, out, ex, ey, ez)
    moved = [(out, c) for c in range(3)]
    put_rows(out_a, out_b, 0, moved, par[0])
    put_columns((out_1, out_2), 0, moved)
    low = out.shape[1] - 8
    lift(start, STR_Z, [out.at[c, low:] for c in range(3)], means, coarse, summed, halves)


def stress_fill(
    par, velocity, bottom, msg_a, msg_b, msg_1, msg_2, tile, halo, ex, ey, ez, low, count
):
    pi, pj = par[0], par[1]
    none = zeros_like_plane(velocity)
    fields = [(velocity, c) for c in range(3)]
    fill_z(ez, fields, lambda k, g: none, bottom, low, count)
    fill_x(ex, fields, msg_a, msg_b, 0, pi, low, count)
    fill_y(
        ey, fields, [d for _, d in STR_Y], msg_1, msg_2, 0, pj, tile, halo, low, count
    )


def stress_kernel(
    par, half, state, medium, half_ghost, known, begin_a, begin_b, begin_2, msg_a, msg_b, msg_1,
    msg_2, tile, halo, out, velocity, out_a, out_b, out_1, out_2, ex, ey, ez, ghost, rows_a, rows_b,
    cols_2, *, base_x, base_y,
):
    depth = half.shape[1]
    add_corners(
        par, half, medium, half_ghost, known, begin_a, begin_b, begin_2, msg_a, msg_b, msg_2,
        velocity, ghost, rows_a, rows_b, cols_2, base_x, base_y,
    )
    stress_fill(
        par, velocity, lambda k, g: ghost[2 * k + g // 2], rows_a, rows_b, msg_1, cols_2,
        tile, halo, ex, ey, ez, 0, depth,
    )

    def put(c, z, n, value):
        out[c, z] = value

    stress_half(
        lambda c, z: state[SXX + c, z], lambda z: medium[1, z], lambda z: medium[2, z],
        put, 0, depth, ex, ey, ez,
    )
    put_rows(out_a, out_b, 0, stress_fields(out, VEL_X), par[0])
    put_columns((out_1, out_2), 0, stress_fields(out, VEL_Y))


def lift(start, table, fields, means, coarse, summed, halves):
    rows = summed.shape[0]
    part = rows // 4
    low = start.shape[1] - 8
    for n, (k, m) in enumerate(above_planes(table)):
        f, new = table[k][0], fields[k]
        z = 2 * m
        total = (start[f, low + z] + start[f, low + z + 1]) + (new[z] + new[z + 1])
        summed[...] = total
        pairs = summed[pl.ds(0, 2 * part, stride=2), :] + summed[pl.ds(1, 2 * part, stride=2), :]
        at = pl.ds(n * part, part)
        halves[0, at, :] = pairs[:part]
        halves[1, at, :] = pairs[part:]
    count = coarse.shape[0]
    upper = dot(jnp.concatenate(split(halves[0, 0:count]), axis=1), means[0])
    lower = dot(jnp.concatenate(split(halves[1, 0:count]), axis=1), means[1])
    coarse[...] = upper + lower


def lower_stress_kernel(
    par, velocity, stress, medium, ghost, start, msg_a, msg_b, msg_1, msg_2, tile, halo, means,
    out, coarse, ex, ey, ez, summed, halves,
):
    depth, rows = velocity.shape[1], velocity.shape[2]
    low = depth - 8
    stress_fill(
        par, velocity, lambda k, g: ghost[2 * k + g // 2], msg_a, msg_b, msg_1, msg_2,
        tile, halo, ex, ey, ez, low, 8,
    )

    def put(c, z, n, value):
        out[c, n] = value

    stress_half(
        lambda c, z: stress[c, z], lambda z: medium[1, z], lambda z: medium[2, z],
        put, low, 8, ex, ey, ez,
    )
    fields = [out.at[f - SXX] for f, _ in VEL_Z]
    lift(start, VEL_Z, fields, means, coarse, summed, halves)


def upper_stress_kernel(
    par, below, velocity, stress, medium, msg_a, msg_b, msg_1, msg_2, tile, halo,
    out, done, ex, ey, ez,
):
    stress_fill(
        par, velocity, None, msg_a, msg_b, msg_1, msg_2, tile, halo, ex, ey, ez, 0, 8
    )
    out[0:3] = velocity[...]
    out[SXX:, velocity.shape[1] - 8 :] = below[...]

    def put(c, z, n, value):
        out[SXX + c, n] = value

    stress_half(
        lambda c, z: stress[c, z], lambda z: medium[1, z], lambda z: medium[2, z],
        put, 0, 8, ex, ey, ez,
    )
    done[...] = jnp.zeros_like(done)


def join(par, own, other, ghost, table, rows):
    half = LANES // 2
    even = par[1] == 0
    left = jnp.where(even, own[...], other[...])
    right = jnp.where(even, other[...], own[...])
    low = lax.broadcasted_iota(jnp.int32, left.shape, 1) < half
    ghost[...] = jnp.where(
        even,
        jnp.where(low, left, pltpu.roll(right, half, 1)),
        jnp.where(low, pltpu.roll(left, half, 1), right),
    )
    planes = above_planes(table)
    none = jnp.zeros((rows, LANES), F32)

    def layer(k, m):
        if (k, m) not in planes:
            return none
        return ghost[pl.ds(planes.index((k, m)) * rows, rows), :]

    return layer


def coarse_velocity_kernel(
    par, state, medium, own, other, msg_a, msg_b, msg_1, msg_2, tile, halo, done,
    out, out_1, out_2, out_c, ex, ey, ez, ghost, *, base_c, base_r,
):
    pi, pj = par[0], par[1]
    rows = state.shape[2]
    above = join(par, own, other, ghost, VEL_Z, state.shape[2])
    none = zeros_like_plane(state)
    fill_z(
        ez, stress_fields(state, VEL_Z),
        above, lambda k, g: none,
    )
    fill_x(ex, stress_fields(state, VEL_X), msg_1, msg_2, base_r, pj)
    fill_y(
        ey, stress_fields(state, VEL_Y), [d for _, d in VEL_Y], msg_a, msg_b, base_c, pi,
        tile, halo,
    )
    velocity_half(state, medium, out, ex, ey, ez)
    moved = [(out, c) for c in range(3)]
    put_rows(out_1, out_2, 0, moved, pj)
    put_columns((out_c,), 0, moved)


def coarse_stress_kernel(
    par, state, medium, velocity, own, other, msg_a, msg_b, msg_1, msg_2, tile, halo,
    out, ex, ey, ez, ghost,
):
    pi, pj = par[0], par[1]
    above = join(par, own, other, ghost, STR_Z, state.shape[2])
    depth, rows = state.shape[1], state.shape[2]
    none = zeros_like_plane(state)
    fields = [(velocity, c) for c in range(3)]
    fill_z(
        ez, fields, above, lambda k, g: none
    )
    fill_x(ex, fields, msg_1, msg_2, 0, pj)
    fill_y(ey, fields, [d for _, d in STR_Y], msg_a, msg_b, 0, pi, tile, halo)
    out[0:3] = velocity[...]

    def put(c, z, n, value):
        out[SXX + c, z] = value

    stress_half(
        lambda c, z: state[SXX + c, z], lambda z: medium[1, z], lambda z: medium[2, z],
        put, 0, depth, ex, ey, ez,
    )


def whole(shape):
    return pl.BlockSpec(shape, functools.partial(lambda rank, _: (0,) * rank, len(shape)))


def call(kernel, args, outs, scratch=(), flops=0, copied=0, light=False):
    specs = []
    for n, a in enumerate(args):
        specs.append(pl.BlockSpec(memory_space=pltpu.HBM) if n < copied else whole(a.shape))
    size = 1024 if light else sum(4 * int(np.prod(a.shape)) for a in args) + sum(4 * int(np.prod(o)) for o in outs)

    def placed(*refs):
        i, j = lax.axis_index("gx"), lax.axis_index("gy")
        kernel((i % 2, j % 2, i, j // 2), *refs)

    return pl.pallas_call(
        placed,
        grid=(1,),
        in_specs=specs,
        out_specs=[whole(o) for o in outs],
        out_shape=[jax.ShapeDtypeStruct(o, F32) for o in outs],
        scratch_shapes=[pltpu.VMEM(s, F32) for s in scratch]
        + ([pltpu.SemaphoreType.DMA((12,))] if copied else []),
        compiler_params=pltpu.CompilerParams(vmem_limit_bytes=(54 if copied else 24) * 1024 * 1024),
        cost_estimate=pl.CostEstimate(flops=flops, bytes_accessed=size, transcendentals=0),
    )(*args)


def matchings(axis):
    size = lax.axis_size(axis)
    result = []
    for start in range(2):
        pairs = []
        for low in range(start, size - 1, 2):
            pairs += [(low, low + 1), (low + 1, low)]
        result.append(pairs)
    return result


def exchange(axis, first, second):
    one, two = matchings(axis)
    return lax.ppermute(first, axis, one), lax.ppermute(second, axis, two)


def body(
    fine_state, fine_medium, coarse_state, coarse_medium, coarse_past, parent_rows, parent_cols
):
    size_x, size_y = lax.axis_size("gx"), lax.axis_size("gy")
    i, j = lax.axis_index("gx"), lax.axis_index("gy")
    depth, rows, cols = fine_state.shape[1:]
    thick, part = coarse_state.shape[1:3]
    blocks = depth * rows // LANES
    tile, halo = (jnp.asarray(c) for c in lane_constants())
    means = jnp.asarray(mean_constants())
    across = [
        (p * size_y + q, (q // 2) * size_y + 2 * p + q % 2)
        for p in range(size_x)
        for q in range(size_y)
    ]
    partner = matchings("gy")[0]

    both = ("gx", "gy")

    rows_msg, cols_msg = 12 * depth, 24 * blocks
    coarse_cols, coarse_rows = 24, 12 * thick
    count = 24 * part
    out_a, out_b, out_1, out_2, planes, outer = call(
        pack_kernel,
        [fine_state, coarse_state, coarse_past, fine_medium],
        [(rows_msg + coarse_cols + 16 + count * 8 // LANES, LANES)] * 2
        + [(cols_msg + coarse_rows + 40, LANES)] * 2
        + [(count, LANES), (24, LANES)],
        [(3,) + fine_state.shape[1:], (3, depth, 8, cols), (3, depth, 8, cols),
         coarse_state.shape, coarse_past.shape, (1, 4, rows, cols)],
        copied=4,
    )
    msg_a, msg_b = exchange("gx", out_a, out_b)
    msg_1, msg_2 = exchange("gy", out_1, out_2)
    begin = msg_a, msg_b, msg_1, msg_2
    crossing, later = call(
        crossing_kernel,
        [planes, msg_a, msg_b, msg_2],
        [(count // 2 + 40, LANES), (count // 2, LANES)],
    )
    own = lax.ppermute(crossing, both, across)

    shape = (depth, rows, cols)

    def scratch_of(depth, rows):
        return [
            (3, depth, rows + 16, LANES), (3, depth * rows, LANES), (3, depth + 8, rows, LANES),
        ]

    cells = depth * rows * cols
    halves = [(rows_msg + 8, LANES)] * 2 + [(cols_msg + 24, LANES), (cols_msg + 16, LANES)]
    (half,) = call(
        first_velocity_kernel,
        [fine_state, fine_medium, msg_a, msg_b, msg_1, msg_2, tile, halo],
        [(3,) + shape],
        scratch_of(depth, rows),
        flops=400 * cells,
    )
    own, half = lax.optimization_barrier((own, half))
    other = lax.ppermute(own, "gy", partner)
    parents = parent_rows.reshape(1, rows), parent_cols.reshape(1, cols)
    half, half_ghost, known, out_a, out_b, out_1, out_2 = call(
        ghost_kernel,
        [half, fine_medium, own, other, *parents],
        [(3,) + shape, (12, rows, cols), (96, LANES)] + [(rows_msg + 24, LANES)] * 2
        + [(cols_msg + 40, LANES), (cols_msg + 32, LANES)],
    )
    msgs = exchange("gx", out_a, out_b) + exchange("gy", out_1, out_2)
    later, half = lax.optimization_barrier((later, half))
    later = lax.ppermute(later, both, across)
    ends = msgs[:2]
    stress, velocity, out_a, out_b, out_1, out_2 = call(
        functools.partial(
            stress_kernel, base_x=rows_msg + coarse_cols, base_y=cols_msg + coarse_rows
        ),
        [half, fine_state, fine_medium, half_ghost, known, begin[0], begin[1], begin[3],
         *msgs, tile, halo],
        [(6,) + shape, (3,) + shape] + halves,
        scratch_of(depth, rows)
        + [(12, rows, cols)] + [(rows_msg + 24, LANES)] * 2 + [(cols_msg + 32, LANES)],
        flops=400 * cells,
    )
    msgs = exchange("gx", out_a, out_b) + exchange("gy", out_1, out_2)
    later, stress = lax.optimization_barrier((later, stress))
    later_other = lax.ppermute(later, "gy", partner)
    (ghost,) = call(
        later_ghost_kernel,
        [own, other, *parents, later, later_other, *ends],
        [(12, rows, cols)],
    )
    moved_v, moved_s = (len(above_planes(t)) * part for t in (STR_Z, VEL_Z))
    lift_scratch = [(rows, cols), (2, count // 2, LANES)]
    velocity, out_a, out_b, out_1, out_2, lifted = call(
        velocity_kernel,
        [velocity, stress, fine_medium, ghost, fine_state, *msgs, tile, halo, means],
        [(3,) + shape] + halves + [(moved_v, LANES)],
        scratch_of(depth, rows) + lift_scratch,
        flops=400 * cells,
    )
    msgs = exchange("gx", out_a, out_b) + exchange("gy", out_1, out_2)
    moving = lax.ppermute(lifted, both, across)
    below, lifted = call(
        lower_stress_kernel,
        [velocity, stress, fine_medium, ghost, fine_state, *msgs, tile, halo, means],
        [(6, 8, rows, cols), (moved_s, LANES)],
        scratch_of(8, rows) + lift_scratch,
        light=True,
    )
    own = lax.ppermute(lifted, both, across)
    fine_out, done = call(
        upper_stress_kernel,
        [below, velocity, stress, fine_medium, *msgs, tile, halo],
        [(9,) + shape, (8, LANES)],
        scratch_of(8, rows),
        flops=200 * cells,
    )
    own, done, moving = lax.optimization_barrier((own, done, moving))
    other = lax.ppermute(own, "gy", partner)
    moving_other = lax.ppermute(moving, "gy", partner)

    shape = (thick, part, LANES)
    velocity, out_1, out_2, out_c = call(
        functools.partial(coarse_velocity_kernel, base_c=rows_msg, base_r=cols_msg),
        [coarse_state, coarse_medium, own, other, *begin, tile, halo, done],
        [(3,) + shape, (coarse_rows, LANES), (coarse_rows, LANES), (coarse_cols, LANES)],
        scratch_of(thick, part) + [(moved_s, LANES)],
    )
    msgs = exchange("gx", out_c, out_c) + exchange("gy", out_1, out_2)
    (coarse_out,) = call(
        coarse_stress_kernel,
        [coarse_state, coarse_medium, velocity, moving, moving_other, *msgs, tile, halo],
        [(9,) + shape],
        scratch_of(thick, part) + [(moved_v, LANES)],
    )
    return (fine_out, coarse_out)


def solution(mesh):
    placed = (
        P(None, None, "gx", "gy"),
        P(None, None, "gx", "gy"),
        P(None, None, "gy", "gx"),
        P(None, None, "gy", "gx"),
        P(None, None, "gy", "gx"),
        P("gx"),
        P("gy"),
    )
    return jax.shard_map(
        body,
        mesh=mesh,
        in_specs=placed,
        out_specs=(P(None, None, "gx", "gy"), P(None, None, "gy", "gx")),
        check_vma=False,
    )
```

```python
import functools

import jax
import jax.numpy as jnp
import ml_dtypes
import numpy as np
from jax import lax
from jax.experimental import pallas as pl
from jax.experimental.pallas import tpu as pltpu
from jax.sharding import PartitionSpec as P

COEFFS = (1225.0 / 1024.0, -245.0 / 3072.0, 49.0 / 5120.0, -5.0 / 7168.0)
STEP = 0.1
LANES = 128
F32 = jnp.float32
BF16 = jnp.bfloat16

VX, VY, VZ, SXX, SYY, SZZ, SXY, SXZ, SYZ = range(9)
CROSSING = (VX, VY, VZ, SXZ, SYZ, SZZ)
VEL_X = ((SXX, True), (SXY, False), (SXZ, False))
VEL_Y = ((SXY, False), (SYY, True), (SYZ, False))
VEL_Z = ((SXZ, False), (SYZ, False), (SZZ, True))
STR_X = ((VX, False), (VY, True), (VZ, True))
STR_Y = ((VX, True), (VY, False), (VZ, True))
STR_Z = ((VX, True), (VY, True), (VZ, False))


def above_planes(table):
    skip = table is VEL_Z
    return [(k, m) for k, (_, forward) in enumerate(table) for m in range(int(skip and forward), 4)]


def band(width, forward):
    matrix = np.zeros((width + 8, width), np.float64)
    for out in range(width):
        for tap, coeff in enumerate(COEFFS, 1):
            upper = out + tap if forward else out + tap - 1
            lower = out + 1 - tap if forward else out - tap
            matrix[4 + upper, out] += coeff
            matrix[4 + lower, out] -= coeff
    return matrix


def two_part(matrix):
    high = matrix.astype(ml_dtypes.bfloat16)
    low = (matrix - high.astype(np.float64)).astype(ml_dtypes.bfloat16)
    return np.block([[high, low], [high, np.zeros_like(low)]]).astype(ml_dtypes.bfloat16)


def lane_constants():
    tile = np.stack([two_part(band(LANES, f)[4:-4]) for f in (False, True)])
    halo = []
    for parity in range(2):
        for forward in (False, True):
            matrix = band(LANES, forward)
            after = np.zeros((8, LANES))
            before = np.zeros((8, LANES))
            after[:4] = matrix[-4:]
            before[4:] = matrix[:4]
            pair = (after, before) if parity == 0 else (before, after)
            halo.append(two_part(np.concatenate(pair)))
    halo = np.stack(halo).reshape(2, 2, 32, 2 * LANES)
    return tile, halo


def mean_constants():
    half = LANES // 2
    place = np.zeros((2, LANES, LANES), np.float32)
    for lane in range(LANES):
        for part in range(2):
            place[part, lane, part * half + lane // 2] = 1.0 / 16.0
    return np.concatenate([place, place], axis=1).astype(ml_dtypes.bfloat16)


def split(x):
    high = x.astype(BF16)
    return high, (x - high.astype(F32)).astype(BF16)


def fold(x):
    half = x.shape[1] // 2
    return x[:, :half] + x[:, half:]


def dot(a, b, dims=((1,), (0,))):
    return lax.dot_general(a, b, (dims, ((), ())), preferred_element_type=F32)


def dot_lanes(x, matrix):
    return fold(dot(jnp.concatenate(split(x), axis=1), matrix))


def dot_rows(x, matrix):
    return fold(dot(jnp.concatenate(split(x), axis=0), matrix, ((0,), (0,))))


def flat(x):
    return x.reshape(x.shape[0] * x.shape[1], x.shape[2])


def upper_half(shape):
    return lax.broadcasted_iota(jnp.int32, shape, 0) < 4


def put_rows(out_a, out_b, base, fields, parity):
    parts = []
    for ref, f in fields:
        rows = ref.shape[2]
        parts.append((ref.at[:, :, 0:8, :], ref.at[:, :, rows - 8 : rows, :], f))
    put_edge_rows(out_a, out_b, base, parts, parity)


def put_edge_rows(out_a, out_b, base, fields, parity):
    even = parity == 0
    top = upper_half((8, LANES))
    for k, (head, tail, f) in enumerate(fields):
        depth = head.shape[1]
        for z in range(0, depth, 2):
            first = jnp.where(top, head[f, z], pltpu.roll(head[f, z + 1], 4, 0))
            last = jnp.where(top, pltpu.roll(tail[f, z], 4, 0), tail[f, z + 1])
            at = pl.ds(base + 4 * (k * depth + z), 8)
            out_a[at, :] = jnp.where(even, last, first)
            out_b[at, :] = jnp.where(even, first, last)


def put_columns(outs, base, fields):
    row = lax.broadcasted_iota(jnp.int32, (8, 2 * LANES), 0)
    lane = lax.broadcasted_iota(jnp.int32, (8, 2 * LANES), 1) % LANES
    edges = (lane == jnp.where(row < 4, row, LANES - 8 + row)).astype(BF16)
    for k, (ref, f) in enumerate(fields):
        x = jnp.concatenate([r[...] for r in ref], axis=0) if f is None else flat(ref[f])
        x = jnp.concatenate(split(x), axis=1)
        turned = dot(edges, x, ((1,), (1,)))
        blocks = turned.shape[1] // LANES
        for m in range(blocks):
            for out in outs:
                out[pl.ds(base + 8 * (k * blocks + m), 8), :] = turned[:, m * LANES : (m + 1) * LANES]


def fill_x(ext, fields, msg_a, msg_b, base, parity, low=0, count=None):
    even = parity == 0
    for k, (ref, f) in enumerate(fields):
        depth, rows = ref.shape[1], ref.shape[2]
        layers = depth if count is None else count
        ext[k, :, 8 : 8 + rows, :] = ref[f, low : low + layers]
        for z in range(0, layers, 2):
            at = pl.ds(base + 4 * (k * depth + low + z), 8)
            a, b = msg_a[at, :], msg_b[at, :]
            after, before = jnp.where(even, a, b), jnp.where(even, b, a)
            ext[k, z, 8 + rows : 16 + rows, :] = after
            ext[k, z + 1, 8 + rows : 16 + rows, :] = pltpu.roll(after, 4, 0)
            ext[k, z, 0:8, :] = pltpu.roll(before, 4, 0)
            ext[k, z + 1, 0:8, :] = before


def fill_y(out, fields, directions, msg_a, msg_b, base, parity, tile, halo, low=0, count=None):
    for k, (ref, f) in enumerate(fields):
        depth, rows = ref.shape[1], ref.shape[2]
        layers = depth if count is None else count
        forward = int(directions[k])
        inner = dot_lanes(flat(ref[f, low : low + layers]), tile[forward])
        factor = halo[parity, forward]
        start, blocks = low * rows // LANES, depth * rows // LANES
        for m in range(layers * rows // LANES):
            at = pl.ds(base + 8 * (k * blocks + start + m), 8)
            outer = dot_rows(jnp.concatenate([msg_a[at, :], msg_b[at, :]], axis=0), factor)
            out[k, m * LANES : (m + 1) * LANES, :] = inner[m * LANES : (m + 1) * LANES] + outer


def fill_z(ext, fields, top, bottom, low=0, count=None):
    for k, (ref, f) in enumerate(fields):
        depth = ref.shape[1]
        layers = depth if count is None else count
        first, last = max(low - 4, 0), min(low + layers + 4, depth)
        ext[k, first - low + 4 : last - low + 4] = ref[f, first:last]
        for g in range(first - (low - 4)):
            ext[k, g] = top(k, 4 - first + low - 4 + g)
        for g in range(low + layers + 4 - last):
            ext[k, last - low + 4 + g] = bottom(k, g)


def taps(read, forward):
    total = None
    for tap, coeff in enumerate(COEFFS, 1):
        upper = tap if forward else tap - 1
        lower = 1 - tap if forward else -tap
        term = coeff * (read(upper) - read(lower))
        total = term if total is None else total + term
    return total


def along_x(ext, k, z, rows, forward):
    return taps(lambda d: ext[k, z, 8 + d : 8 + d + rows, :], forward)


def along_z(ext, k, z, forward):
    return taps(lambda d: ext[k, z + 4 + d], forward)


def along_y(values, k, z, rows):
    return values[k, pl.ds(pl.multiple_of(z * rows, rows), rows), :]


def velocity_half(old, buoyancy, out, ex, ey, ez):
    depth, rows = out.shape[1], out.shape[2]

    def layer(z, _):
        scale = STEP * buoyancy[0, z]
        zx = along_z(ez, 0, z, False)
        zy = along_z(ez, 1, z, False)
        zz = along_z(ez, 2, z, True)
        x = along_x(ex, 0, z, rows, True)
        out[0, z] = old[0, z] + scale * (x + along_y(ey, 0, z, rows) + zx)
        x = along_x(ex, 1, z, rows, False)
        out[1, z] = old[1, z] + scale * (x + along_y(ey, 1, z, rows) + zy)
        x = along_x(ex, 2, z, rows, False)
        out[2, z] = old[2, z] + scale * (x + along_y(ey, 2, z, rows) + zz)
        return 0

    lax.fori_loop(0, depth, layer, 0, unroll=4 if rows > 16 else depth)


def stress_half(old, lame, shear, put, low, count, ex, ey, ez):
    rows = ex.shape[2] - 16

    def layer(n, _):
        z = n + low
        exx = along_x(ex, 0, n, rows, False)
        eyy = along_y(ey, 1, n, rows)
        ezz = along_z(ez, 2, n, False)
        mu = STEP * shear(z)
        common = (STEP * lame(z)) * (exx + eyy + ezz)
        double = mu + mu
        put(0, z, n, old(0, z) + (common + double * exx))
        put(1, z, n, old(1, z) + (common + double * eyy))
        put(2, z, n, old(2, z) + (common + double * ezz))
        x = along_x(ex, 1, n, rows, True)
        put(3, z, n, old(3, z) + mu * (along_y(ey, 0, n, rows) + x))
        x = along_x(ex, 2, n, rows, True)
        put(4, z, n, old(4, z) + mu * (along_z(ez, 0, n, True) + x))
        y = along_y(ey, 2, n, rows)
        put(5, z, n, old(5, z) + mu * (along_z(ez, 1, n, True) + y))
        return 0

    lax.fori_loop(0, count, layer, 0, unroll=4 if rows > 16 else count)


def zeros_like_plane(ref):
    return jnp.zeros(ref.shape[-2:], F32)


def after_before(msg_a, msg_b, at, parity):
    even = parity == 0
    a, b = msg_a[at, :], msg_b[at, :]
    return jnp.where(even, a, b), jnp.where(even, b, a)


def pack_kernel(
    par, fine, coarse, past, medium, out_a, out_b, out_1, out_2, planes, planes_2, outer,
    turned, first, last, state, before, light, sems,
):
    pi, pj = par[0], par[1]
    depth, rows = fine.shape[1], fine.shape[2]
    part = coarse.shape[2]
    copies = [
        pltpu.make_async_copy(coarse, state, sems.at[0]),
        pltpu.make_async_copy(past, before, sems.at[1]),
        pltpu.make_async_copy(medium.at[0:1, depth - 4 :], light, sems.at[2]),
    ]
    for k, (f, _) in enumerate(VEL_X):
        head, tail = fine.at[f, :, 0:8, :], fine.at[f, :, rows - 8 : rows, :]
        copies.append(pltpu.make_async_copy(head, first.at[k], sems.at[3 + 2 * k]))
        copies.append(pltpu.make_async_copy(tail, last.at[k], sems.at[4 + 2 * k]))
    for k, (f, _) in enumerate(VEL_Y):
        copies.append(pltpu.make_async_copy(fine.at[f], turned.at[k], sems.at[9 + k]))
    for copy in copies:
        copy.start()
    for copy in copies[:3]:
        copy.wait()
    upper = pj == 0
    for n, f in enumerate(CROSSING):
        for layer in range(2):
            now = state[f, layer]
            later = 1.5 * now - 0.5 * before[f, layer]
            for p, plane in ((2 * n + layer, now), (12 + 2 * n + layer, later)):
                target = planes if p < 12 else planes_2
                target[pl.ds(p % 12 * part, part), :] = plane
                outer[p : p + 1, :] = jnp.where(upper, plane[:1], plane[part - 1 :])
    base = 12 * depth
    put_columns((out_a, out_b), base, [(state, f) for f, _ in VEL_Y])
    put_rows(out_a, out_b, base + 24, [(light, 0)], pi)
    put_columns((out_a, out_b), base + 40, [((planes, planes_2), None)])
    base = 24 * (depth * rows // LANES)
    put_rows(out_1, out_2, base, [(state, f) for f, _ in VEL_X], pj)
    base += 12 * coarse.shape[1]
    put_columns((out_1, out_2), base, [(light, 0)])
    out_1[base + 16 : base + 40, :] = outer[...]
    out_2[base + 16 : base + 40, :] = outer[...]
    for copy in copies[3:9]:
        copy.wait()
    put_edge_rows(out_a, out_b, 0, [(first, last, k) for k in range(3)], pi)
    for k in range(3):
        copies[9 + k].wait()
        base = 8 * k * (depth * rows // LANES)
        put_columns((out_1, out_2), base, [(turned, k)])


def crossing_kernel(par, planes, msg_a, msg_b, msg_2, first):
    count = 2 * planes.shape[0]
    blocks = count // LANES
    even = par[0] == 0
    base = msg_a.shape[0] - 8 * blocks
    left, right = [], []
    for m in range(blocks):
        a = msg_a[pl.ds(base + 8 * m, 8), :]
        b = msg_b[pl.ds(base + 8 * m, 8), :]
        left.append(jnp.where(even, b, a)[7:8])
        right.append(jnp.where(even, a, b)[0:1])
    fill = [jnp.zeros((8 - blocks, LANES), F32)]
    left, right = (jnp.concatenate(side + fill, axis=0) for side in (left, right))
    half = count // 2
    first[0:half, :] = planes[...]
    first[half : half + 24, :] = msg_2[msg_2.shape[0] - 24 :, :]
    first[half + 24 : half + 32, :] = left
    first[half + 32 : half + 40, :] = right


def expand_ghosts(
    par, own, other, prow, pcol, ghost, level, planes, ends=None, known=None
):
    core = par[1]
    row_base, col_base = par[2] * (prow.shape[1] // 2), par[3] * LANES
    part = (own.shape[0] - 40) // 12
    rows = prow.shape[1]
    low = core == 0
    count = 12 * part
    source = lax.broadcasted_iota(jnp.int32, (LANES, LANES), 0)
    pick_cols = (source == pcol[...] - col_base).astype(BF16)
    pick_cols = jnp.concatenate([pick_cols, pick_cols], axis=0)
    source = lax.broadcasted_iota(jnp.int32, (2 * part, rows), 0)
    pick_rows = (source == prow[...] - row_base).astype(BF16)
    pick_rows = jnp.concatenate([pick_rows, pick_rows], axis=0)

    def spread(x):
        return dot(jnp.concatenate(split(x), axis=1), pick_cols)

    mine, theirs = (
        spread(jnp.concatenate([main[0:count, :], ref[count : count + 24, :]], axis=0))
        for main, ref in zip(planes, (own, other))
    )
    first, second = jnp.where(low, mine, theirs), jnp.where(low, theirs, mine)
    above, below = first[count:], second[count:]
    beside = []
    for ref in (own, other):
        side = jnp.where(low, ref[count + 24 : count + 32, :], ref[count + 32 : count + 40, :])
        side = jnp.concatenate([side, jnp.zeros((LANES - 8, LANES), F32)], axis=0)
        beside.append(side.T)
    side_1 = jnp.where(low, beside[0], beside[1])
    side_2 = jnp.where(low, beside[1], beside[0])
    lane = lax.broadcasted_iota(jnp.int32, (rows, LANES), 1)
    row = lax.broadcasted_iota(jnp.int32, (rows, LANES), 0)
    edge = lane == jnp.where(low, 0, LANES - 1)
    edge_row = edge[:1]
    if ends is not None:
        above = above + jnp.where(edge_row, ends[0], 0.0)
        below = below + jnp.where(edge_row, ends[1], 0.0)
    group = LANES // part
    if known is not None:
        own_row, other_row = own[count : count + 24, :], other[count : count + 24, :]
        for base, x in (
            (48, jnp.where(low, own_row, other_row)), (72, jnp.where(low, other_row, own_row))
        ):
            x = jnp.where(low, x[:, :1], x[:, LANES - 1 :])
            known[base : base + 24, :] = jnp.broadcast_to(x, (24, LANES))
        for p in range(24):
            q, t = p % group, p // group
            last = side_2[(q + 1) * part - 1 : (q + 1) * part, t : t + 1]
            first_row = side_1[q * part : q * part + 1, t : t + 1]
            known[p : p + 1, :] = jnp.broadcast_to(last, (1, LANES))
            known[24 + p : 25 + p, :] = jnp.broadcast_to(first_row, (1, LANES))
    columns = []
    for q in range(group):
        at = slice(q * part, (q + 1) * part)
        column = jnp.concatenate([side_1[at], side_2[at]], axis=0)
        columns.append(dot(pick_rows, jnp.concatenate(split(column), axis=0), ((0,), (0,))))
    for n in range(12):
        p = 12 * level + n
        at = slice(n * part, (n + 1) * part)
        plane = jnp.concatenate([first[at], second[at]], axis=0)
        full = dot(pick_rows, jnp.concatenate(split(plane), axis=0), ((0,), (0,)))
        column = columns[p % group][:, p // group : p // group + 1]
        full = full + jnp.where(edge, column, 0.0)
        full = full + jnp.where(row == 0, above[p : p + 1], 0.0)
        ghost[n] = full + jnp.where(row == rows - 1, below[p : p + 1], 0.0)


def ends_of(par, msg_a, msg_b):
    base = msg_a.shape[0] - 24
    below, above = after_before(msg_a, msg_b, slice(base, base + 24), par[0])
    return above, below


def later_ghost_kernel(
    par, own, other, prow, pcol, later_own, later_other, msg_a, msg_b, ghost
):
    planes = later_own, later_other
    ends = ends_of(par, msg_a, msg_b)
    expand_ghosts(par, own, other, prow, pcol, ghost, 1, planes, ends=ends)


def ghost_rate(planes, z, depth, forward):
    total = None
    for tap, coeff in enumerate(COEFFS, 1):
        g = z + (tap if forward else tap - 1) - depth
        if g >= 0:
            term = coeff * planes[g // 2]
            total = term if total is None else total + term
    return total


def ghost_kernel(
    par, half, buoyancy, own, other, prow, pcol,
    out, ghost, known, out_a, out_b, out_1, out_2,
):
    planes = own, other
    expand_ghosts(par, own, other, prow, pcol, ghost, 0, planes, known=known)
    depth = half.shape[1]
    for c, (f, forward) in enumerate(VEL_Z):
        out[c, 0 : depth - 4] = half[c, 0 : depth - 4]
        n = CROSSING.index(f)
        planes = [ghost[2 * n], ghost[2 * n + 1]]
        for z in range(depth - 4, depth):
            value = half[c, z]
            rate = ghost_rate(planes, z, depth, forward)
            if rate is not None:
                value = value + (STEP * buoyancy[0, z]) * rate
            out[c, z] = value
    moved = [(out, c) for c in range(3)]
    put_rows(out_a, out_b, 0, moved, par[0])
    put_columns((out_1, out_2), 0, moved)
    even = par[0] == 0
    up, down = known[0:24, :], known[24:48, :]
    base = 12 * depth
    out_a[base:, :] = jnp.where(even, up, down)
    out_b[base:, :] = jnp.where(even, down, up)


def add_corners(
    par, half, buoyancy, half_ghost, known, begin_a, begin_b, begin_2, msg_a, msg_b, msg_2,
    velocity, ghost, rows_a, rows_b, cols_2, base_x, base_y,
):
    pi, low = par[0], par[1] == 0
    depth, rows = half.shape[1], half.shape[2]
    lane = lax.broadcasted_iota(jnp.int32, (rows, LANES), 1)
    row = lax.broadcasted_iota(jnp.int32, (rows, LANES), 0)
    edge = lane == jnp.where(low, 0, LANES - 1)
    first, last = edge & (row == 0), edge & (row == rows - 1)
    above, below = ends_of(par, msg_a, msg_b)
    for n in range(12):
        plane = half_ghost[n] + jnp.where(first, above[n : n + 1], 0.0)
        ghost[n] = plane + jnp.where(last, below[n : n + 1], 0.0)
    for source, target in ((msg_a, rows_a), (msg_b, rows_b), (msg_2, cols_2)):
        target[...] = source[...]
    even = pi == 0
    near = lax.broadcasted_iota(jnp.int32, (8, LANES), 0)
    lane = lax.broadcasted_iota(jnp.int32, (8, LANES), 1)
    edge = lane == jnp.where(low, 0, LANES - 1)
    beside = near == jnp.where(low, 7, 0)
    blocks = depth * rows // LANES
    none = jnp.zeros((1, LANES), F32)

    def rates(x, n, z, forward):
        found = []
        for odd in range(2):
            rate = ghost_rate([x[2 * n : 2 * n + 1], x[2 * n + 1 : 2 * n + 2]], z + odd, depth, forward)
            found.append(none if rate is None else rate)
        return found

    up, down = known[0:12, :], known[24:36, :]
    row_above, row_below = known[48:60, :], known[72:84, :]
    for c, (f, forward) in enumerate(VEL_Z):
        n = CROSSING.index(f)
        velocity[c, 0 : depth - 4] = half[c, 0 : depth - 4]
        for pair in range(2):
            z = depth - 4 + 2 * pair
            tops, bottoms = rates(above, n, z, forward), rates(below, n, z, forward)
            for odd in range(2):
                change = jnp.where(first, tops[odd], 0.0) + jnp.where(last, bottoms[odd], 0.0)
                scale = STEP * buoyancy[0, z + odd]
                velocity[c, z + odd] = half[c, z + odd] + scale * change
            after, before = after_before(
                begin_a, begin_b, slice(base_x + 8 * pair, base_x + 8 * pair + 8), pi
            )
            rate = rates(up, n, z, forward)
            change = jnp.where(near == 0, rate[0], jnp.where(near == 4, rate[1], 0.0))
            after = jnp.where(edge, (STEP * after) * change, 0.0)
            rate = rates(down, n, z, forward)
            change = jnp.where(near == 3, rate[0], jnp.where(near == 7, rate[1], 0.0))
            before = jnp.where(edge, (STEP * before) * change, 0.0)
            at = pl.ds(4 * (c * depth + z), 8)
            rows_a[at, :] = rows_a[at, :] + jnp.where(even, after, before)
            rows_b[at, :] = rows_b[at, :] + jnp.where(even, before, after)
            tops, bottoms = rates(row_above, n, z, forward), rates(row_below, n, z, forward)
            change = jnp.where(lane == 0, tops[0], jnp.where(lane == rows - 1, bottoms[0], 0.0))
            change = jnp.where(lane == rows, tops[1], change)
            change = jnp.where(lane == 2 * rows - 1, bottoms[1], change)
            light = begin_2[base_y + 8 * pair : base_y + 8 * pair + 8, :]
            at = pl.ds(8 * (c * blocks + blocks - 2 + pair), 8)
            cols_2[at, :] = cols_2[at, :] + jnp.where(beside, (STEP * light) * change, 0.0)


def stress_fields(ref, table):
    offset = 9 - ref.shape[0]
    return [(ref, f - offset) for f, _ in table]


def velocity_fill(par, stress, msg_a, msg_b, msg_1, msg_2, tile, halo, bottom, ex, ey, ez):
    pi, pj = par[0], par[1]
    none = zeros_like_plane(stress)
    fill_z(ez, stress_fields(stress, VEL_Z), lambda k, g: none, bottom)
    fill_x(ex, stress_fields(stress, VEL_X), msg_a, msg_b, 0, pi)
    fill_y(
        ey, stress_fields(stress, VEL_Y), [d for _, d in VEL_Y], msg_1, msg_2, 0, pj, tile, halo
    )


def first_velocity_kernel(
    par, state, buoyancy, msg_a, msg_b, msg_1, msg_2, tile, halo, out, ex, ey, ez
):
    none = zeros_like_plane(state)
    velocity_fill(
        par, state, msg_a, msg_b, msg_1, msg_2, tile, halo, lambda k, g: none, ex, ey, ez
    )
    velocity_half(state, buoyancy, out, ex, ey, ez)


def velocity_kernel(
    par, old, stress, buoyancy, ghost, start, msg_a, msg_b, msg_1, msg_2, tile, halo, means,
    out, out_a, out_b, out_1, out_2, coarse, ex, ey, ez, summed, halves,
):
    order = [CROSSING.index(f) for f, _ in VEL_Z]
    velocity_fill(
        par, stress, msg_a, msg_b, msg_1, msg_2, tile, halo,
        lambda k, g: ghost[2 * order[k] + g // 2], ex, ey, ez,
    )
    velocity_half(old, buoyancy, out, ex, ey, ez)
    moved = [(out, c) for c in range(3)]
    put_rows(out_a, out_b, 0, moved, par[0])
    put_columns((out_1, out_2), 0, moved)
    low = out.shape[1] - 8
    lift(start, STR_Z, [out.at[c, low:] for c in range(3)], means, coarse, summed, halves)


def stress_fill(
    par, velocity, bottom, msg_a, msg_b, msg_1, msg_2, tile, halo, ex, ey, ez, low, count
):
    pi, pj = par[0], par[1]
    none = zeros_like_plane(velocity)
    fields = [(velocity, c) for c in range(3)]
    fill_z(ez, fields, lambda k, g: none, bottom, low, count)
    fill_x(ex, fields, msg_a, msg_b, 0, pi, low, count)
    fill_y(
        ey, fields, [d for _, d in STR_Y], msg_1, msg_2, 0, pj, tile, halo, low, count
    )


def stress_kernel(
    par, half, state, medium, half_ghost, known, begin_a, begin_b, begin_2, msg_a, msg_b, msg_1,
    msg_2, tile, halo, out, velocity, out_a, out_b, out_1, out_2, ex, ey, ez, ghost, rows_a, rows_b,
    cols_2, *, base_x, base_y,
):
    depth = half.shape[1]
    add_corners(
        par, half, medium, half_ghost, known, begin_a, begin_b, begin_2, msg_a, msg_b, msg_2,
        velocity, ghost, rows_a, rows_b, cols_2, base_x, base_y,
    )
    stress_fill(
        par, velocity, lambda k, g: ghost[2 * k + g // 2], rows_a, rows_b, msg_1, cols_2,
        tile, halo, ex, ey, ez, 0, depth,
    )

    def put(c, z, n, value):
        out[c, z] = value

    stress_half(
        lambda c, z: state[SXX + c, z], lambda z: medium[1, z], lambda z: medium[2, z],
        put, 0, depth, ex, ey, ez,
    )
    put_rows(out_a, out_b, 0, stress_fields(out, VEL_X), par[0])
    put_columns((out_1, out_2), 0, stress_fields(out, VEL_Y))


def lift(start, table, fields, means, coarse, summed, halves):
    rows = summed.shape[0]
    part = rows // 4
    low = start.shape[1] - 8
    for n, (k, m) in enumerate(above_planes(table)):
        f, new = table[k][0], fields[k]
        z = 2 * m
        total = (start[f, low + z] + start[f, low + z + 1]) + (new[z] + new[z + 1])
        summed[...] = total
        pairs = summed[pl.ds(0, 2 * part, stride=2), :] + summed[pl.ds(1, 2 * part, stride=2), :]
        at = pl.ds(n * part, part)
        halves[0, at, :] = pairs[:part]
        halves[1, at, :] = pairs[part:]
    count = coarse.shape[0]
    upper = dot(jnp.concatenate(split(halves[0, 0:count]), axis=1), means[0])
    lower = dot(jnp.concatenate(split(halves[1, 0:count]), axis=1), means[1])
    coarse[...] = upper + lower


def lower_stress_kernel(
    par, velocity, stress, medium, ghost, start, msg_a, msg_b, msg_1, msg_2, tile, halo, means,
    out, coarse, ex, ey, ez, summed, halves,
):
    depth, rows = velocity.shape[1], velocity.shape[2]
    low = depth - 8
    stress_fill(
        par, velocity, lambda k, g: ghost[2 * k + g // 2], msg_a, msg_b, msg_1, msg_2,
        tile, halo, ex, ey, ez, low, 8,
    )

    def put(c, z, n, value):
        out[c, n] = value

    stress_half(
        lambda c, z: stress[c, z], lambda z: medium[1, z], lambda z: medium[2, z],
        put, low, 8, ex, ey, ez,
    )
    fields = [out.at[f - SXX] for f, _ in VEL_Z]
    lift(start, VEL_Z, fields, means, coarse, summed, halves)


def upper_stress_kernel(
    par, below, velocity, stress, medium, msg_a, msg_b, msg_1, msg_2, tile, halo,
    out, done, ex, ey, ez,
):
    stress_fill(
        par, velocity, None, msg_a, msg_b, msg_1, msg_2, tile, halo, ex, ey, ez, 0, 8
    )
    out[0:3] = velocity[...]
    out[SXX:, velocity.shape[1] - 8 :] = below[...]

    def put(c, z, n, value):
        out[SXX + c, n] = value

    stress_half(
        lambda c, z: stress[c, z], lambda z: medium[1, z], lambda z: medium[2, z],
        put, 0, 8, ex, ey, ez,
    )
    done[...] = jnp.zeros_like(done)


def join(par, own, other, ghost, table, rows):
    half = LANES // 2
    even = par[1] == 0
    left = jnp.where(even, own[...], other[...])
    right = jnp.where(even, other[...], own[...])
    low = lax.broadcasted_iota(jnp.int32, left.shape, 1) < half
    ghost[...] = jnp.where(
        even,
        jnp.where(low, left, pltpu.roll(right, half, 1)),
        jnp.where(low, pltpu.roll(left, half, 1), right),
    )
    planes = above_planes(table)
    none = jnp.zeros((rows, LANES), F32)

    def layer(k, m):
        if (k, m) not in planes:
            return none
        return ghost[pl.ds(planes.index((k, m)) * rows, rows), :]

    return layer


def coarse_velocity_kernel(
    par, state, medium, own, other, msg_a, msg_b, msg_1, msg_2, tile, halo, done,
    out, out_1, out_2, out_c, ex, ey, ez, ghost, *, base_c, base_r,
):
    pi, pj = par[0], par[1]
    rows = state.shape[2]
    above = join(par, own, other, ghost, VEL_Z, state.shape[2])
    none = zeros_like_plane(state)
    fill_z(
        ez, stress_fields(state, VEL_Z),
        above, lambda k, g: none,
    )
    fill_x(ex, stress_fields(state, VEL_X), msg_1, msg_2, base_r, pj)
    fill_y(
        ey, stress_fields(state, VEL_Y), [d for _, d in VEL_Y], msg_a, msg_b, base_c, pi,
        tile, halo,
    )
    velocity_half(state, medium, out, ex, ey, ez)
    moved = [(out, c) for c in range(3)]
    put_rows(out_1, out_2, 0, moved, pj)
    put_columns((out_c,), 0, moved)


def coarse_stress_kernel(
    par, state, medium, velocity, own, other, msg_a, msg_b, msg_1, msg_2, tile, halo,
    out, ex, ey, ez, ghost,
):
    pi, pj = par[0], par[1]
    above = join(par, own, other, ghost, STR_Z, state.shape[2])
    depth, rows = state.shape[1], state.shape[2]
    none = zeros_like_plane(state)
    fields = [(velocity, c) for c in range(3)]
    fill_z(
        ez, fields, above, lambda k, g: none
    )
    fill_x(ex, fields, msg_1, msg_2, 0, pj)
    fill_y(ey, fields, [d for _, d in STR_Y], msg_a, msg_b, 0, pi, tile, halo)
    out[0:3] = velocity[...]

    def put(c, z, n, value):
        out[SXX + c, z] = value

    stress_half(
        lambda c, z: state[SXX + c, z], lambda z: medium[1, z], lambda z: medium[2, z],
        put, 0, depth, ex, ey, ez,
    )


def whole(shape):
    return pl.BlockSpec(shape, functools.partial(lambda rank, _: (0,) * rank, len(shape)))


def call(kernel, args, outs, scratch=(), flops=0, copied=0, light=False):
    specs = []
    for n, a in enumerate(args):
        specs.append(pl.BlockSpec(memory_space=pltpu.HBM) if n < copied else whole(a.shape))
    size = 1024 if light else sum(4 * int(np.prod(a.shape)) for a in args) + sum(4 * int(np.prod(o)) for o in outs)

    def placed(*refs):
        i, j = lax.axis_index("gx"), lax.axis_index("gy")
        kernel((i % 2, j % 2, i, j // 2), *refs)

    return pl.pallas_call(
        placed,
        grid=(1,),
        in_specs=specs,
        out_specs=[whole(o) for o in outs],
        out_shape=[jax.ShapeDtypeStruct(o, F32) for o in outs],
        scratch_shapes=[pltpu.VMEM(s, F32) for s in scratch]
        + ([pltpu.SemaphoreType.DMA((12,))] if copied else []),
        compiler_params=pltpu.CompilerParams(vmem_limit_bytes=(54 if copied else 24) * 1024 * 1024),
        cost_estimate=pl.CostEstimate(flops=flops, bytes_accessed=size, transcendentals=0),
    )(*args)


def matchings(axis):
    size = lax.axis_size(axis)
    result = []
    for start in range(2):
        pairs = []
        for low in range(start, size - 1, 2):
            pairs += [(low, low + 1), (low + 1, low)]
        result.append(pairs)
    return result


def exchange(axis, first, second):
    one, two = matchings(axis)
    return lax.ppermute(first, axis, one), lax.ppermute(second, axis, two)


def body(
    fine_state, fine_medium, coarse_state, coarse_medium, coarse_past, parent_rows, parent_cols
):
    size_x, size_y = lax.axis_size("gx"), lax.axis_size("gy")
    i, j = lax.axis_index("gx"), lax.axis_index("gy")
    depth, rows, cols = fine_state.shape[1:]
    thick, part = coarse_state.shape[1:3]
    blocks = depth * rows // LANES
    tile, halo = (jnp.asarray(c) for c in lane_constants())
    means = jnp.asarray(mean_constants())
    across = [
        (p * size_y + q, (q // 2) * size_y + 2 * p + q % 2)
        for p in range(size_x)
        for q in range(size_y)
    ]
    partner = matchings("gy")[0]

    both = ("gx", "gy")

    rows_msg, cols_msg = 12 * depth, 24 * blocks
    coarse_cols, coarse_rows = 24, 12 * thick
    count = 24 * part
    out_a, out_b, out_1, out_2, planes, later, _ = call(
        pack_kernel,
        [fine_state, coarse_state, coarse_past, fine_medium],
        [(rows_msg + coarse_cols + 16 + count * 8 // LANES, LANES)] * 2
        + [(cols_msg + coarse_rows + 56, LANES), (cols_msg + coarse_rows + 40, LANES)]
        + [(count // 2, LANES)] * 2 + [(24, LANES)],
        [(3,) + fine_state.shape[1:], (3, depth, 8, cols), (3, depth, 8, cols),
         coarse_state.shape, coarse_past.shape, (1, 4, rows, cols)],
        copied=4,
    )
    msg_a, msg_b = exchange("gx", out_a, out_b)
    msg_1, msg_2 = exchange("gy", out_1, out_2)
    begin = msg_a, msg_b, msg_1, msg_2
    (crossing,) = call(
        crossing_kernel,
        [planes, msg_a, msg_b, msg_2],
        [(count // 2 + 40, LANES)],
    )
    own = lax.ppermute(crossing, both, across)

    shape = (depth, rows, cols)

    def scratch_of(depth, rows):
        return [
            (3, depth, rows + 16, LANES), (3, depth * rows, LANES), (3, depth + 8, rows, LANES),
        ]

    cells = depth * rows * cols
    halves = [(rows_msg + 8, LANES)] * 2 + [(cols_msg + 24, LANES), (cols_msg + 16, LANES)]
    (half,) = call(
        first_velocity_kernel,
        [fine_state, fine_medium, msg_a, msg_b, msg_1, msg_2, tile, halo],
        [(3,) + shape],
        scratch_of(depth, rows),
        flops=400 * cells,
    )
    own, half = lax.optimization_barrier((own, half))
    other = lax.ppermute(own, "gy", partner)
    parents = parent_rows.reshape(1, rows), parent_cols.reshape(1, cols)
    half, half_ghost, known, out_a, out_b, out_1, out_2 = call(
        ghost_kernel,
        [half, fine_medium, own, other, *parents],
        [(3,) + shape, (12, rows, cols), (96, LANES)] + [(rows_msg + 24, LANES)] * 2
        + [(cols_msg + 40, LANES), (cols_msg + 32, LANES)],
    )
    msgs = exchange("gx", out_a, out_b) + exchange("gy", out_1, out_2)
    later, half = lax.optimization_barrier((later, half))
    later = lax.ppermute(later, both, across)
    ends = msgs[:2]
    stress, velocity, out_a, out_b, out_1, out_2 = call(
        functools.partial(
            stress_kernel, base_x=rows_msg + coarse_cols, base_y=cols_msg + coarse_rows
        ),
        [half, fine_state, fine_medium, half_ghost, known, begin[0], begin[1], begin[3],
         *msgs, tile, halo],
        [(6,) + shape, (3,) + shape] + halves,
        scratch_of(depth, rows)
        + [(12, rows, cols)] + [(rows_msg + 24, LANES)] * 2 + [(cols_msg + 32, LANES)],
        flops=400 * cells,
    )
    msgs = exchange("gx", out_a, out_b) + exchange("gy", out_1, out_2)
    later, stress = lax.optimization_barrier((later, stress))
    later_other = lax.ppermute(later, "gy", partner)
    (ghost,) = call(
        later_ghost_kernel,
        [own, other, *parents, later, later_other, *ends],
        [(12, rows, cols)],
    )
    moved_v, moved_s = (len(above_planes(t)) * part for t in (STR_Z, VEL_Z))
    lift_scratch = [(rows, cols), (2, count // 2, LANES)]
    velocity, out_a, out_b, out_1, out_2, lifted = call(
        velocity_kernel,
        [velocity, stress, fine_medium, ghost, fine_state, *msgs, tile, halo, means],
        [(3,) + shape] + halves + [(moved_v, LANES)],
        scratch_of(depth, rows) + lift_scratch,
        flops=400 * cells,
    )
    msgs = exchange("gx", out_a, out_b) + exchange("gy", out_1, out_2)
    moving = lax.ppermute(lifted, both, across)
    below, lifted = call(
        lower_stress_kernel,
        [velocity, stress, fine_medium, ghost, fine_state, *msgs, tile, halo, means],
        [(6, 8, rows, cols), (moved_s, LANES)],
        scratch_of(8, rows) + lift_scratch,
        light=True,
    )
    own = lax.ppermute(lifted, both, across)
    fine_out, done = call(
        upper_stress_kernel,
        [below, velocity, stress, fine_medium, *msgs, tile, halo],
        [(9,) + shape, (8, LANES)],
        scratch_of(8, rows),
        flops=200 * cells,
    )
    own, done, moving = lax.optimization_barrier((own, done, moving))
    other = lax.ppermute(own, "gy", partner)
    moving_other = lax.ppermute(moving, "gy", partner)

    shape = (thick, part, LANES)
    velocity, out_1, out_2, out_c = call(
        functools.partial(coarse_velocity_kernel, base_c=rows_msg, base_r=cols_msg),
        [coarse_state, coarse_medium, own, other, *begin, tile, halo, done],
        [(3,) + shape, (coarse_rows, LANES), (coarse_rows, LANES), (coarse_cols, LANES)],
        scratch_of(thick, part) + [(moved_s, LANES)],
    )
    msgs = exchange("gx", out_c, out_c) + exchange("gy", out_1, out_2)
    (coarse_out,) = call(
        coarse_stress_kernel,
        [coarse_state, coarse_medium, velocity, moving, moving_other, *msgs, tile, halo],
        [(9,) + shape],
        scratch_of(thick, part) + [(moved_v, LANES)],
    )
    return (fine_out, coarse_out)


def solution(mesh):
    placed = (
        P(None, None, "gx", "gy"),
        P(None, None, "gx", "gy"),
        P(None, None, "gy", "gx"),
        P(None, None, "gy", "gx"),
        P(None, None, "gy", "gx"),
        P("gx"),
        P("gy"),
    )
    return jax.shard_map(
        body,
        mesh=mesh,
        in_specs=placed,
        out_specs=(P(None, None, "gx", "gy"), P(None, None, "gy", "gx")),
        check_vma=False,
    )
```

```python
import functools

import jax
import jax.numpy as jnp
import ml_dtypes
import numpy as np
from jax import lax
from jax.experimental import pallas as pl
from jax.experimental.pallas import tpu as pltpu
from jax.sharding import PartitionSpec as P

COEFFS = (1225.0 / 1024.0, -245.0 / 3072.0, 49.0 / 5120.0, -5.0 / 7168.0)
STEP = 0.1
LANES = 128
F32 = jnp.float32
BF16 = jnp.bfloat16

VX, VY, VZ, SXX, SYY, SZZ, SXY, SXZ, SYZ = range(9)
CROSSING = (VX, VY, VZ, SXZ, SYZ, SZZ)
VEL_X = ((SXX, True), (SXY, False), (SXZ, False))
VEL_Y = ((SXY, False), (SYY, True), (SYZ, False))
VEL_Z = ((SXZ, False), (SYZ, False), (SZZ, True))
STR_X = ((VX, False), (VY, True), (VZ, True))
STR_Y = ((VX, True), (VY, False), (VZ, True))
STR_Z = ((VX, True), (VY, True), (VZ, False))


def above_planes(table):
    skip = table is VEL_Z
    return [(k, m) for k, (_, forward) in enumerate(table) for m in range(int(skip and forward), 4)]


def band(width, forward):
    matrix = np.zeros((width + 8, width), np.float64)
    for out in range(width):
        for tap, coeff in enumerate(COEFFS, 1):
            upper = out + tap if forward else out + tap - 1
            lower = out + 1 - tap if forward else out - tap
            matrix[4 + upper, out] += coeff
            matrix[4 + lower, out] -= coeff
    return matrix


def two_part(matrix):
    high = matrix.astype(ml_dtypes.bfloat16)
    low = (matrix - high.astype(np.float64)).astype(ml_dtypes.bfloat16)
    return np.block([[high, low], [high, np.zeros_like(low)]]).astype(ml_dtypes.bfloat16)


def lane_constants():
    tile = np.stack([two_part(band(LANES, f)[4:-4]) for f in (False, True)])
    halo = []
    for parity in range(2):
        for forward in (False, True):
            matrix = band(LANES, forward)
            after = np.zeros((8, LANES))
            before = np.zeros((8, LANES))
            after[:4] = matrix[-4:]
            before[4:] = matrix[:4]
            pair = (after, before) if parity == 0 else (before, after)
            halo.append(two_part(np.concatenate(pair)))
    halo = np.stack(halo).reshape(2, 2, 32, 2 * LANES)
    return tile, halo


def mean_constants():
    half = LANES // 2
    place = np.zeros((2, LANES, LANES), np.float32)
    for lane in range(LANES):
        for part in range(2):
            place[part, lane, part * half + lane // 2] = 1.0 / 16.0
    return np.concatenate([place, place], axis=1).astype(ml_dtypes.bfloat16)


def split(x):
    high = x.astype(BF16)
    return high, (x - high.astype(F32)).astype(BF16)


def fold(x):
    half = x.shape[1] // 2
    return x[:, :half] + x[:, half:]


def dot(a, b, dims=((1,), (0,))):
    return lax.dot_general(a, b, (dims, ((), ())), preferred_element_type=F32)


def dot_lanes(x, matrix):
    return fold(dot(jnp.concatenate(split(x), axis=1), matrix))


def dot_rows(x, matrix):
    return fold(dot(jnp.concatenate(split(x), axis=0), matrix, ((0,), (0,))))


def flat(x):
    return x.reshape(x.shape[0] * x.shape[1], x.shape[2])


def upper_half(shape):
    return lax.broadcasted_iota(jnp.int32, shape, 0) < 4


def put_rows(out_a, out_b, base, fields, parity):
    parts = []
    for ref, f in fields:
        rows = ref.shape[2]
        parts.append((ref.at[:, :, 0:8, :], ref.at[:, :, rows - 8 : rows, :], f))
    put_edge_rows(out_a, out_b, base, parts, parity)


def put_edge_rows(out_a, out_b, base, fields, parity):
    even = parity == 0
    top = upper_half((8, LANES))
    for k, (head, tail, f) in enumerate(fields):
        depth = head.shape[1]
        for z in range(0, depth, 2):
            first = jnp.where(top, head[f, z], pltpu.roll(head[f, z + 1], 4, 0))
            last = jnp.where(top, pltpu.roll(tail[f, z], 4, 0), tail[f, z + 1])
            at = pl.ds(base + 4 * (k * depth + z), 8)
            out_a[at, :] = jnp.where(even, last, first)
            out_b[at, :] = jnp.where(even, first, last)


def put_columns(outs, base, fields):
    row = lax.broadcasted_iota(jnp.int32, (8, 2 * LANES), 0)
    lane = lax.broadcasted_iota(jnp.int32, (8, 2 * LANES), 1) % LANES
    edges = (lane == jnp.where(row < 4, row, LANES - 8 + row)).astype(BF16)
    for k, (ref, f) in enumerate(fields):
        x = jnp.concatenate([r[...] for r in ref], axis=0) if f is None else flat(ref[f])
        x = jnp.concatenate(split(x), axis=1)
        turned = dot(edges, x, ((1,), (1,)))
        blocks = turned.shape[1] // LANES
        for m in range(blocks):
            for out in outs:
                out[pl.ds(base + 8 * (k * blocks + m), 8), :] = turned[:, m * LANES : (m + 1) * LANES]


def fill_x(ext, fields, msg_a, msg_b, base, parity, low=0, count=None):
    even = parity == 0
    for k, (ref, f) in enumerate(fields):
        depth, rows = ref.shape[1], ref.shape[2]
        layers = depth if count is None else count
        ext[k, :, 8 : 8 + rows, :] = ref[f, low : low + layers]
        for z in range(0, layers, 2):
            at = pl.ds(base + 4 * (k * depth + low + z), 8)
            a, b = msg_a[at, :], msg_b[at, :]
            after, before = jnp.where(even, a, b), jnp.where(even, b, a)
            ext[k, z, 8 + rows : 16 + rows, :] = after
            ext[k, z + 1, 8 + rows : 16 + rows, :] = pltpu.roll(after, 4, 0)
            ext[k, z, 0:8, :] = pltpu.roll(before, 4, 0)
            ext[k, z + 1, 0:8, :] = before


def fill_y(out, fields, directions, msg_a, msg_b, base, parity, tile, halo, low=0, count=None):
    for k, (ref, f) in enumerate(fields):
        depth, rows = ref.shape[1], ref.shape[2]
        layers = depth if count is None else count
        forward = int(directions[k])
        inner = dot_lanes(flat(ref[f, low : low + layers]), tile[forward])
        factor = halo[parity, forward]
        start, blocks = low * rows // LANES, depth * rows // LANES
        for m in range(layers * rows // LANES):
            at = pl.ds(base + 8 * (k * blocks + start + m), 8)
            outer = dot_rows(jnp.concatenate([msg_a[at, :], msg_b[at, :]], axis=0), factor)
            out[k, m * LANES : (m + 1) * LANES, :] = inner[m * LANES : (m + 1) * LANES] + outer


def fill_z(ext, fields, top, bottom, low=0, count=None):
    for k, (ref, f) in enumerate(fields):
        depth = ref.shape[1]
        layers = depth if count is None else count
        first, last = max(low - 4, 0), min(low + layers + 4, depth)
        ext[k, first - low + 4 : last - low + 4] = ref[f, first:last]
        for g in range(first - (low - 4)):
            ext[k, g] = top(k, 4 - first + low - 4 + g)
        for g in range(low + layers + 4 - last):
            ext[k, last - low + 4 + g] = bottom(k, g)


def taps(read, forward):
    total = None
    for tap, coeff in enumerate(COEFFS, 1):
        upper = tap if forward else tap - 1
        lower = 1 - tap if forward else -tap
        term = coeff * (read(upper) - read(lower))
        total = term if total is None else total + term
    return total


def along_x(ext, k, z, rows, forward):
    return taps(lambda d: ext[k, z, 8 + d : 8 + d + rows, :], forward)


def along_z(ext, k, z, forward):
    return taps(lambda d: ext[k, z + 4 + d], forward)


def along_y(values, k, z, rows):
    return values[k, pl.ds(pl.multiple_of(z * rows, rows), rows), :]


def velocity_half(old, buoyancy, out, ex, ey, ez):
    depth, rows = out.shape[1], out.shape[2]

    def layer(z, _):
        scale = STEP * buoyancy[0, z]
        zx = along_z(ez, 0, z, False)
        zy = along_z(ez, 1, z, False)
        zz = along_z(ez, 2, z, True)
        x = along_x(ex, 0, z, rows, True)
        out[0, z] = old[0, z] + scale * (x + along_y(ey, 0, z, rows) + zx)
        x = along_x(ex, 1, z, rows, False)
        out[1, z] = old[1, z] + scale * (x + along_y(ey, 1, z, rows) + zy)
        x = along_x(ex, 2, z, rows, False)
        out[2, z] = old[2, z] + scale * (x + along_y(ey, 2, z, rows) + zz)
        return 0

    lax.fori_loop(0, depth, layer, 0, unroll=8 if rows > 16 else depth)


def stress_half(old, lame, shear, put, low, count, ex, ey, ez):
    rows = ex.shape[2] - 16

    def layer(n, _):
        z = n + low
        exx = along_x(ex, 0, n, rows, False)
        eyy = along_y(ey, 1, n, rows)
        ezz = along_z(ez, 2, n, False)
        mu = STEP * shear(z)
        common = (STEP * lame(z)) * (exx + eyy + ezz)
        double = mu + mu
        put(0, z, n, old(0, z) + (common + double * exx))
        put(1, z, n, old(1, z) + (common + double * eyy))
        put(2, z, n, old(2, z) + (common + double * ezz))
        x = along_x(ex, 1, n, rows, True)
        put(3, z, n, old(3, z) + mu * (along_y(ey, 0, n, rows) + x))
        x = along_x(ex, 2, n, rows, True)
        put(4, z, n, old(4, z) + mu * (along_z(ez, 0, n, True) + x))
        y = along_y(ey, 2, n, rows)
        put(5, z, n, old(5, z) + mu * (along_z(ez, 1, n, True) + y))
        return 0

    lax.fori_loop(0, count, layer, 0, unroll=8 if rows > 16 else count)


def zeros_like_plane(ref):
    return jnp.zeros(ref.shape[-2:], F32)


def after_before(msg_a, msg_b, at, parity):
    even = parity == 0
    a, b = msg_a[at, :], msg_b[at, :]
    return jnp.where(even, a, b), jnp.where(even, b, a)


def pack_kernel(
    par, fine, coarse, past, medium, out_a, out_b, out_1, out_2, planes, planes_2, outer,
    turned, first, last, state, before, light, sems,
):
    pi, pj = par[0], par[1]
    depth, rows = fine.shape[1], fine.shape[2]
    part = coarse.shape[2]
    copies = [
        pltpu.make_async_copy(coarse, state, sems.at[0]),
        pltpu.make_async_copy(past, before, sems.at[1]),
        pltpu.make_async_copy(medium.at[0:1, depth - 4 :], light, sems.at[2]),
    ]
    for k, (f, _) in enumerate(VEL_X):
        head, tail = fine.at[f, :, 0:8, :], fine.at[f, :, rows - 8 : rows, :]
        copies.append(pltpu.make_async_copy(head, first.at[k], sems.at[3 + 2 * k]))
        copies.append(pltpu.make_async_copy(tail, last.at[k], sems.at[4 + 2 * k]))
    for k, (f, _) in enumerate(VEL_Y):
        copies.append(pltpu.make_async_copy(fine.at[f], turned.at[k], sems.at[9 + k]))
    for copy in copies:
        copy.start()
    for copy in copies[:3]:
        copy.wait()
    upper = pj == 0
    for n, f in enumerate(CROSSING):
        for layer in range(2):
            now = state[f, layer]
            later = 1.5 * now - 0.5 * before[f, layer]
            for p, plane in ((2 * n + layer, now), (12 + 2 * n + layer, later)):
                target = planes if p < 12 else planes_2
                target[pl.ds(p % 12 * part, part), :] = plane
                outer[p : p + 1, :] = jnp.where(upper, plane[:1], plane[part - 1 :])
    base = 12 * depth
    put_columns((out_a, out_b), base, [(state, f) for f, _ in VEL_Y])
    put_rows(out_a, out_b, base + 24, [(light, 0)], pi)
    put_columns((out_a, out_b), base + 40, [((planes, planes_2), None)])
    base = 24 * (depth * rows // LANES)
    put_rows(out_1, out_2, base, [(state, f) for f, _ in VEL_X], pj)
    base += 12 * coarse.shape[1]
    put_columns((out_1, out_2), base, [(light, 0)])
    out_1[base + 16 : base + 40, :] = outer[...]
    out_2[base + 16 : base + 40, :] = outer[...]
    for copy in copies[3:9]:
        copy.wait()
    put_edge_rows(out_a, out_b, 0, [(first, last, k) for k in range(3)], pi)
    for k in range(3):
        copies[9 + k].wait()
        base = 8 * k * (depth * rows // LANES)
        put_columns((out_1, out_2), base, [(turned, k)])


def crossing_kernel(par, planes, msg_a, msg_b, msg_2, first):
    count = 2 * planes.shape[0]
    blocks = count // LANES
    even = par[0] == 0
    base = msg_a.shape[0] - 8 * blocks
    left, right = [], []
    for m in range(blocks):
        a = msg_a[pl.ds(base + 8 * m, 8), :]
        b = msg_b[pl.ds(base + 8 * m, 8), :]
        left.append(jnp.where(even, b, a)[7:8])
        right.append(jnp.where(even, a, b)[0:1])
    fill = [jnp.zeros((8 - blocks, LANES), F32)]
    left, right = (jnp.concatenate(side + fill, axis=0) for side in (left, right))
    half = count // 2
    first[0:half, :] = planes[...]
    first[half : half + 24, :] = msg_2[msg_2.shape[0] - 24 :, :]
    first[half + 24 : half + 32, :] = left
    first[half + 32 : half + 40, :] = right


def expand_ghosts(
    par, own, other, prow, pcol, ghost, level, planes, ends=None, known=None
):
    core = par[1]
    row_base, col_base = par[2] * (prow.shape[1] // 2), par[3] * LANES
    part = (own.shape[0] - 40) // 12
    rows = prow.shape[1]
    low = core == 0
    count = 12 * part
    source = lax.broadcasted_iota(jnp.int32, (LANES, LANES), 0)
    pick_cols = (source == pcol[...] - col_base).astype(BF16)
    pick_cols = jnp.concatenate([pick_cols, pick_cols], axis=0)
    source = lax.broadcasted_iota(jnp.int32, (2 * part, rows), 0)
    pick_rows = (source == prow[...] - row_base).astype(BF16)
    pick_rows = jnp.concatenate([pick_rows, pick_rows], axis=0)

    def spread(x):
        return dot(jnp.concatenate(split(x), axis=1), pick_cols)

    mine, theirs = (
        spread(jnp.concatenate([main[0:count, :], ref[count : count + 24, :]], axis=0))
        for main, ref in zip(planes, (own, other))
    )
    first, second = jnp.where(low, mine, theirs), jnp.where(low, theirs, mine)
    above, below = first[count:], second[count:]
    beside = []
    for ref in (own, other):
        side = jnp.where(low, ref[count + 24 : count + 32, :], ref[count + 32 : count + 40, :])
        side = jnp.concatenate([side, jnp.zeros((LANES - 8, LANES), F32)], axis=0)
        beside.append(side.T)
    side_1 = jnp.where(low, beside[0], beside[1])
    side_2 = jnp.where(low, beside[1], beside[0])
    lane = lax.broadcasted_iota(jnp.int32, (rows, LANES), 1)
    row = lax.broadcasted_iota(jnp.int32, (rows, LANES), 0)
    edge = lane == jnp.where(low, 0, LANES - 1)
    edge_row = edge[:1]
    if ends is not None:
        above = above + jnp.where(edge_row, ends[0], 0.0)
        below = below + jnp.where(edge_row, ends[1], 0.0)
    group = LANES // part
    if known is not None:
        own_row, other_row = own[count : count + 24, :], other[count : count + 24, :]
        for base, x in (
            (48, jnp.where(low, own_row, other_row)), (72, jnp.where(low, other_row, own_row))
        ):
            x = jnp.where(low, x[:, :1], x[:, LANES - 1 :])
            known[base : base + 24, :] = jnp.broadcast_to(x, (24, LANES))
        for p in range(24):
            q, t = p % group, p // group
            last = side_2[(q + 1) * part - 1 : (q + 1) * part, t : t + 1]
            first_row = side_1[q * part : q * part + 1, t : t + 1]
            known[p : p + 1, :] = jnp.broadcast_to(last, (1, LANES))
            known[24 + p : 25 + p, :] = jnp.broadcast_to(first_row, (1, LANES))
    columns = []
    for q in range(group):
        at = slice(q * part, (q + 1) * part)
        column = jnp.concatenate([side_1[at], side_2[at]], axis=0)
        columns.append(dot(pick_rows, jnp.concatenate(split(column), axis=0), ((0,), (0,))))
    for n in range(12):
        p = 12 * level + n
        at = slice(n * part, (n + 1) * part)
        plane = jnp.concatenate([first[at], second[at]], axis=0)
        full = dot(pick_rows, jnp.concatenate(split(plane), axis=0), ((0,), (0,)))
        column = columns[p % group][:, p // group : p // group + 1]
        full = full + jnp.where(edge, column, 0.0)
        full = full + jnp.where(row == 0, above[p : p + 1], 0.0)
        ghost[n] = full + jnp.where(row == rows - 1, below[p : p + 1], 0.0)


def ends_of(par, msg_a, msg_b):
    base = msg_a.shape[0] - 24
    below, above = after_before(msg_a, msg_b, slice(base, base + 24), par[0])
    return above, below


def later_ghost_kernel(
    par, own, other, prow, pcol, later_own, later_other, msg_a, msg_b, ghost
):
    planes = later_own, later_other
    ends = ends_of(par, msg_a, msg_b)
    expand_ghosts(par, own, other, prow, pcol, ghost, 1, planes, ends=ends)


def ghost_rate(planes, z, depth, forward):
    total = None
    for tap, coeff in enumerate(COEFFS, 1):
        g = z + (tap if forward else tap - 1) - depth
        if g >= 0:
            term = coeff * planes[g // 2]
            total = term if total is None else total + term
    return total


def ghost_kernel(
    par, half, buoyancy, own, other, prow, pcol,
    out, ghost, known, out_a, out_b, out_1, out_2,
):
    planes = own, other
    expand_ghosts(par, own, other, prow, pcol, ghost, 0, planes, known=known)
    depth = half.shape[1]
    for c, (f, forward) in enumerate(VEL_Z):
        out[c, 0 : depth - 4] = half[c, 0 : depth - 4]
        n = CROSSING.index(f)
        planes = [ghost[2 * n], ghost[2 * n + 1]]
        for z in range(depth - 4, depth):
            value = half[c, z]
            rate = ghost_rate(planes, z, depth, forward)
            if rate is not None:
                value = value + (STEP * buoyancy[0, z]) * rate
            out[c, z] = value
    moved = [(out, c) for c in range(3)]
    put_rows(out_a, out_b, 0, moved, par[0])
    put_columns((out_1, out_2), 0, moved)
    even = par[0] == 0
    up, down = known[0:24, :], known[24:48, :]
    base = 12 * depth
    out_a[base:, :] = jnp.where(even, up, down)
    out_b[base:, :] = jnp.where(even, down, up)


def add_corners(
    par, half, buoyancy, half_ghost, known, begin_a, begin_b, begin_2, msg_a, msg_b, msg_2,
    velocity, ghost, rows_a, rows_b, cols_2, base_x, base_y,
):
    pi, low = par[0], par[1] == 0
    depth, rows = half.shape[1], half.shape[2]
    lane = lax.broadcasted_iota(jnp.int32, (rows, LANES), 1)
    row = lax.broadcasted_iota(jnp.int32, (rows, LANES), 0)
    edge = lane == jnp.where(low, 0, LANES - 1)
    first, last = edge & (row == 0), edge & (row == rows - 1)
    above, below = ends_of(par, msg_a, msg_b)
    for n in range(12):
        plane = half_ghost[n] + jnp.where(first, above[n : n + 1], 0.0)
        ghost[n] = plane + jnp.where(last, below[n : n + 1], 0.0)
    for source, target in ((msg_a, rows_a), (msg_b, rows_b), (msg_2, cols_2)):
        target[...] = source[...]
    even = pi == 0
    near = lax.broadcasted_iota(jnp.int32, (8, LANES), 0)
    lane = lax.broadcasted_iota(jnp.int32, (8, LANES), 1)
    edge = lane == jnp.where(low, 0, LANES - 1)
    beside = near == jnp.where(low, 7, 0)
    blocks = depth * rows // LANES
    none = jnp.zeros((1, LANES), F32)

    def rates(x, n, z, forward):
        found = []
        for odd in range(2):
            rate = ghost_rate([x[2 * n : 2 * n + 1], x[2 * n + 1 : 2 * n + 2]], z + odd, depth, forward)
            found.append(none if rate is None else rate)
        return found

    up, down = known[0:12, :], known[24:36, :]
    row_above, row_below = known[48:60, :], known[72:84, :]
    for c, (f, forward) in enumerate(VEL_Z):
        n = CROSSING.index(f)
        velocity[c, 0 : depth - 4] = half[c, 0 : depth - 4]
        for pair in range(2):
            z = depth - 4 + 2 * pair
            tops, bottoms = rates(above, n, z, forward), rates(below, n, z, forward)
            for odd in range(2):
                change = jnp.where(first, tops[odd], 0.0) + jnp.where(last, bottoms[odd], 0.0)
                scale = STEP * buoyancy[0, z + odd]
                velocity[c, z + odd] = half[c, z + odd] + scale * change
            after, before = after_before(
                begin_a, begin_b, slice(base_x + 8 * pair, base_x + 8 * pair + 8), pi
            )
            rate = rates(up, n, z, forward)
            change = jnp.where(near == 0, rate[0], jnp.where(near == 4, rate[1], 0.0))
            after = jnp.where(edge, (STEP * after) * change, 0.0)
            rate = rates(down, n, z, forward)
            change = jnp.where(near == 3, rate[0], jnp.where(near == 7, rate[1], 0.0))
            before = jnp.where(edge, (STEP * before) * change, 0.0)
            at = pl.ds(4 * (c * depth + z), 8)
            rows_a[at, :] = rows_a[at, :] + jnp.where(even, after, before)
            rows_b[at, :] = rows_b[at, :] + jnp.where(even, before, after)
            tops, bottoms = rates(row_above, n, z, forward), rates(row_below, n, z, forward)
            change = jnp.where(lane == 0, tops[0], jnp.where(lane == rows - 1, bottoms[0], 0.0))
            change = jnp.where(lane == rows, tops[1], change)
            change = jnp.where(lane == 2 * rows - 1, bottoms[1], change)
            light = begin_2[base_y + 8 * pair : base_y + 8 * pair + 8, :]
            at = pl.ds(8 * (c * blocks + blocks - 2 + pair), 8)
            cols_2[at, :] = cols_2[at, :] + jnp.where(beside, (STEP * light) * change, 0.0)


def stress_fields(ref, table):
    offset = 9 - ref.shape[0]
    return [(ref, f - offset) for f, _ in table]


def velocity_fill(par, stress, msg_a, msg_b, msg_1, msg_2, tile, halo, bottom, ex, ey, ez):
    pi, pj = par[0], par[1]
    none = zeros_like_plane(stress)
    fill_z(ez, stress_fields(stress, VEL_Z), lambda k, g: none, bottom)
    fill_x(ex, stress_fields(stress, VEL_X), msg_a, msg_b, 0, pi)
    fill_y(
        ey, stress_fields(stress, VEL_Y), [d for _, d in VEL_Y], msg_1, msg_2, 0, pj, tile, halo
    )


def first_velocity_kernel(
    par, state, buoyancy, msg_a, msg_b, msg_1, msg_2, tile, halo, out, ex, ey, ez
):
    none = zeros_like_plane(state)
    velocity_fill(
        par, state, msg_a, msg_b, msg_1, msg_2, tile, halo, lambda k, g: none, ex, ey, ez
    )
    velocity_half(state, buoyancy, out, ex, ey, ez)


def velocity_kernel(
    par, old, stress, buoyancy, ghost, start, msg_a, msg_b, msg_1, msg_2, tile, halo, means,
    out, out_a, out_b, out_1, out_2, coarse, ex, ey, ez, summed, halves,
):
    order = [CROSSING.index(f) for f, _ in VEL_Z]
    velocity_fill(
        par, stress, msg_a, msg_b, msg_1, msg_2, tile, halo,
        lambda k, g: ghost[2 * order[k] + g // 2], ex, ey, ez,
    )
    velocity_half(old, buoyancy, out, ex, ey, ez)
    moved = [(out, c) for c in range(3)]
    put_rows(out_a, out_b, 0, moved, par[0])
    put_columns((out_1, out_2), 0, moved)
    low = out.shape[1] - 8
    lift(start, STR_Z, [out.at[c, low:] for c in range(3)], means, coarse, summed, halves)


def stress_fill(
    par, velocity, bottom, msg_a, msg_b, msg_1, msg_2, tile, halo, ex, ey, ez, low, count
):
    pi, pj = par[0], par[1]
    none = zeros_like_plane(velocity)
    fields = [(velocity, c) for c in range(3)]
    fill_z(ez, fields, lambda k, g: none, bottom, low, count)
    fill_x(ex, fields, msg_a, msg_b, 0, pi, low, count)
    fill_y(
        ey, fields, [d for _, d in STR_Y], msg_1, msg_2, 0, pj, tile, halo, low, count
    )


def stress_kernel(
    par, half, state, medium, half_ghost, known, begin_a, begin_b, begin_2, msg_a, msg_b, msg_1,
    msg_2, tile, halo, out, velocity, out_a, out_b, out_1, out_2, ex, ey, ez, ghost, rows_a, rows_b,
    cols_2, *, base_x, base_y,
):
    depth = half.shape[1]
    add_corners(
        par, half, medium, half_ghost, known, begin_a, begin_b, begin_2, msg_a, msg_b, msg_2,
        velocity, ghost, rows_a, rows_b, cols_2, base_x, base_y,
    )
    stress_fill(
        par, velocity, lambda k, g: ghost[2 * k + g // 2], rows_a, rows_b, msg_1, cols_2,
        tile, halo, ex, ey, ez, 0, depth,
    )

    def put(c, z, n, value):
        out[c, z] = value

    stress_half(
        lambda c, z: state[SXX + c, z], lambda z: medium[1, z], lambda z: medium[2, z],
        put, 0, depth, ex, ey, ez,
    )
    put_rows(out_a, out_b, 0, stress_fields(out, VEL_X), par[0])
    put_columns((out_1, out_2), 0, stress_fields(out, VEL_Y))


def lift(start, table, fields, means, coarse, summed, halves):
    rows = summed.shape[0]
    part = rows // 4
    low = start.shape[1] - 8
    for n, (k, m) in enumerate(above_planes(table)):
        f, new = table[k][0], fields[k]
        z = 2 * m
        total = (start[f, low + z] + start[f, low + z + 1]) + (new[z] + new[z + 1])
        summed[...] = total
        pairs = summed[pl.ds(0, 2 * part, stride=2), :] + summed[pl.ds(1, 2 * part, stride=2), :]
        at = pl.ds(n * part, part)
        halves[0, at, :] = pairs[:part]
        halves[1, at, :] = pairs[part:]
    count = coarse.shape[0]
    upper = dot(jnp.concatenate(split(halves[0, 0:count]), axis=1), means[0])
    lower = dot(jnp.concatenate(split(halves[1, 0:count]), axis=1), means[1])
    coarse[...] = upper + lower


def lower_stress_kernel(
    par, velocity, stress, medium, ghost, start, msg_a, msg_b, msg_1, msg_2, tile, halo, means,
    out, coarse, ex, ey, ez, summed, halves,
):
    depth, rows = velocity.shape[1], velocity.shape[2]
    low = depth - 8
    stress_fill(
        par, velocity, lambda k, g: ghost[2 * k + g // 2], msg_a, msg_b, msg_1, msg_2,
        tile, halo, ex, ey, ez, low, 8,
    )

    def put(c, z, n, value):
        out[c, n] = value

    stress_half(
        lambda c, z: stress[c, z], lambda z: medium[1, z], lambda z: medium[2, z],
        put, low, 8, ex, ey, ez,
    )
    fields = [out.at[f - SXX] for f, _ in VEL_Z]
    lift(start, VEL_Z, fields, means, coarse, summed, halves)


def upper_stress_kernel(
    par, below, velocity, stress, medium, msg_a, msg_b, msg_1, msg_2, tile, halo,
    out, done, ex, ey, ez,
):
    stress_fill(
        par, velocity, None, msg_a, msg_b, msg_1, msg_2, tile, halo, ex, ey, ez, 0, 8
    )
    out[0:3] = velocity[...]
    out[SXX:, velocity.shape[1] - 8 :] = below[...]

    def put(c, z, n, value):
        out[SXX + c, n] = value

    stress_half(
        lambda c, z: stress[c, z], lambda z: medium[1, z], lambda z: medium[2, z],
        put, 0, 8, ex, ey, ez,
    )
    done[...] = jnp.zeros_like(done)


def join(par, own, other, ghost, table, rows):
    half = LANES // 2
    even = par[1] == 0
    left = jnp.where(even, own[...], other[...])
    right = jnp.where(even, other[...], own[...])
    low = lax.broadcasted_iota(jnp.int32, left.shape, 1) < half
    ghost[...] = jnp.where(
        even,
        jnp.where(low, left, pltpu.roll(right, half, 1)),
        jnp.where(low, pltpu.roll(left, half, 1), right),
    )
    planes = above_planes(table)
    none = jnp.zeros((rows, LANES), F32)

    def layer(k, m):
        if (k, m) not in planes:
            return none
        return ghost[pl.ds(planes.index((k, m)) * rows, rows), :]

    return layer


def coarse_velocity_kernel(
    par, state, medium, own, other, msg_a, msg_b, msg_1, msg_2, tile, halo, done,
    out, out_1, out_2, out_c, ex, ey, ez, ghost, *, base_c, base_r,
):
    pi, pj = par[0], par[1]
    rows = state.shape[2]
    above = join(par, own, other, ghost, VEL_Z, state.shape[2])
    none = zeros_like_plane(state)
    fill_z(
        ez, stress_fields(state, VEL_Z),
        above, lambda k, g: none,
    )
    fill_x(ex, stress_fields(state, VEL_X), msg_1, msg_2, base_r, pj)
    fill_y(
        ey, stress_fields(state, VEL_Y), [d for _, d in VEL_Y], msg_a, msg_b, base_c, pi,
        tile, halo,
    )
    velocity_half(state, medium, out, ex, ey, ez)
    moved = [(out, c) for c in range(3)]
    put_rows(out_1, out_2, 0, moved, pj)
    put_columns((out_c,), 0, moved)


def coarse_stress_kernel(
    par, state, medium, velocity, own, other, msg_a, msg_b, msg_1, msg_2, tile, halo,
    out, ex, ey, ez, ghost,
):
    pi, pj = par[0], par[1]
    above = join(par, own, other, ghost, STR_Z, state.shape[2])
    depth, rows = state.shape[1], state.shape[2]
    none = zeros_like_plane(state)
    fields = [(velocity, c) for c in range(3)]
    fill_z(
        ez, fields, above, lambda k, g: none
    )
    fill_x(ex, fields, msg_1, msg_2, 0, pj)
    fill_y(ey, fields, [d for _, d in STR_Y], msg_a, msg_b, 0, pi, tile, halo)
    out[0:3] = velocity[...]

    def put(c, z, n, value):
        out[SXX + c, z] = value

    stress_half(
        lambda c, z: state[SXX + c, z], lambda z: medium[1, z], lambda z: medium[2, z],
        put, 0, depth, ex, ey, ez,
    )


def whole(shape):
    return pl.BlockSpec(shape, functools.partial(lambda rank, _: (0,) * rank, len(shape)))


def call(kernel, args, outs, scratch=(), flops=0, copied=0, light=False):
    specs = []
    for n, a in enumerate(args):
        specs.append(pl.BlockSpec(memory_space=pltpu.HBM) if n < copied else whole(a.shape))
    size = 1024 if light else sum(4 * int(np.prod(a.shape)) for a in args) + sum(4 * int(np.prod(o)) for o in outs)

    def placed(*refs):
        i, j = lax.axis_index("gx"), lax.axis_index("gy")
        kernel((i % 2, j % 2, i, j // 2), *refs)

    return pl.pallas_call(
        placed,
        grid=(1,),
        in_specs=specs,
        out_specs=[whole(o) for o in outs],
        out_shape=[jax.ShapeDtypeStruct(o, F32) for o in outs],
        scratch_shapes=[pltpu.VMEM(s, F32) for s in scratch]
        + ([pltpu.SemaphoreType.DMA((12,))] if copied else []),
        compiler_params=pltpu.CompilerParams(vmem_limit_bytes=(54 if copied else 24) * 1024 * 1024),
        cost_estimate=pl.CostEstimate(flops=flops, bytes_accessed=size, transcendentals=0),
    )(*args)


def matchings(axis):
    size = lax.axis_size(axis)
    result = []
    for start in range(2):
        pairs = []
        for low in range(start, size - 1, 2):
            pairs += [(low, low + 1), (low + 1, low)]
        result.append(pairs)
    return result


def exchange(axis, first, second):
    one, two = matchings(axis)
    return lax.ppermute(first, axis, one), lax.ppermute(second, axis, two)


def body(
    fine_state, fine_medium, coarse_state, coarse_medium, coarse_past, parent_rows, parent_cols
):
    size_x, size_y = lax.axis_size("gx"), lax.axis_size("gy")
    i, j = lax.axis_index("gx"), lax.axis_index("gy")
    depth, rows, cols = fine_state.shape[1:]
    thick, part = coarse_state.shape[1:3]
    blocks = depth * rows // LANES
    tile, halo = (jnp.asarray(c) for c in lane_constants())
    means = jnp.asarray(mean_constants())
    across = [
        (p * size_y + q, (q // 2) * size_y + 2 * p + q % 2)
        for p in range(size_x)
        for q in range(size_y)
    ]
    partner = matchings("gy")[0]

    both = ("gx", "gy")

    rows_msg, cols_msg = 12 * depth, 24 * blocks
    coarse_cols, coarse_rows = 24, 12 * thick
    count = 24 * part
    out_a, out_b, out_1, out_2, planes, later, _ = call(
        pack_kernel,
        [fine_state, coarse_state, coarse_past, fine_medium],
        [(rows_msg + coarse_cols + 16 + count * 8 // LANES, LANES)] * 2
        + [(cols_msg + coarse_rows + 56, LANES), (cols_msg + coarse_rows + 40, LANES)]
        + [(count // 2, LANES)] * 2 + [(24, LANES)],
        [(3,) + fine_state.shape[1:], (3, depth, 8, cols), (3, depth, 8, cols),
         coarse_state.shape, coarse_past.shape, (1, 4, rows, cols)],
        copied=4,
    )
    msg_a, msg_b = exchange("gx", out_a, out_b)
    msg_1, msg_2 = exchange("gy", out_1, out_2)
    begin = msg_a, msg_b, msg_1, msg_2
    (crossing,) = call(
        crossing_kernel,
        [planes, msg_a, msg_b, msg_2],
        [(count // 2 + 40, LANES)],
    )
    own = lax.ppermute(crossing, both, across)

    shape = (depth, rows, cols)

    def scratch_of(depth, rows):
        return [
            (3, depth, rows + 16, LANES), (3, depth * rows, LANES), (3, depth + 8, rows, LANES),
        ]

    cells = depth * rows * cols
    halves = [(rows_msg + 8, LANES)] * 2 + [(cols_msg + 24, LANES), (cols_msg + 16, LANES)]
    (half,) = call(
        first_velocity_kernel,
        [fine_state, fine_medium, msg_a, msg_b, msg_1, msg_2, tile, halo],
        [(3,) + shape],
        scratch_of(depth, rows),
        flops=400 * cells,
    )
    own, half = lax.optimization_barrier((own, half))
    other = lax.ppermute(own, "gy", partner)
    parents = parent_rows.reshape(1, rows), parent_cols.reshape(1, cols)
    half, half_ghost, known, out_a, out_b, out_1, out_2 = call(
        ghost_kernel,
        [half, fine_medium, own, other, *parents],
        [(3,) + shape, (12, rows, cols), (96, LANES)] + [(rows_msg + 24, LANES)] * 2
        + [(cols_msg + 40, LANES), (cols_msg + 32, LANES)],
    )
    msgs = exchange("gx", out_a, out_b) + exchange("gy", out_1, out_2)
    later, half = lax.optimization_barrier((later, half))
    later = lax.ppermute(later, both, across)
    ends = msgs[:2]
    stress, velocity, out_a, out_b, out_1, out_2 = call(
        functools.partial(
            stress_kernel, base_x=rows_msg + coarse_cols, base_y=cols_msg + coarse_rows
        ),
        [half, fine_state, fine_medium, half_ghost, known, begin[0], begin[1], begin[3],
         *msgs, tile, halo],
        [(6,) + shape, (3,) + shape] + halves,
        scratch_of(depth, rows)
        + [(12, rows, cols)] + [(rows_msg + 24, LANES)] * 2 + [(cols_msg + 32, LANES)],
        flops=400 * cells,
    )
    msgs = exchange("gx", out_a, out_b) + exchange("gy", out_1, out_2)
    later, stress = lax.optimization_barrier((later, stress))
    later_other = lax.ppermute(later, "gy", partner)
    (ghost,) = call(
        later_ghost_kernel,
        [own, other, *parents, later, later_other, *ends],
        [(12, rows, cols)],
    )
    moved_v, moved_s = (len(above_planes(t)) * part for t in (STR_Z, VEL_Z))
    lift_scratch = [(rows, cols), (2, count // 2, LANES)]
    velocity, out_a, out_b, out_1, out_2, lifted = call(
        velocity_kernel,
        [velocity, stress, fine_medium, ghost, fine_state, *msgs, tile, halo, means],
        [(3,) + shape] + halves + [(moved_v, LANES)],
        scratch_of(depth, rows) + lift_scratch,
        flops=400 * cells,
    )
    msgs = exchange("gx", out_a, out_b) + exchange("gy", out_1, out_2)
    moving = lax.ppermute(lifted, both, across)
    below, lifted = call(
        lower_stress_kernel,
        [velocity, stress, fine_medium, ghost, fine_state, *msgs, tile, halo, means],
        [(6, 8, rows, cols), (moved_s, LANES)],
        scratch_of(8, rows) + lift_scratch,
        light=True,
    )
    own = lax.ppermute(lifted, both, across)
    fine_out, done = call(
        upper_stress_kernel,
        [below, velocity, stress, fine_medium, *msgs, tile, halo],
        [(9,) + shape, (8, LANES)],
        scratch_of(8, rows),
        flops=200 * cells,
    )
    own, done, moving = lax.optimization_barrier((own, done, moving))
    other = lax.ppermute(own, "gy", partner)
    moving_other = lax.ppermute(moving, "gy", partner)

    shape = (thick, part, LANES)
    velocity, out_1, out_2, out_c = call(
        functools.partial(coarse_velocity_kernel, base_c=rows_msg, base_r=cols_msg),
        [coarse_state, coarse_medium, own, other, *begin, tile, halo, done],
        [(3,) + shape, (coarse_rows, LANES), (coarse_rows, LANES), (coarse_cols, LANES)],
        scratch_of(thick, part) + [(moved_s, LANES)],
    )
    msgs = exchange("gx", out_c, out_c) + exchange("gy", out_1, out_2)
    (coarse_out,) = call(
        coarse_stress_kernel,
        [coarse_state, coarse_medium, velocity, moving, moving_other, *msgs, tile, halo],
        [(9,) + shape],
        scratch_of(thick, part) + [(moved_v, LANES)],
    )
    return (fine_out, coarse_out)


def solution(mesh):
    placed = (
        P(None, None, "gx", "gy"),
        P(None, None, "gx", "gy"),
        P(None, None, "gy", "gx"),
        P(None, None, "gy", "gx"),
        P(None, None, "gy", "gx"),
        P("gx"),
        P("gy"),
    )
    return jax.shard_map(
        body,
        mesh=mesh,
        in_specs=placed,
        out_specs=(P(None, None, "gx", "gy"), P(None, None, "gy", "gx")),
        check_vma=False,
    )
```
